32 devices in a mesh: seq: 8 (over z, x), dp: 4 (over y, core).
Axes of the slice: x: 2, y: 2, z: 4, core: 2. Of those that a mesh axis runs over, the one named last changes fastest.
Arguments:
- tokens: bfloat16 [4, 8192, 512], P('dp', 'seq'), may hold values from -6 to 6
- lengths: int32 [4, 3], P('dp'), may hold values from 256 to 7424, as said below
- gain: float32 [512], replicated, may hold values from 0.5 to 1.5
- b_proj: bfloat16 [2, 512, 256], replicated, may hold values from -0.25 to 0.25
- c_proj: bfloat16 [2, 256, 512], replicated, may hold values from -0.25 to 0.25
- skip: float32 [512], replicated, may hold values from -3 to 3
- nu: float32 [256], replicated, may hold values from -12 to -3
- theta: float32 [256], replicated, may hold values from -2.5 to 0
- gamma_log: float32 [256], replicated, may hold values from -7 to 0
- glu: bfloat16 [512, 1024], replicated, may hold values from -0.25 to 0.25
- out_grad: bfloat16 [4, 8192, 512], P('dp', 'seq'), may hold values from -6 to 6
Outputs:
- block_out: bfloat16 [4, 8192, 512], P('dp', 'seq')
- in_grad: bfloat16 [4, 8192, 512], P('dp', 'seq')
- gain_grad: float32 [512], replicated
- b_grad: float32 [2, 512, 256], replicated
- c_grad: float32 [2, 256, 512], replicated
- skip_grad: float32 [512], replicated
- nu_grad: float32 [256], replicated
- theta_grad: float32 [256], replicated
- gamma_grad: float32 [256], replicated
- glu_grad: float32 [512, 1024], replicated
The draws below stay inside these ranges and needn't reach their ends.
Inputs may be any that keep to these rules, and one draw needn't show every extreme that they name: Each row holds 3 lengths summing to 8192: 256, 512 and 7424, in an order drawn from the seed.
All inputs are finite; a program needn't handle non-finite values.
Results may differ from the reference program's by a relative error of at most 0.02.
Values may be sent and summed in bfloat16 or wider, within the bound.
A program may use at most 128 MiB of HBM per device.

```python
from functools import partial
import jax
import jax.numpy as jnp
from jax import lax

D = 512
N = 256
TOK_DEV = 1024
SEQS = 3
GROUPS = 4
GROUP_TOK = 8192


def decay_rates(key, slow_share):
    pick_key, slow_key, fast_key = jax.random.split(key, 3)
    slow_mask = jax.random.uniform(pick_key, (N,)) < slow_share
    low_end = jnp.log(0.25 / GROUP_TOK)
    mid_end = jnp.log(2.0 / GROUP_TOK)
    high_end = jnp.log(1.0 / 30.0)
    slow_log = low_end + (mid_end - low_end) * jax.random.uniform(slow_key, (N,))
    fast_log = mid_end + (high_end - mid_end) * jax.random.uniform(fast_key, (N,))
    return jnp.exp(jnp.where(slow_mask, slow_log, fast_log))


def draw_nu(key, part):
    slow_share = 0.5
    decay_rate = decay_rates(key, slow_share)
    return jnp.log(decay_rate)


def draw_gamma_log(key, part):
    slow_share = 0.5
    decay_rate = decay_rates(key, slow_share)
    key = jax.random.fold_in(key, 5)
    jitter_term = jax.random.uniform(key, (N,), minval=-0.4, maxval=0.4)
    return 0.5 * jnp.log(-jnp.expm1(-2.0 * decay_rate)) + jitter_term


def draw_lengths(key, part):
    key = jax.random.fold_in(key, 11)
    order_key, slot_key = jax.random.split(key, 2)
    quarter = TOK_DEV // 4
    half_dev = TOK_DEV // 2
    long_len = GROUP_TOK - 3 * quarter
    flips = jax.random.randint(order_key, (GROUPS, 1), 0, 2)
    first_short = jnp.where(flips == 0, quarter, half_dev).astype(jnp.int32)
    second_short = (quarter + half_dev - first_short).astype(jnp.int32)
    long_slot = jax.random.randint(slot_key, (GROUPS, 1), 0, SEQS)
    places = jnp.arange(SEQS, dtype=jnp.int32)[None, :]
    short_place = places - (places > long_slot).astype(jnp.int32)
    merged = jnp.where(places == long_slot, long_len, jnp.where(short_place == 0, first_short, second_short))
    return merged.astype(jnp.int32)


def block_levels(own_key, dims, pieces, least, high):
    level = 1.0
    for dim, parts in pieces:
        draws = jax.random.uniform(jax.random.fold_in(jax.random.fold_in(own_key, 6), dim), (parts,), jnp.float32, least / len(pieces), high / len(pieces))
        level = level * jnp.repeat(jnp.exp(draws), dims[dim] // parts).reshape((-1,) + (1,) * (len(dims) - 1 - dim))
    return level


def centred(rng, shape, deviation, most, pieces=(), kind=jnp.bfloat16):
    array = jax.random.normal(rng, shape, jnp.float32) * deviation
    if len(pieces) > 0:
        array = block_levels(rng, shape, pieces, -0.22, 0.18) * array
    return jnp.clip(array, min=-most, max=most).astype(kind)


def setup_inputs(seed: int = 0) -> dict:
    arg_keys = jax.random.split(jax.random.key(seed), 12)
    return {
        "tokens": centred(arg_keys[0], (GROUPS, GROUP_TOK, D), 1.0, 6.0, ((0, 4), (1, 8))),
        "lengths": draw_lengths(jax.random.fold_in(arg_keys[11], 71), 0),
        "gain": jnp.clip(1.0 + 0.1 * jax.random.normal(arg_keys[2], (D,), jnp.float32), 0.5, 1.5),
        "b_proj": centred(arg_keys[3], (2, D, N), D ** -0.5, 0.25),
        "c_proj": centred(arg_keys[4], (2, N, D), (2 * N) ** -0.5, 0.25),
        "skip": centred(arg_keys[5], (D,), 0.5, 3.0, (), jnp.float32),
        "nu": draw_nu(jax.random.fold_in(arg_keys[11], 71), 0),
        "theta": jnp.clip(jax.random.uniform(arg_keys[7], (N,), jnp.float32, -2.5, 0.0), -2.5, 0.0),
        "gamma_log": draw_gamma_log(jax.random.fold_in(arg_keys[11], 71), 0),
        "glu": centred(arg_keys[9], (D, 2 * D), D ** -0.5, 0.25),
        "out_grad": centred(arg_keys[10], (GROUPS, GROUP_TOK, D), 1.0, 6.0, ((0, 4), (1, 8))),
    }


@jax.custom_vjp
def low(v):
    return lax.optimization_barrier(v.astype(jnp.bfloat16)).astype(jnp.float32)

@jax.custom_vjp
def low_back(v):
    return v

def low_keep(v):
    return (low(v), None)

def low_pass(kept, grad):
    return (grad,)

def back_keep(v):
    return (v, None)

def back_low(kept, grad):
    return (low(grad),)
low.defvjp(low_keep, low_pass)
low_back.defvjp(back_keep, back_low)
eps = 1e-05
highest = lax.Precision.HIGHEST

def combine_pairs(first, second):
    a_re, a_im, b_re, b_im = first
    c_re, c_im, d_re, d_im = second
    return (a_re * c_re - a_im * c_im, a_re * c_im + a_im * c_re, c_re * b_re - c_im * b_im + d_re, c_re * b_im + c_im * b_re + d_im)

def gelu_tanh(values):
    return 0.5 * values * (1.0 + jnp.tanh(0.7978845608028654 * (values + 0.044715 * values * values * values)))

def matmul(left, right):
    return jnp.dot(left, right, precision=highest, preferred_element_type=jnp.float32)

def group_block(weights, inputs, keep_mask):
    gain, b_proj, c_proj, skip, nu, theta, gamma_log, glu = weights
    row_mean = lax.optimization_barrier(jnp.mean(inputs, axis=1, keepdims=True))
    centered = inputs - row_mean
    row_var = lax.optimization_barrier(jnp.mean(centered * centered, axis=1, keepdims=True))
    u_low = low(centered * lax.rsqrt(row_var + eps) * gain)
    drive_re = low_back(low(matmul(u_low, b_proj[0])))
    drive_im = low_back(low(matmul(u_low, b_proj[1])))
    modulus = jnp.exp(-jnp.exp(nu))
    angles = jnp.exp(theta)
    scaling = jnp.exp(gamma_log)
    lam_re = (modulus * jnp.cos(angles))[None, :] * keep_mask[:, None]
    lam_im = (modulus * jnp.sin(angles))[None, :] * keep_mask[:, None]
    scanned = lax.associative_scan(combine_pairs, (lam_re, lam_im, scaling * drive_re, scaling * drive_im), axis=0)
    h_re = low_back(low(scanned[2]))
    h_im = low_back(low(scanned[3]))
    mixed = matmul(h_re, c_proj[0]) - matmul(h_im, c_proj[1]) + skip * u_low
    g_low = low(gelu_tanh(low_back(mixed)))
    gated = low_back(matmul(g_low, glu))
    return inputs + gated[:, :D] * jax.nn.sigmoid(gated[:, D:])

def apply_group(weights, item):
    return group_block(weights, item[0], item[1])

def forward(inputs, weights, keep_all):
    block = jax.checkpoint(partial(apply_group, weights))
    return lax.map(block, (inputs, keep_all))

def reference(tokens, lengths, gain, b_proj, c_proj, skip, nu, theta, gamma_log, glu, out_grad):
    starts = jnp.cumsum(lengths, axis=1) - lengths
    positions = jnp.arange(GROUP_TOK, dtype=jnp.int32)
    hit_mask = jnp.any(positions[None, :, None] == starts[:, None, :].astype(jnp.int32), axis=2)
    keep_all = jnp.where(hit_mask, 0.0, 1.0).astype(jnp.float32)
    weights = (gain, b_proj.astype(jnp.float32), c_proj.astype(jnp.float32), skip, nu, theta, gamma_log, glu.astype(jnp.float32))
    inputs = tokens.astype(jnp.float32)

    def run_block(inputs, weights):
        return forward(inputs, weights, keep_all)
    block_out, pullback = jax.vjp(run_block, inputs, weights)
    in_grad, weight_grads = pullback(out_grad.astype(jnp.float32))
    return (block_out.astype(jnp.bfloat16), in_grad.astype(jnp.bfloat16), weight_grads[0], weight_grads[1], weight_grads[2], weight_grads[3], weight_grads[4], weight_grads[5], weight_grads[6], weight_grads[7])
```

```python
import functools
import math

import jax
import jax.numpy as jnp
from jax import lax
from jax.experimental import pallas as pl
from jax.experimental.pallas import tpu as pltpu
from jax.sharding import PartitionSpec as P

MESH = pl.DeviceIdType.MESH
F32, BF16 = jnp.float32, jnp.bfloat16
EPS = 1e-5
RESET = 256
TILE = 256
BLOCKS = 16
LANES = 128
ROWS = 512
NT = (((1,), (1,)), ((), ()))
TN = (((0,), (0,)), ((), ()))


def mm(a, b, dims=(((1,), (0,)), ((), ()))):
    return lax.dot_general(a, b, dims, preferred_element_type=F32)


def cmul(a, b):
    return a[0] * b[0] - a[1] * b[1], a[0] * b[1] + a[1] * b[0]


def cpow2(a, times):
    for _ in range(times):
        a = cmul(a, a)
    return a


def fold(value):
    return jnp.sum(value.reshape(-1, 8, value.shape[1]), axis=0)


class Place:
    def __init__(self, seq, dp):
        self.seq, self.dp = seq, dp
        self.nx = max(1, math.isqrt(seq // 2))
        self.nz = seq // self.nx
        self.ny = dp // 2
        self.np = self.nx * self.ny
        self.s, self.d = lax.axis_index("seq"), lax.axis_index("dp")
        self.z, self.x = self.s // self.nx, lax.rem(self.s, self.nx)
        self.y, self.c = self.d // 2, lax.rem(self.d, 2)
        self.p = self.x * self.ny + self.y

    def core(self):
        return (self.s, self.y * 2 + 1 - self.c)

    def plane(self, p):
        return (self.z * self.nx + p // self.ny, lax.rem(p, self.ny) * 2 + self.c)

    def line(self, z):
        return (z * self.nx + self.x, self.d)

    def group(self, s):
        return (s, self.d)


def remote(src, dst, send, recv, device):
    return pltpu.make_async_remote_copy(
        src_ref=src, dst_ref=dst, send_sem=send, recv_sem=recv, device_id=device, device_id_type=MESH
    )


class Sum:
    def __init__(self, at, part, out, rc, sc, rx, sx, rz, send, recv):
        self.at, self.part, self.out = at, part, out
        self.rc, self.sc, self.rx, self.sx, self.rz = rc, sc, rx, sx, rz
        self.send, self.recv = send, recv
        self.sent, self.slot, self.pending = [], 0, []
        self.half = ROWS // 2
        self.quarter = self.half // at.np
        self.piece = self.quarter // at.nz
        self.scatter = self.piece % 16 == 0
        self.row0 = pl.multiple_of(at.c * self.half, 16)
        self.row1 = pl.multiple_of(self.row0 + at.p * self.quarter, 16)
        if self.scatter:
            self.row2 = pl.multiple_of(self.row1 + at.z * self.piece, 16)

    def go(self, src, dst, device):
        copy = remote(src, dst, self.send.at[self.slot], self.recv.at[self.slot], device)
        self.slot += 1
        copy.start()
        self.sent.append(copy)
        self.pending.append(copy)

    def arrive(self):
        for copy in self.pending:
            copy.wait_recv()
        self.pending = []

    def start_core(self):
        other = pl.multiple_of((1 - self.at.c) * self.half, 16)
        self.go(self.part.at[pl.ds(other, self.half)], self.rc, self.at.core())

    def start_plane(self):
        at = self.at
        self.arrive()
        own = self.part[pl.ds(self.row0, self.half), :].astype(F32)
        self.sc[...] = (own + self.rc[...].astype(F32)).astype(BF16)
        for o in range(1, at.np):
            p = lax.rem(at.p + o, at.np)
            rows = pl.ds(pl.multiple_of(p * self.quarter, 16), self.quarter)
            self.go(self.sc.at[rows], self.rx.at[o - 1], at.plane(p))

    def start_line(self):
        at = self.at
        self.arrive()
        total = self.sc[pl.ds(pl.multiple_of(at.p * self.quarter, 16), self.quarter), :].astype(F32)
        for o in range(1, at.np):
            total += self.rx[o - 1].astype(F32)
        if self.scatter:
            self.sx[...] = total.astype(BF16)
            for o in range(1, at.nz):
                z = lax.rem(at.z + o, at.nz)
                rows = pl.ds(pl.multiple_of(z * self.piece, 16), self.piece)
                self.go(self.sx.at[rows], self.rz.at[o - 1], at.line(z))
        else:
            self.rz[at.z] = total.astype(BF16)
            for o in range(1, at.nz):
                self.go(self.rz.at[at.z], self.rz.at[at.z], at.line(lax.rem(at.z + o, at.nz)))

    def back_line(self):
        at = self.at
        self.arrive()
        if not self.scatter:
            return
        total = self.sx[pl.ds(pl.multiple_of(at.z * self.piece, 16), self.piece), :].astype(F32)
        for o in range(1, at.nz):
            total += self.rz[o - 1].astype(F32)
        mine = pl.ds(self.row2, self.piece)
        self.out[mine, :] = total.astype(BF16)
        for o in range(1, at.nz):
            self.go(self.out.at[mine], self.out.at[mine], at.line(lax.rem(at.z + o, at.nz)))

    def back_plane(self):
        at = self.at
        mine = pl.ds(self.row1, self.quarter)
        if self.scatter:
            self.arrive()
        else:
            total = self.rz[0].astype(F32)
            for z in range(1, at.nz):
                total += self.rz[z].astype(F32)
            self.out[mine, :] = total.astype(BF16)
        for o in range(1, at.np):
            self.go(self.out.at[mine], self.out.at[mine], at.plane(lax.rem(at.p + o, at.np)))

    def back_core(self):
        self.arrive()
        mine = pl.ds(self.row0, self.half)
        self.go(self.out.at[mine], self.out.at[mine], self.at.core())

    def drain(self):
        for copy in self.sent:
            copy.wait_send()


def kernel(
    seq, dp,
    tok_hbm, og_hbm, b_hbm, c_hbm, glu_hbm, len_ref, gain_ref, skip_ref, nu_ref, theta_ref, gam_ref,
    block_hbm, ing_hbm, grads_ref, small_ref,
    tok, og, bw, cw, gw, bout, xhat, rstd, u, x, h, hl, g, dz, dy, dh,
    edge, init, msg, rmsg, part, rc, sc, rx, sx, rz, sm, smz,
    load_sem, store_sem, msend, mrecv, asend, arecv, ssend, srecv,
):
    at = Place(seq, dp)
    tokens, width = tok.shape
    chan = width // 2
    step = tokens // BLOCKS
    tiles = tokens // TILE
    lo, hi = slice(0, chan), slice(chan, width)

    loads = []

    def load(src, dst):
        copy = pltpu.make_async_copy(src, dst, load_sem.at[len(loads)])
        copy.start()
        loads.append(copy)
        return copy

    tok_in = [load(tok_hbm.at[0, pl.ds(i * TILE, TILE)], tok.at[pl.ds(i * TILE, TILE)]) for i in range(tiles)]
    b_in = [load(b_hbm.at[k], bw.at[:, pl.ds(k * chan, chan)]) for k in range(2)]
    c_in = [load(c_hbm.at[k], cw.at[pl.ds(k * chan, chan)]) for k in range(2)]
    glu_in = load(glu_hbm, gw)
    og_in = load(og_hbm.at[0], og)

    barrier = pltpu.get_barrier_semaphore()
    peers = [at.core()] + [at.group(lax.rem(at.s + o, seq)) for o in range(1, seq)]
    for oy in range(1, at.ny):
        for ox in range(at.nx):
            y, xx = lax.rem(at.y + oy, at.ny), lax.rem(at.x + ox, at.nx)
            peers.append((at.z * at.nx + xx, y * 2 + at.c))
    for peer in peers:
        pl.semaphore_signal(barrier, inc=1, device_id=peer, device_id_type=MESH)

    modulus = jnp.exp(-jnp.exp(nu_ref[...]))
    angle = jnp.exp(theta_ref[...])
    lam = (modulus * jnp.cos(angle), modulus * jnp.sin(angle))
    conj = (lam[0], -lam[1])
    lam_step = cpow2(lam, int(math.log2(step)))
    lam_all = cpow2(lam_step, int(math.log2(BLOCKS)))
    conj_step, conj_all = (lam_step[0], -lam_step[1]), (lam_all[0], -lam_all[1])
    scaling = jnp.exp(gam_ref[...])
    scale2 = jnp.concatenate([scaling, -scaling], axis=1)

    starts, total = [], jnp.int32(0)
    for k in range(len_ref.shape[1]):
        starts.append(total)
        total = total + len_ref[0, k]

    def keep_at(position):
        hit = functools.reduce(jnp.logical_or, [position == start for start in starts])
        return jnp.where(hit, 0.0, 1.0).astype(F32)

    def keep_all(device):
        first = device * tokens
        hits = [jnp.logical_and(start >= first, start < first + tokens) for start in starts]
        return jnp.where(functools.reduce(jnp.logical_or, hits), 0.0, 1.0).astype(F32)

    block_keep = [
        keep_at(at.s * tokens + k * step) if (k * step) % RESET == 0 else None for k in range(BLOCKS)
    ]

    def kept(k, value):
        if block_keep[k] is None:
            return value
        return value[0] * block_keep[k], value[1] * block_keep[k]

    def put(ref, rows, value):
        for k in range(width // LANES):
            ref[k, rows, :] = value[:, k * LANES : (k + 1) * LANES]

    def take(ref, rows):
        return jnp.concatenate([ref[k, rows, :] for k in range(width // LANES)], axis=1)

    gain = gain_ref[...]
    skip = skip_ref[...]
    for copy in b_in:
        copy.wait()
    for i in range(tiles):
        tok_in[i].wait()

    def front(i, carry):
        rows = pl.ds(pl.multiple_of(i * TILE, TILE), TILE)
        value = tok[rows, :].astype(F32)
        centered = value - jnp.mean(value, axis=1, keepdims=True)
        inv = lax.rsqrt(jnp.mean(centered * centered, axis=1, keepdims=True) + EPS)
        normal = centered * inv
        xhat[rows, :] = normal
        rstd[rows, :] = inv
        low = (normal * gain).astype(BF16)
        u[rows, :] = low
        put(x, rows, mm(low, bw[...]).astype(BF16).astype(F32) * scale2)
        return carry

    lax.fori_loop(0, tiles, front, 0)

    def add(a, b):
        return a[0] + b[0], a[1] + b[1]

    halves = chan // LANES

    def rows_of(j):
        return pl.ds(j, BLOCKS, stride=step)

    zeros = jnp.zeros((BLOCKS, chan), F32)

    def strided(ref, j):
        return take_half(ref, rows_of(j), 0), take_half(ref, rows_of(j), halves)

    def take_half(ref, rows, first):
        return jnp.concatenate([ref[first + k, rows, :] for k in range(halves)], axis=1)

    def put_strided(ref, j, value):
        for k in range(halves):
            ref[k, rows_of(j), :] = value[0][:, k * LANES : (k + 1) * LANES]
            ref[halves + k, rows_of(j), :] = value[1][:, k * LANES : (k + 1) * LANES]

    def advance(j, carry):
        return add(cmul(conj, carry), strided(x, j))

    last = lax.fori_loop(0, step, advance, (zeros, zeros), unroll=8)
    edge[:, lo], edge[:, hi] = last

    zero_row = (jnp.zeros((1, chan), F32), jnp.zeros((1, chan), F32))

    def edge_row(k):
        return edge[k : k + 1, lo], edge[k : k + 1, hi]

    state = zero_row
    for k in range(BLOCKS):
        state = add(edge_row(k), cmul(conj_step, kept(k, state)))

    def exchange(which, value):
        msg[which, :, lo], msg[which, :, hi] = value
        copies = []
        for o in range(seq - 1, 0, -1):
            copy = remote(
                msg.at[which], rmsg.at[which, o], msend.at[which, o], mrecv.at[which, o],
                at.group(lax.rem(at.s + o, seq)),
            )
            copy.start()
            copies.append(copy)
        return copies

    def gather(which, factor, copies, ahead):
        for copy in copies:
            copy.wait_recv()
        result = zero_row
        for o in range(seq - 1, 0, -1):
            source = at.s + o if ahead else at.s - o
            slot = seq - o if ahead else o
            there = (rmsg[which, slot, :, lo], rmsg[which, slot, :, hi])
            k = keep_all(source)
            new = add(there, cmul((factor[0] * k, factor[1] * k), result))
            valid = source < seq if ahead else source >= 0
            result = tuple(jnp.where(valid, a, b) for a, b in zip(new, result))
        return result

    pl.semaphore_wait(barrier, len(peers))
    sent_forward = exchange(0, state)
    carry = gather(0, conj_all, sent_forward, False)

    for k in range(BLOCKS):
        begin = kept(k, carry)
        init[k : k + 1, lo], init[k : k + 1, hi] = begin
        if k + 1 < BLOCKS:
            carry = add(edge_row(k), cmul(conj_step, begin))

    def advance_store(j, carry):
        carry = advance(j, carry)
        put_strided(h, j, carry)
        return carry

    lax.fori_loop(0, step, advance_store, (init[:, lo], init[:, hi]), unroll=8)

    for copy in c_in:
        copy.wait()
    glu_in.wait()
    og_in.wait()

    def middle(i, skip_sum):
        rows = pl.ds(pl.multiple_of(i * TILE, TILE), TILE)
        low = take(h, rows).astype(BF16)
        hl[rows, :] = low
        ul = u[rows, :].astype(F32)
        v = mm(low, cw[...]) + skip * ul
        square = v * v
        t = jnp.tanh(0.7978845608028654 * (v + 0.044715 * v * square))
        half = 0.5 * (1.0 + t)
        gl = (v * half).astype(BF16)
        slope = half + 0.5 * v * (1.0 - t * t) * (0.7978845608028654 * (1.0 + 3 * 0.044715 * square))
        g[rows, :] = gl
        value = mm(gl, gw[:, :width])
        s = jax.nn.sigmoid(mm(gl, gw[:, width:]))
        branch = value * s
        bout[rows, :] = (tok[rows, :].astype(F32) + branch).astype(BF16)
        cot = og[rows, :].astype(F32)
        dvalue = (cot * s).astype(BF16)
        dgate = (cot * branch * (1.0 - s)).astype(BF16)
        dz[rows, :width] = dvalue
        dz[rows, width:] = dgate
        back = mm(dvalue, gw[:, :width], NT) + mm(dgate, gw[:, width:], NT)
        dyl = (back * slope).astype(BF16)
        dy[rows, :] = dyl
        put(dh, rows, mm(dyl, cw[...], NT).astype(BF16).astype(F32))
        return skip_sum + fold(dyl.astype(F32) * ul)

    skip_sum = lax.fori_loop(0, tiles, middle, jnp.zeros((8, width), F32))
    out_block = pltpu.make_async_copy(bout, block_hbm.at[0], store_sem.at[0])
    out_block.start()

    def retreat(k, carry):
        j = step - 1 - k
        return cmul(lam, add(strided(dh, j), carry))

    first = lax.fori_loop(0, step, retreat, (zeros, zeros), unroll=8)
    edge[:, lo], edge[:, hi] = first
    state = zero_row
    for k in range(BLOCKS - 1, -1, -1):
        state = kept(k, add(edge_row(k), cmul(lam_step, state)))
    sent_backward = exchange(1, state)

    def stream(k):
        return Sum(
            at, part.at[k], grads_ref.at[k], rc.at[k], sc.at[k], rx.at[k], sx.at[k], rz.at[k],
            asend.at[k], arecv.at[k],
        )

    sums = [stream(k) for k in range(4)]
    part[0] = mm(g[...], dz[:, :width], TN).astype(BF16)
    sums[0].start_core()
    part[1] = mm(g[...], dz[:, width:], TN).astype(BF16)
    sums[1].start_core()
    part[2] = mm(hl[...], dy[...], TN).astype(BF16)
    sums[2].start_core()

    incoming = gather(1, lam_all, sent_backward, True)
    for k in range(BLOCKS - 1, -1, -1):
        edge_k = edge_row(k)
        if k > 0:
            following = kept(k, add(edge_k, cmul(lam_step, incoming)))
        edge[k : k + 1, lo], edge[k : k + 1, hi] = incoming
        if k > 0:
            incoming = following

    def adjoint(j, carry, before):
        sre, sim, pre, pim, gsum = carry
        wre, wim = add(strided(dh, j), (sre, sim))
        yre, yim = before
        xre, xim = strided(x, j)
        pre = pre + (yre * wre + yim * wim)
        pim = pim + (yim * wre - yre * wim)
        gsum = gsum + (xre * wre + xim * wim)
        put_strided(dh, j, (scaling * wre, -scaling * wim))
        sre, sim = cmul(lam, (wre, wim))
        return sre, sim, pre, pim, gsum

    def adjoint_step(k, carry):
        j = step - 1 - k
        return adjoint(j, carry, strided(h, j - 1))

    carry = lax.fori_loop(0, step - 1, adjoint_step, (edge[:, lo], edge[:, hi], zeros, zeros, zeros), unroll=7)
    carry = adjoint(0, carry, (init[:, lo], init[:, hi]))
    pre, pim, gsum = (jnp.sum(part_sum, axis=0, keepdims=True) for part_sum in carry[2:])

    def lower(i, carry):
        rows = pl.ds(pl.multiple_of(i * TILE, TILE), TILE)
        hl[rows, :] = take(dh, rows).astype(BF16)
        return carry

    lax.fori_loop(0, tiles, lower, 0)
    part[3] = mm(u[...], hl[...], TN).astype(BF16)
    sums[3].start_core()
    for one in sums:
        one.start_plane()

    def last_tile(i, gain_sum):
        rows = pl.ds(pl.multiple_of(i * TILE, TILE), TILE)
        du = mm(hl[rows, :], bw[...], NT) + skip * dy[rows, :].astype(F32)
        normal = xhat[rows, :]
        e = gain * du
        mean_e = jnp.mean(e, axis=1, keepdims=True)
        mean_ex = jnp.mean(e * normal, axis=1, keepdims=True)
        grad = og[rows, :].astype(F32) + (e - mean_e - normal * mean_ex) * rstd[rows, :]
        tok[rows, :] = grad.astype(BF16)
        return gain_sum + fold(du * normal)

    gain_sum = lax.fori_loop(0, tiles, last_tile, jnp.zeros((8, width), F32))
    out_ing = pltpu.make_async_copy(tok, ing_hbm.at[0], store_sem.at[1])
    out_ing.start()

    small = [
        jnp.sum(gain_sum, axis=0, keepdims=True),
        jnp.sum(skip_sum, axis=0, keepdims=True),
        jnp.concatenate(
            [
                -jnp.exp(nu_ref[...]) * (lam[0] * pre + lam[1] * pim),
                angle * (lam[0] * pim - lam[1] * pre),
            ],
            axis=1,
        ),
        jnp.concatenate([gsum, gsum], axis=1),
        jnp.zeros((4, width), F32),
    ]
    small_slot = 0
    small_sent = []

    def spread(buffer, index, targets):
        nonlocal small_slot
        copies = []
        for target in targets:
            copy = remote(buffer.at[index], buffer.at[index], ssend.at[small_slot], srecv.at[small_slot], target)
            small_slot += 1
            copy.start()
            copies.append(copy)
        small_sent.extend(copies)
        return copies

    def collect(buffer, count, copies):
        for copy in copies:
            copy.wait_recv()
        value = buffer[0]
        for k in range(1, count):
            value = value + buffer[k]
        return value

    sm_core, sm_plane, sm_line = smz
    sm_core[at.c] = jnp.concatenate(small, axis=0)
    copies = spread(sm_core, at.c, [at.core()])
    for one in sums:
        one.start_line()
    sm_plane[at.p] = collect(sm_core, 2, copies)
    copies = spread(sm_plane, at.p, [at.plane(lax.rem(at.p + o, at.np)) for o in range(1, at.np)])
    for one in sums:
        one.back_line()
    sm_line[at.z] = collect(sm_plane, at.np, copies)
    copies = spread(sm_line, at.z, [at.line(lax.rem(at.z + o, at.nz)) for o in range(1, at.nz)])
    for one in sums:
        one.back_plane()
    small_ref[...] = collect(sm_line, at.nz, copies)
    for one in sums:
        one.back_core()
    for one in sums:
        one.arrive()
    for one in sums:
        one.drain()
    for copy in sent_forward + sent_backward + small_sent:
        copy.wait_send()
    out_block.wait()
    out_ing.wait()


def on_device(seq, dp, tokens, lengths, gain, b_proj, c_proj, skip, nu, theta, gamma_log, glu, out_grad):
    _, count, width = tokens.shape
    chan = nu.shape[0]
    at_nx = max(1, math.isqrt(seq // 2))
    at_nz, at_np = seq // at_nx, at_nx * (dp // 2)
    quarter = ROWS // 2 // at_np
    piece = quarter // at_nz
    rz_shape = (4, at_nz - 1, piece, ROWS) if piece % 16 == 0 else (4, at_nz, quarter, ROWS)
    slots = 2 + 2 * (at_np - 1) + 2 * (at_nz - 1)
    small_slots = 1 + (at_np - 1) + (at_nz - 1)
    anywhere = pl.BlockSpec(memory_space=pl.ANY)
    vmem = pl.BlockSpec(memory_space=pltpu.VMEM)
    smem = pl.BlockSpec(memory_space=pltpu.SMEM)
    dma = pltpu.SemaphoreType.DMA
    scan = pltpu.VMEM((width // LANES, count, LANES), F32)
    wide, low = pltpu.VMEM((count, width), F32), pltpu.VMEM((count, width), BF16)
    block_out, in_grad, grads, small = pl.pallas_call(
        functools.partial(kernel, seq, dp),
        out_shape=(
            jax.ShapeDtypeStruct(tokens.shape, BF16),
            jax.ShapeDtypeStruct(tokens.shape, BF16),
            jax.ShapeDtypeStruct((4, ROWS, ROWS), BF16),
            jax.ShapeDtypeStruct((8, width), F32),
        ),
        in_specs=[anywhere] * 5 + [smem] + [vmem] * 5,
        out_specs=(anywhere, anywhere, vmem, vmem),
        scratch_shapes=[
            low, low,
            pltpu.VMEM((width, 2 * chan), BF16),
            pltpu.VMEM((2 * chan, width), BF16),
            pltpu.VMEM((width, 2 * width), BF16),
            low,
            wide,
            pltpu.VMEM((count, 1), F32),
            low,
            scan, scan,
            low, low,
            pltpu.VMEM((count, 2 * width), BF16),
            low,
            scan,
            pltpu.VMEM((BLOCKS, 2 * chan), F32),
            pltpu.VMEM((BLOCKS, 2 * chan), F32),
            pltpu.VMEM((2, 1, 2 * chan), F32),
            pltpu.VMEM((2, seq, 1, 2 * chan), F32),
            pltpu.VMEM((4, ROWS, ROWS), BF16),
            pltpu.VMEM((4, ROWS // 2, ROWS), BF16),
            pltpu.VMEM((4, ROWS // 2, ROWS), BF16),
            pltpu.VMEM((4, at_np - 1, quarter, ROWS), BF16),
            pltpu.VMEM((4, quarter, ROWS), BF16),
            pltpu.VMEM(rz_shape, BF16),
            pltpu.VMEM((8, width), F32),
            (
                pltpu.VMEM((2, 8, width), F32),
                pltpu.VMEM((at_np, 8, width), F32),
                pltpu.VMEM((at_nz, 8, width), F32),
            ),
            dma((12,)),
            dma((2,)),
            dma((2, seq)),
            dma((2, seq)),
            dma((4, slots)),
            dma((4, slots)),
            dma((small_slots,)),
            dma((small_slots,)),
        ],
        compiler_params=pltpu.CompilerParams(
            collective_id=0, has_side_effects=True, vmem_limit_bytes=56 * 2**20
        ),
    )(
        tokens, out_grad, b_proj, c_proj, glu, lengths,
        gain[None], skip[None], nu[None], theta[None], gamma_log[None],
    )
    grads = grads.astype(F32)
    b_grad = jnp.stack([grads[3][:, :chan], grads[3][:, chan:]])
    c_grad = grads[2].reshape(2, chan, width)
    glu_grad = jnp.concatenate([grads[0], grads[1]], axis=1)
    return (
        block_out, in_grad, small[0], b_grad, c_grad, small[1],
        small[2, :chan], small[2, chan:], small[3, :chan], glu_grad,
    )


def solution(mesh):
    rows, whole = P("dp", "seq", None), P()
    return jax.shard_map(
        functools.partial(on_device, mesh.shape["seq"], mesh.shape["dp"]),
        mesh=mesh,
        in_specs=(rows, P("dp", None)) + (whole,) * 8 + (rows,),
        out_specs=(rows, rows) + (whole,) * 8,
        check_vma=False,
    )
```

```python
import functools
import math

import jax
import jax.numpy as jnp
from jax import lax
from jax.experimental import pallas as pl
from jax.experimental.pallas import tpu as pltpu
from jax.sharding import PartitionSpec as P

MESH = pl.DeviceIdType.MESH
F32, BF16 = jnp.float32, jnp.bfloat16
EPS = 1e-5
TILE = 256
LANES = 128
SUB = 8
STEPS = TILE // SUB
ROWS = 512
NT = (((1,), (1,)), ((), ()))
TN = (((0,), (0,)), ((), ()))


def mm(a, b, dims=(((1,), (0,)), ((), ()))):
    return lax.dot_general(a, b, dims, preferred_element_type=F32)


def add(a, b):
    return a[0] + b[0], a[1] + b[1]


def cmul(a, b):
    return a[0] * b[0] - a[1] * b[1], a[0] * b[1] + a[1] * b[0]


def cpow2(a, times):
    for _ in range(times):
        a = cmul(a, a)
    return a


def fold(value):
    return jnp.sum(value.reshape(-1, 8, value.shape[1]), axis=0)


class Place:
    def __init__(self, seq, dp):
        self.seq, self.dp = seq, dp
        self.nx = max(1, math.isqrt(seq // 2))
        self.nz = seq // self.nx
        self.ny = dp // 2
        plane = self.nx * self.ny
        self.zl = 2 if self.nz % 2 == 0 and (ROWS // 2 // (2 * plane)) % 16 == 0 else 1
        self.near_count, self.far_count = self.zl * plane, self.nz // self.zl

    def here(self):
        self.s, self.d = lax.axis_index("seq"), lax.axis_index("dp")
        self.z, self.x = self.s // self.nx, lax.rem(self.s, self.nx)
        self.y, self.c = self.d // 2, lax.rem(self.d, 2)
        self.zh, self.zo = self.z // self.zl, lax.rem(self.z, self.zl)
        self.q = (self.zo * self.nx + self.x) * self.ny + self.y
        return self

    def core(self):
        return (self.s, self.y * 2 + 1 - self.c)

    def near(self, o):
        q = lax.rem(self.q + o, self.near_count)
        z = self.zh * self.zl + q // (self.nx * self.ny)
        x = lax.rem(q // self.ny, self.nx)
        return (z * self.nx + x, lax.rem(q, self.ny) * 2 + self.c)

    def far(self, o):
        zh = lax.rem(self.zh + o, self.far_count)
        return ((zh * self.zl + self.zo) * self.nx + self.x, self.d)

    def group(self, o):
        return (lax.rem(self.s + o, self.seq), self.d)

    def peers(self):
        found = [self.core()] + [self.group(o) for o in range(1, self.seq)]
        for oy in range(1, self.ny):
            y = lax.rem(self.y + oy, self.ny)
            for zo in range(self.zl):
                for x in range(self.nx):
                    found.append(((self.zh * self.zl + zo) * self.nx + x, y * 2 + self.c))
        return found


def remote(src, dst, send, recv, device):
    return pltpu.make_async_remote_copy(
        src_ref=src, dst_ref=dst, send_sem=send, recv_sem=recv, device_id=device, device_id_type=MESH
    )


class Sum:
    def __init__(self, at, part, out, rc, sc, rx, fz, send, recv):
        self.at, self.part, self.out = at, part, out
        self.rc, self.sc, self.rx, self.fz = rc, sc, rx, fz
        self.send, self.recv = send, recv
        self.sent, self.slot = [], 0
        self.half = ROWS // 2
        self.piece = self.half // at.near_count
        self.row0 = pl.multiple_of(at.c * self.half, 16)

    def go(self, src, dst, device):
        copy = remote(src, dst, self.send.at[self.slot], self.recv.at[self.slot], device)
        self.slot += 1
        copy.start()
        self.sent.append(copy)
        return copy

    def place(self, q):
        return pl.multiple_of(lax.rem(q, self.at.near_count) * self.piece, 16)

    def rows(self, q):
        return pl.ds(pl.multiple_of(self.row0 + self.place(q), 16), self.piece)

    def start_core(self, left, right):
        for k in range(2):
            first = pl.multiple_of((1 - self.at.c if k == 0 else self.at.c) * self.half, self.half)
            rows = pl.ds(first, self.half)

            def columns(n, carry, rows=rows):
                cols = pl.ds(pl.multiple_of(n * self.half, self.half), self.half)
                self.part[rows, cols] = mm(left[:, rows], right[:, cols], TN).astype(BF16)
                return carry

            lax.fori_loop(0, ROWS // self.half, columns, 0)
            if k == 0:
                self.coming = [self.go(self.part.at[rows], self.rc, self.at.core())]

    def both(self, q):
        return self.part[self.rows(q), :].astype(F32) + self.rc[pl.ds(self.place(q), self.piece), :].astype(F32)

    def start_near(self):
        at = self.at
        self.coming[0].wait_recv()
        self.coming = []
        for o in range(1, at.near_count):
            self.sc[o - 1] = self.both(at.q + o).astype(BF16)
            self.coming.append(self.go(self.sc.at[o - 1], self.rx.at[o - 1], at.near(o)))

    def start_far(self):
        at = self.at
        total = self.both(at.q)
        for o in range(1, at.near_count):
            self.coming[o - 1].wait_recv()
            total += self.rx[o - 1].astype(F32)
        self.fz[at.zh] = total.astype(BF16)
        self.coming = [self.go(self.fz.at[at.zh], self.fz.at[at.zh], at.far(o)) for o in range(1, at.far_count)]

    def back_near(self):
        at = self.at
        for copy in self.coming:
            copy.wait_recv()
        total = self.fz[0].astype(F32)
        for k in range(1, at.far_count):
            total += self.fz[k].astype(F32)
        mine = self.rows(at.q)
        self.out[mine, :] = total.astype(BF16)
        src = self.out.at[mine]
        self.coming = [self.go(src, src, at.near(o)) for o in range(1, at.near_count)]
        self.crossing = [self.go(src, src, at.core())]

    def back_core(self):
        at = self.at
        for o in range(1, at.near_count):
            self.coming[o - 1].wait_recv()
            src = self.out.at[self.rows(at.q - o + at.near_count)]
            self.crossing.append(self.go(src, src, at.core()))

    def finish(self):
        for copy in self.crossing:
            copy.wait_recv()
        for copy in self.sent:
            copy.wait_send()


def kernel(
    at,
    tok_hbm, og_hbm, b_hbm, c_hbm, glu_hbm, len_hbm, gain_hbm, skip_hbm, nu_hbm, theta_hbm, gam_hbm,
    block_ref, ing_ref, grads_ref, small_ref,
    tok, og, bw, cw, gw, bout, xhat, rstd, u, x, h, hl, dg, g, dz, dy, dh, order, back_order,
    edge, init, msg, rmsg, part, rc, sc, rx, fz, smc, smn, smf,
    len_ref, gain_ref, skip_ref, nu_ref, theta_ref, gam_ref,
    load_sem, msend, mrecv, asend, arecv, ssend, srecv,
):
    at.here()
    seq = at.seq
    tokens, width = tok.shape
    chan = width // 2
    tiles = tokens // TILE
    blocks = tiles * SUB
    lo, hi = slice(0, chan), slice(chan, width)

    def tile_rows(i):
        return pl.ds(pl.multiple_of(i * TILE, TILE), TILE)

    loads = []

    def load(src, dst):
        copy = pltpu.make_async_copy(src, dst, load_sem.at[len(loads)])
        copy.start()
        loads.append(copy)
        return copy

    def tok_in(i):
        return pltpu.make_async_copy(tok_hbm.at[0, tile_rows(i)], tok.at[tile_rows(i)], load_sem.at[i])

    for i in range(tiles):
        tok_in(i).start()
        loads.append(None)
    vectors = [
        load(src, dst)
        for src, dst in (
            (nu_hbm, nu_ref), (theta_hbm, theta_ref), (gam_hbm, gam_ref), (gain_hbm, gain_ref),
            (skip_hbm, skip_ref), (len_hbm, len_ref),
        )
    ]
    b_in = [load(b_hbm.at[k], bw.at[:, pl.ds(k * chan, chan)]) for k in range(2)]
    c_in = [load(c_hbm.at[k], cw.at[pl.ds(k * chan, chan)]) for k in range(2)]
    glu_in = load(glu_hbm, gw)
    og_in = load(og_hbm.at[0], og)

    barrier = pltpu.get_barrier_semaphore()
    peers = at.peers()
    for peer in peers:
        pl.semaphore_signal(barrier, inc=1, device_id=peer, device_id_type=MESH)

    first = lax.broadcasted_iota(jnp.int32, (TILE, TILE), 0)
    second = lax.broadcasted_iota(jnp.int32, (TILE, TILE), 1)
    order[...] = (second == (first % SUB) * STEPS + first // SUB).astype(F32).astype(BF16)
    back_order[...] = (first == (second % SUB) * STEPS + second // SUB).astype(F32).astype(BF16)

    for copy in vectors:
        copy.wait()
    modulus = jnp.exp(-jnp.exp(nu_ref[...]))
    angle = jnp.exp(theta_ref[...])
    lam = (modulus * jnp.cos(angle), modulus * jnp.sin(angle))
    conj = (lam[0], -lam[1])
    lam_step = cpow2(lam, int(math.log2(STEPS)))
    lam_all = cpow2(lam_step, int(math.log2(blocks)))
    conj_step, conj_all = (lam_step[0], -lam_step[1]), (lam_all[0], -lam_all[1])
    scaling = jnp.exp(gam_ref[...])
    scale2 = jnp.concatenate([scaling, -scaling], axis=1)

    starts, total = [], jnp.int32(0)
    for k in range(len_ref.shape[1]):
        starts.append(total)
        total = total + len_ref[0, k]

    def keep_at(position):
        hit = functools.reduce(jnp.logical_or, [position == start for start in starts])
        return jnp.where(hit, 0.0, 1.0).astype(F32)

    def keep_all(device):
        begin = device * tokens
        hits = [jnp.logical_and(start >= begin, start < begin + tokens) for start in starts]
        return jnp.where(functools.reduce(jnp.logical_or, hits), 0.0, 1.0).astype(F32)

    tile_keep = [keep_at(at.s * tokens + i * TILE) for i in range(tiles)]

    def kept(k, value):
        if k % SUB:
            return value
        return value[0] * tile_keep[k // SUB], value[1] * tile_keep[k // SUB]

    gain = gain_ref[...]
    skip = skip_ref[...]
    for copy in b_in:
        copy.wait()

    def front(i, carry):
        rows = tile_rows(i)
        tok_in(i).wait()
        value = mm(order[...], tok[rows, :])
        tok[rows, :] = value.astype(BF16)
        centered = value - jnp.mean(value, axis=1, keepdims=True)
        inv = lax.rsqrt(jnp.mean(centered * centered, axis=1, keepdims=True) + EPS)
        normal = centered * inv
        xhat[rows, :] = normal
        rstd[rows, :] = inv
        low = (normal * gain).astype(BF16)
        u[rows, :] = low
        x[rows, :] = mm(low, bw[...]).astype(BF16).astype(F32) * scale2
        return carry

    lax.fori_loop(0, tiles, front, 0)

    def at_step(i, j, count=SUB):
        return pl.ds(pl.multiple_of(i * TILE + j * SUB, count), count)

    def pick(ref, i, j):
        rows = at_step(i, j)
        return ref[rows, lo], ref[rows, hi]

    def pick_tile(ref, i):
        return ref[i * SUB : (i + 1) * SUB, lo], ref[i * SUB : (i + 1) * SUB, hi]

    def both(value):
        return jnp.concatenate(value, axis=1)

    nothing = (jnp.zeros((SUB, chan), F32),) * 2
    zero_row = (jnp.zeros((1, chan), F32),) * 2

    def advance(j, carry):
        return [add(cmul(conj, carry[i]), pick(x, i, j)) for i in range(tiles)]

    def keep_edges(values):
        for i in range(tiles):
            edge[i * SUB : (i + 1) * SUB, :] = both(values[i])

    keep_edges(lax.fori_loop(0, STEPS, advance, [nothing] * tiles, unroll=4))

    def edge_row(k):
        return edge[k : k + 1, lo], edge[k : k + 1, hi]

    state = zero_row
    for k in range(blocks):
        state = add(edge_row(k), cmul(conj_step, kept(k, state)))

    def exchange(which, value):
        msg[which] = both(value)
        copies = []
        for o in range(seq - 1, 0, -1):
            copy = remote(
                msg.at[which], rmsg.at[which, o], msend.at[which, o], mrecv.at[which, o], at.group(o)
            )
            copy.start()
            copies.append(copy)
        return copies

    def gather(which, factor, copies, ahead):
        for copy in copies:
            copy.wait_recv()
        result = zero_row
        for o in range(seq - 1, 0, -1):
            source = at.s + o if ahead else at.s - o
            slot = seq - o if ahead else o
            there = (rmsg[which, slot, :, lo], rmsg[which, slot, :, hi])
            k = keep_all(source)
            new = add(there, cmul((factor[0] * k, factor[1] * k), result))
            valid = source < seq if ahead else source >= 0
            result = tuple(jnp.where(valid, a, b) for a, b in zip(new, result))
        return result

    pl.semaphore_wait(barrier, len(peers))
    sent_forward = exchange(0, state)
    carry = gather(0, conj_all, sent_forward, False)

    for k in range(blocks):
        begin = kept(k, carry)
        init[k : k + 1, :] = both(begin)
        if k + 1 < blocks:
            carry = add(edge_row(k), cmul(conj_step, begin))

    def advance_store(pair, carry):
        states = [[], []]
        for n in range(2):
            carry = advance(pair * 2 + n, carry)
            states[n] = [both(value) for value in carry]
        for i in range(tiles):
            rows = at_step(i, pair * 2, 2 * SUB)
            value = jnp.concatenate([states[0][i], states[1][i]], axis=0)
            h[rows, :] = value
            hl[rows, :] = value.astype(BF16)
        return carry

    lax.fori_loop(0, STEPS // 2, advance_store, [pick_tile(init, i) for i in range(tiles)], unroll=2)

    for copy in c_in:
        copy.wait()
    glu_in.wait()
    og_in.wait()

    def middle(i, skip_sum):
        rows = tile_rows(i)
        ul = u[rows, :].astype(F32)
        v = mm(hl[rows, :], cw[...]) + skip * ul
        square = v * v
        t = jnp.tanh(v * (0.7978845608028654 + 0.7978845608028654 * 0.044715 * square))
        half = 0.5 + 0.5 * t
        wide = v * half
        slope = half + wide * (1.0 - half) * (2 * 0.7978845608028654 + 6 * 0.7978845608028654 * 0.044715 * square)
        gl = wide.astype(BF16)
        g[rows, :] = gl
        value = mm(gl, gw[:, :width])
        s = 0.5 + 0.5 * jnp.tanh(0.5 * mm(gl, gw[:, width:]))
        branch = value * s
        bout[rows, :] = (tok[rows, :].astype(F32) + branch).astype(BF16)
        cot = mm(order[...], og[rows, :])
        og[rows, :] = cot.astype(BF16)
        scaled = cot * s
        dvalue = scaled.astype(BF16)
        dgate = (scaled * (value - branch)).astype(BF16)
        dz[rows, :width] = dvalue
        dz[rows, width:] = dgate
        back = mm(dvalue, gw[:, :width], NT) + mm(dgate, gw[:, width:], NT)
        dyl = (back * slope).astype(BF16)
        dy[rows, :] = dyl
        dh[rows, :] = mm(dyl, cw[...], NT).astype(BF16).astype(F32)
        return skip_sum + fold(dyl.astype(F32) * ul)

    skip_sum = lax.fori_loop(0, tiles, middle, jnp.zeros((8, width), F32))

    def retreat(k, carry):
        j = STEPS - 1 - k
        return [cmul(lam, add(pick(dh, i, j), carry[i])) for i in range(tiles)]

    keep_edges(lax.fori_loop(0, STEPS, retreat, [nothing] * tiles, unroll=4))
    state = zero_row
    for k in range(blocks - 1, -1, -1):
        state = kept(k, add(edge_row(k), cmul(lam_step, state)))
    sent_backward = exchange(1, state)

    sums = [
        Sum(
            at, part.at[k], grads_ref.at[k], rc.at[k], sc.at[k], rx.at[k], fz.at[k], asend.at[k], arecv.at[k]
        )
        for k in range(4)
    ]
    sums[0].start_core(g, dz.at[:, pl.ds(0, width)])
    sums[1].start_core(g, dz.at[:, pl.ds(width, width)])
    sums[0].start_near()
    sums[2].start_core(hl, dy)
    sums[1].start_near()

    incoming = gather(1, lam_all, sent_backward, True)
    for k in range(blocks - 1, -1, -1):
        if k > 0:
            following = kept(k, add(edge_row(k), cmul(lam_step, incoming)))
        edge[k : k + 1, :] = both(incoming)
        if k > 0:
            incoming = following

    def adjoint(j, carry, before):
        states, sums_of = carry
        pre, pim, gsum = sums_of
        result, grads = [], []
        for i in range(tiles):
            wre, wim = add(pick(dh, i, j), states[i])
            yre, yim = before[i]
            xre, xim = pick(x, i, j)
            pre = pre + (yre * wre + yim * wim)
            pim = pim + (yim * wre - yre * wim)
            gsum = gsum + (xre * wre + xim * wim)
            grads.append(both((scaling * wre, -scaling * wim)))
            result.append(cmul(lam, (wre, wim)))
        return (result, (pre, pim, gsum)), grads

    def put_pair(pair, early, late):
        for i in range(tiles):
            dg[at_step(i, pair * 2, 2 * SUB), :] = jnp.concatenate([early[i], late[i]], axis=0).astype(BF16)

    def before_of(j):
        return [pick(h, i, j - 1) for i in range(tiles)]

    def adjoint_pair(k, carry):
        pair = STEPS // 2 - 1 - k
        carry, late = adjoint(pair * 2 + 1, carry, before_of(pair * 2 + 1))
        carry, early = adjoint(pair * 2, carry, before_of(pair * 2))
        put_pair(pair, early, late)
        return carry

    carry = ([pick_tile(edge, i) for i in range(tiles)], (jnp.zeros((SUB, chan), F32),) * 3)
    carry = lax.fori_loop(0, STEPS // 2 - 1, adjoint_pair, carry)
    carry, late = adjoint(1, carry, before_of(1))
    carry, early = adjoint(0, carry, [pick_tile(init, i) for i in range(tiles)])
    put_pair(0, early, late)
    pre, pim, gsum = (jnp.sum(value, axis=0, keepdims=True) for value in carry[1])

    sums[3].start_core(u, dg)

    def put_block(i, carry):
        block_ref[0, tile_rows(i), :] = mm(back_order[...], bout[tile_rows(i), :]).astype(BF16)
        return carry

    lax.fori_loop(0, tiles, put_block, 0)
    sums[3].start_near()
    sums[2].start_near()

    def last_tile(i, gain_sum):
        rows = tile_rows(i)
        du = mm(dg[rows, :], bw[...], NT) + skip * dy[rows, :].astype(F32)
        normal = xhat[rows, :]
        e = gain * du
        mean_e = jnp.mean(e, axis=1, keepdims=True)
        mean_ex = jnp.mean(e * normal, axis=1, keepdims=True)
        grad = og[rows, :].astype(F32) + (e - mean_e - normal * mean_ex) * rstd[rows, :]
        ing_ref[0, rows, :] = mm(back_order[...], grad.astype(BF16)).astype(BF16)
        return gain_sum + fold(du * normal)

    gain_sum = lax.fori_loop(0, tiles, last_tile, jnp.zeros((8, width), F32))

    small = [
        jnp.sum(gain_sum, axis=0, keepdims=True),
        jnp.sum(skip_sum, axis=0, keepdims=True),
        -jnp.exp(nu_ref[...]) * (lam[0] * pre + lam[1] * pim),
        angle * (lam[0] * pim - lam[1] * pre),
        gsum,
    ]
    row = 0
    for value in small:
        for k in range(value.shape[1] // LANES):
            smc[at.c, row : row + 1, :] = value[:, k * LANES : (k + 1) * LANES]
            row += 1
    smc[at.c, row:, :] = jnp.zeros((smc.shape[1] - row, LANES), F32)
    small_slot = 0
    small_sent = []

    def spread(buffer, index, targets):
        nonlocal small_slot
        copies = []
        for target in targets:
            copy = remote(buffer.at[index], buffer.at[index], ssend.at[small_slot], srecv.at[small_slot], target)
            small_slot += 1
            copy.start()
            copies.append(copy)
        small_sent.extend(copies)
        return copies

    def collect(buffer, count, copies):
        for copy in copies:
            copy.wait_recv()
        value = buffer[0]
        for k in range(1, count):
            value = value + buffer[k]
        return value

    copies = spread(smc, at.c, [at.core()])
    sums[0].start_far()
    sums[1].start_far()
    smn[at.q] = collect(smc, 2, copies)
    copies = spread(smn, at.q, [at.near(o) for o in range(1, at.near_count)])
    sums[3].start_far()
    sums[2].start_far()
    sums[0].back_near()
    sums[1].back_near()
    smf[at.zh] = collect(smn, at.near_count, copies)
    copies = spread(smf, at.zh, [at.far(o) for o in range(1, at.far_count)])
    sums[3].back_near()
    sums[2].back_near()
    for k in (0, 1, 3, 2):
        sums[k].back_core()
    small_ref[...] = collect(smf, at.far_count, copies)
    for one in sums:
        one.finish()
    for copy in sent_forward + sent_backward + small_sent:
        copy.wait_send()


def finish(
    block_in, ing_in, grads, small, block_out, in_grad, b_grad, c_grad, glu_grad, gain, skip, nu, theta, gamma,
    wide, sem,
):
    rows, chan = grads.shape[1], b_grad.shape[2]
    copies = []

    def store(src, dst):
        copy = pltpu.make_async_copy(src, dst, sem.at[len(copies)])
        copy.start()
        copies.append(copy)

    store(block_in, block_out)
    store(ing_in, in_grad)
    for k, targets in enumerate((
        [(slice(None), glu_grad.at[:, pl.ds(0, rows)])],
        [(slice(None), glu_grad.at[:, pl.ds(rows, rows)])],
        [(slice(0, chan), c_grad.at[0]), (slice(chan, rows), c_grad.at[1])],
    )):
        wide[k] = grads[k].astype(F32)
        for part, target in targets:
            store(wide.at[k, part], target)
    wide[3] = grads[3].astype(F32)
    for k in range(2):
        store(wide.at[3, :, pl.ds(k * chan, chan)], b_grad.at[k])
    row = 0
    for ref in (gain, skip, nu, theta, gamma):
        ref[...] = small[row : row + ref.shape[0], :]
        row += ref.shape[0]
    for copy in copies:
        copy.wait()


def on_device(seq, dp, tokens, lengths, gain, b_proj, c_proj, skip, nu, theta, gamma_log, glu, out_grad):
    _, count, width = tokens.shape
    chan = nu.shape[0]
    at = Place(seq, dp)
    piece = ROWS // 2 // at.near_count
    slots = 1 + 3 * at.near_count - 2 + at.far_count - 1
    small_slots = 1 + (at.near_count - 1) + (at.far_count - 1)
    blocks = count // STEPS
    anywhere = pl.BlockSpec(memory_space=pl.ANY)
    vmem = pl.BlockSpec(memory_space=pltpu.VMEM)
    dma = pltpu.SemaphoreType.DMA
    wide, low = pltpu.VMEM((count, width), F32), pltpu.VMEM((count, width), BF16)
    block, ing, grads, small = pl.pallas_call(
        functools.partial(kernel, at),
        out_shape=(
            pltpu.VMEM(tokens.shape, BF16),
            pltpu.VMEM(tokens.shape, BF16),
            pltpu.VMEM((4, ROWS, ROWS), BF16),
            pltpu.VMEM((16, LANES), F32),
        ),
        in_specs=[anywhere] * 11,
        out_specs=(vmem,) * 4,
        scratch_shapes=[
            low, low,
            pltpu.VMEM((width, 2 * chan), BF16),
            pltpu.VMEM((2 * chan, width), BF16),
            pltpu.VMEM((width, 2 * width), BF16),
            low,
            wide,
            pltpu.VMEM((count, 1), F32),
            low,
            wide, wide,
            low, low, low,
            pltpu.VMEM((count, 2 * width), BF16),
            low,
            wide,
            pltpu.VMEM((TILE, TILE), BF16),
            pltpu.VMEM((TILE, TILE), BF16),
            pltpu.VMEM((blocks, 2 * chan), F32),
            pltpu.VMEM((blocks, 2 * chan), F32),
            pltpu.VMEM((2, 1, 2 * chan), F32),
            pltpu.VMEM((2, seq, 1, 2 * chan), F32),
            pltpu.VMEM((4, ROWS, ROWS), BF16),
            pltpu.VMEM((4, ROWS // 2, ROWS), BF16),
            pltpu.VMEM((4, at.near_count - 1, piece, ROWS), BF16),
            pltpu.VMEM((4, at.near_count - 1, piece, ROWS), BF16),
            pltpu.VMEM((4, at.far_count, piece, ROWS), BF16),
            pltpu.VMEM((2, 16, LANES), F32),
            pltpu.VMEM((at.near_count, 16, LANES), F32),
            pltpu.VMEM((at.far_count, 16, LANES), F32),
            pltpu.SMEM(lengths.shape, jnp.int32),
            pltpu.VMEM((1, width), F32),
            pltpu.VMEM((1, width), F32),
            pltpu.VMEM((1, chan), F32),
            pltpu.VMEM((1, chan), F32),
            pltpu.VMEM((1, chan), F32),
            dma((count // TILE + 12,)),
            dma((2, seq)),
            dma((2, seq)),
            dma((4, slots)),
            dma((4, slots)),
            dma((small_slots,)),
            dma((small_slots,)),
        ],
        compiler_params=pltpu.CompilerParams(
            collective_id=0, has_side_effects=True, vmem_limit_bytes=40 * 2**20
        ),
    )(
        *(
            pltpu.with_memory_space_constraint(value, pltpu.HBM)
            for value in (
                tokens, out_grad, b_proj, c_proj, glu, lengths,
                gain[None], skip[None], nu[None], theta[None], gamma_log[None],
            )
        )
    )
    lines = [(k, LANES) for k in (width // LANES,) * 2 + (chan // LANES,) * 3]
    block_out, in_grad, b_grad, c_grad, glu_grad, *rest = pl.pallas_call(
        finish,
        out_shape=(
            jax.ShapeDtypeStruct(tokens.shape, BF16),
            jax.ShapeDtypeStruct(tokens.shape, BF16),
            jax.ShapeDtypeStruct(b_proj.shape, F32),
            jax.ShapeDtypeStruct(c_proj.shape, F32),
            jax.ShapeDtypeStruct(glu.shape, F32),
        ) + tuple(jax.ShapeDtypeStruct(line, F32) for line in lines),
        in_specs=[vmem] * 4,
        out_specs=(anywhere,) * 5 + (vmem,) * 5,
        scratch_shapes=[pltpu.VMEM((4, ROWS, ROWS), F32), dma((8,))],
        compiler_params=pltpu.CompilerParams(vmem_limit_bytes=16 * 2**20),
    )(block, ing, grads, small)
    gain_grad, skip_grad, nu_grad, theta_grad, gamma_grad = (value.reshape(-1) for value in rest)
    return (
        block_out, in_grad, gain_grad, b_grad, c_grad, skip_grad, nu_grad, theta_grad, gamma_grad, glu_grad,
    )


def solution(mesh):
    rows, whole = P("dp", "seq", None), P()
    return jax.shard_map(
        functools.partial(on_device, mesh.shape["seq"], mesh.shape["dp"]),
        mesh=mesh,
        in_specs=(rows, P("dp", None)) + (whole,) * 8 + (rows,),
        out_specs=(rows, rows) + (whole,) * 8,
        check_vma=False,
    )
```

```python
import functools
import math

import jax
import jax.numpy as jnp
from jax import lax
from jax.experimental import pallas as pl
from jax.experimental.pallas import tpu as pltpu
from jax.sharding import PartitionSpec as P

MESH = pl.DeviceIdType.MESH
F32, BF16 = jnp.float32, jnp.bfloat16
EPS = 1e-5
TILE = 256
LANES = 128
SUB = 8
STEPS = TILE // SUB
ROWS = 512
NT = (((1,), (1,)), ((), ()))
TN = (((0,), (0,)), ((), ()))


def mm(a, b, dims=(((1,), (0,)), ((), ()))):
    return lax.dot_general(a, b, dims, preferred_element_type=F32)


def add(a, b):
    return a[0] + b[0], a[1] + b[1]


def cmul(a, b):
    return a[0] * b[0] - a[1] * b[1], a[0] * b[1] + a[1] * b[0]


def cpow2(a, times):
    for _ in range(times):
        a = cmul(a, a)
    return a


def fold(value):
    return jnp.sum(value.reshape(-1, 8, value.shape[1]), axis=0)


class Place:
    def __init__(self, seq, dp):
        self.seq, self.dp = seq, dp
        self.nx = max(1, math.isqrt(seq // 2))
        self.nz = seq // self.nx
        self.ny = dp // 2
        plane = self.nx * self.ny
        self.zl = 2 if self.nz % 2 == 0 and (ROWS // 2 // (2 * plane)) % 16 == 0 else 1
        self.near_count, self.far_count = self.zl * plane, self.nz // self.zl
        self.sizes = (self.zl, self.nx, self.ny)

    def here(self):
        self.s, self.d = lax.axis_index("seq"), lax.axis_index("dp")
        self.z, self.x = self.s // self.nx, lax.rem(self.s, self.nx)
        self.y, self.c = self.d // 2, lax.rem(self.d, 2)
        self.zh, self.zo = self.z // self.zl, lax.rem(self.z, self.zl)
        self.q = (self.zo * self.nx + self.x) * self.ny + self.y
        self.inner = (self.zo, self.x, self.y)
        return self

    def member(self, inner):
        return ((self.zh * self.zl + inner[0]) * self.nx + inner[1], inner[2] * 2 + self.c)

    def core(self):
        return (self.s, self.y * 2 + 1 - self.c)

    def near(self, o):
        q = lax.rem(self.q + o, self.near_count)
        return self.member((q // (self.nx * self.ny), lax.rem(q // self.ny, self.nx), lax.rem(q, self.ny)))

    def far(self, o):
        zh = lax.rem(self.zh + o, self.far_count)
        return ((zh * self.zl + self.zo) * self.nx + self.x, self.d)

    def group(self, o):
        return (lax.rem(self.s + o, self.seq), self.d)

    def peers(self):
        found = [self.core()] + [self.group(o) for o in range(1, self.seq)]
        for oy in range(1, self.ny):
            y = lax.rem(self.y + oy, self.ny)
            for zo in range(self.zl):
                for x in range(self.nx):
                    found.append(((self.zh * self.zl + zo) * self.nx + x, y * 2 + self.c))
        return found


def remote(src, dst, send, recv, device):
    copy = pltpu.make_async_remote_copy(
        src_ref=src, dst_ref=dst, send_sem=send, recv_sem=recv, device_id=device, device_id_type=MESH
    )
    copy.start()


def take(ref, sem):
    pltpu.make_async_copy(ref, ref, sem).wait()


class Sum:
    @staticmethod
    def scratch(at, width, first, last):
        half, piece = ROWS // 2, ROWS // 2 // at.near_count
        count = at.near_count // (1 if first is None else at.sizes[first])
        dma = pltpu.SemaphoreType.DMA
        shapes = [(half, width), (count - 1, piece, width), (count - 1, piece, width), (at.far_count, piece, width)]
        if first is not None:
            shapes += [(half // 2, width), (half // 2, width)]
        return [pltpu.VMEM(shape, BF16) for shape in shapes] + [
            dma((1,)), dma((5 + (first is not None) + 2 * (last is not None),))
        ]

    def __init__(self, at, first, last, out, part, rc, sc, rx, fz, *rest):
        self.at, self.first, self.last, self.out, self.part = at, first, last, out, part
        self.rc, self.sc, self.rx, self.fz = rc, sc, rx, fz
        self.send, self.recv = rest[-2:]
        if first is not None:
            self.s1, self.r1 = rest[:2]
        self.sent = 0
        self.half = ROWS // 2
        self.piece = self.half // at.near_count
        self.row0 = pl.multiple_of(at.c * self.half, 16)
        self.major = first if first is not None else last if last is not None else 0
        self.axes = [self.major] + [k for k in range(3) if k != self.major]
        self.rest = math.prod(at.sizes[k] for k in self.axes[1:])
        self.me = 0
        for k in self.axes:
            self.me = self.me * at.sizes[k] + at.inner[k]
        self.base = at.inner[self.major] * self.rest

    def others(self, axis):
        at = self.at
        count = at.near_count if axis is None else self.rest
        first = 0 if axis is None else self.base
        for o in range(1, count):
            place = first + lax.rem(self.me - first + o, count)
            inner, left = [None] * 3, place
            for k in reversed(self.axes):
                inner[k] = lax.rem(left, at.sizes[k])
                left = left // at.sizes[k]
            yield at.member(inner), place

    def mirror(self):
        inner = list(self.at.inner)
        inner[self.major] = 1 - inner[self.major]
        return self.at.member(inner)

    def go(self, slot, src, dst, device):
        remote(src, dst, self.send.at[0], self.recv.at[slot], device)
        self.sent += math.prod(src.shape[:-1])

    def share(self, slot, src, device):
        self.go(slot, src, src, device)

    def drain(self):
        if self.sent:
            take(self.part.at[pl.ds(0, self.sent)], self.send.at[0])
        self.sent = 0

    def local(self, place, count=1):
        return pl.ds(pl.multiple_of(place * self.piece, 16), count * self.piece)

    def rows(self, place, count=1):
        return pl.ds(pl.multiple_of(self.row0 + place * self.piece, 16), count * self.piece)

    def theirs(self):
        return (1 - self.at.inner[self.major]) * self.rest

    def start_core(self):
        other = pl.ds(pl.multiple_of((1 - self.at.c) * self.half, self.half), self.half)
        self.go(0, self.part.at[other], self.rc, self.at.core())

    def both(self, place, count=1):
        mine = self.part[self.rows(place, count), :].astype(F32)
        return mine + self.rc[self.local(place, count), :].astype(F32)

    def start_axis(self):
        take(self.rc, self.recv.at[0])
        self.drain()
        if self.first is not None:
            self.s1[...] = self.both(self.theirs(), self.rest).astype(BF16)
            self.go(5, self.s1, self.r1, self.mirror())

    def held(self, place):
        value = self.both(place)
        if self.first is not None:
            value = value + self.r1[self.local(place - self.base), :].astype(F32)
        return value

    def start_near(self):
        if self.first is not None:
            take(self.r1, self.recv.at[5])
            self.drain()
        for o, (device, place) in enumerate(self.others(self.first)):
            self.sc[o] = self.held(place).astype(BF16)
            self.go(1, self.sc.at[o], self.rx.at[o], device)

    def start_far(self):
        at = self.at
        total = self.held(self.me)
        take(self.rx, self.recv.at[1])
        self.drain()
        for o in range(self.rx.shape[0]):
            total += self.rx[o].astype(F32)
        self.fz[at.zh] = total.astype(BF16)
        for o in range(1, at.far_count):
            self.share(2, self.fz.at[at.zh], at.far(o))

    def back_near(self):
        at = self.at
        if at.far_count > 1:
            take(self.fz.at[pl.ds(0, at.far_count - 1)], self.recv.at[2])
        self.drain()
        total = self.fz[0].astype(F32)
        for k in range(1, at.far_count):
            total += self.fz[k].astype(F32)
        mine = self.rows(self.me)
        self.out[mine, :] = total.astype(BF16)
        for device, _ in self.others(self.last):
            self.share(3, self.out.at[mine], device)

    def back_axis(self):
        count = self.at.near_count if self.last is None else self.rest
        take(self.out.at[pl.ds(0, (count - 1) * self.piece)], self.recv.at[3])
        self.drain()
        src = self.out.at[self.rows(0 if self.last is None else self.base, count)]
        if self.last is not None:
            self.share(self.recv.shape[0] - 2, src, self.mirror())
        self.share(4, src, self.at.core())

    def back_core(self):
        if self.last is not None:
            src = self.out.at[self.rows(self.theirs(), self.rest)]
            take(src, self.recv.at[self.recv.shape[0] - 2])
            self.drain()
            self.share(self.recv.shape[0] - 1, src, self.at.core())

    def finish(self):
        count = self.at.near_count if self.last is None else self.rest
        took = self.out.at[pl.ds(0, count * self.piece)]
        take(took, self.recv.at[4])
        if self.last is not None:
            take(took, self.recv.at[self.recv.shape[0] - 1])
        self.drain()


STAGES = {
    "a": "start_axis", "n": "start_near", "f": "start_far",
    "b": "back_near", "x": "back_axis", "c": "back_core", "e": "finish",
}


PLAN = (
    ("m01", "m23", "m45", "a0", "a1", "a2", "a3", "n3",),
    (),
    ("a4", "a5", "n5",),
    ("m67",),
    (),
    ("a6", "a7", "n0", "n1", "n2",),
    (
        "s0", "n4", "f3", "s1", "f5", "n6", "n7", "f0", "f1", "f2", "b3", "f4", "s2", "b5",
        "f6", "f7", "b0", "b1", "b2", "s3", "x3", "b4", "x5", "b6", "c3", "e3", "b7", "x0",
        "x1", "x2", "x4", "c0", "e0", "c5", "e5", "x6", "c1", "x7", "c2", "c6", "e6", "c4",
        "e1", "c7", "e7", "e2", "e4",
    ),
)
AXES = (
    (0, None), (1, 1), (2, 2), (None, None), (0, 0), (None, 0), (1, None), (0, None),
)


def unit_specs(at):
    return AXES if at.sizes == (2, 2, 2) else ((None, None),) * len(AXES)


def kernel(
    at,
    tok_hbm, og_hbm, b_hbm, c_hbm, glu_hbm, len_hbm, gain_hbm, skip_hbm, nu_hbm, theta_hbm, gam_hbm,
    block_ref, ing_ref, out_refs, small_ref,
    tok, og, bw, cw, gw, bout, xhat, rstd, u, x, h, hl, dg, ut, ht, gt, dz, dy, dh, order, back_order,
    edge, init, msg, rmsg, part, units, smc, smn, smf,
    len_ref, vectors,
    load_sem, msend, mrecv, ssend, srecv,
):
    at.here()
    seq = at.seq
    tokens, width = tok.shape
    chan = width // 2
    tiles = tokens // TILE
    blocks = tiles * SUB
    lo, hi = slice(0, chan), slice(chan, width)

    def tile_rows(i):
        return pl.ds(pl.multiple_of(i * TILE, TILE), TILE)

    barrier = pltpu.get_barrier_semaphore()
    peers = at.peers()
    for peer in peers:
        pl.semaphore_signal(barrier, inc=1, device_id=peer, device_id_type=MESH)

    def tok_in(i):
        return pltpu.make_async_copy(tok_hbm.at[0, tile_rows(i)], tok.at[tile_rows(i)], load_sem.at[6 + i])

    def load(src, dst, sem):
        pltpu.make_async_copy(src, dst, load_sem.at[sem]).start()

    vector_at, spans = 0, []
    for src in (nu_hbm, theta_hbm, gam_hbm, gain_hbm, skip_hbm):
        here = pl.ds(vector_at, src.shape[1])
        load(src, vectors.at[:, here], 0)
        spans.append(here)
        vector_at += src.shape[1]
    load(len_hbm, len_ref, 1)
    tok_in(0).start()
    for k in range(2):
        load(b_hbm.at[k], bw.at[:, pl.ds(k * chan, chan)], 2)
    for i in range(1, tiles):
        tok_in(i).start()
    for k in range(2):
        load(c_hbm.at[k], cw.at[pl.ds(k * chan, chan)], 3)
    load(glu_hbm, gw, 4)
    load(og_hbm.at[0], og, 5)

    first = lax.broadcasted_iota(jnp.int32, (TILE, TILE), 0)
    second = lax.broadcasted_iota(jnp.int32, (TILE, TILE), 1)
    order[...] = (second == (first % SUB) * STEPS + first // SUB).astype(F32).astype(BF16)
    back_order[...] = (first == (second % SUB) * STEPS + second // SUB).astype(F32).astype(BF16)

    take(vectors, load_sem.at[0])
    take(len_ref, load_sem.at[1])
    nu, theta, gamma, gain, skip = (vectors[:, here] for here in spans)
    modulus = jnp.exp(-jnp.exp(nu))
    angle = jnp.exp(theta)
    lam = (modulus * jnp.cos(angle), modulus * jnp.sin(angle))
    conj = (lam[0], -lam[1])
    lam_step = cpow2(lam, int(math.log2(STEPS)))
    lam_all = cpow2(lam_step, int(math.log2(blocks)))
    conj_step, conj_all = (lam_step[0], -lam_step[1]), (lam_all[0], -lam_all[1])
    scaling = jnp.exp(gamma)
    scale2 = jnp.concatenate([scaling, -scaling], axis=1)

    starts, total = [], jnp.int32(0)
    for k in range(len_ref.shape[1]):
        starts.append(total)
        total = total + len_ref[0, k]

    def keep_at(position):
        hit = functools.reduce(jnp.logical_or, [position == start for start in starts])
        return jnp.where(hit, 0.0, 1.0).astype(F32)

    def keep_all(device):
        begin = device * tokens
        hits = [jnp.logical_and(start >= begin, start < begin + tokens) for start in starts]
        return jnp.where(functools.reduce(jnp.logical_or, hits), 0.0, 1.0).astype(F32)

    tile_keep = [keep_at(at.s * tokens + i * TILE) for i in range(tiles)]

    def kept(k, value):
        if k % SUB:
            return value
        return value[0] * tile_keep[k // SUB], value[1] * tile_keep[k // SUB]

    take(bw, load_sem.at[2])

    def front(i, carry):
        rows = tile_rows(i)
        tok_in(i).wait()
        value = mm(order[...], tok[rows, :])
        tok[rows, :] = value.astype(BF16)
        centered = value - jnp.mean(value, axis=1, keepdims=True)
        inv = lax.rsqrt(jnp.mean(centered * centered, axis=1, keepdims=True) + EPS)
        normal = centered * inv
        xhat[rows, :] = normal
        rstd[rows, :] = inv
        low = (normal * gain).astype(BF16)
        u[rows, :] = low
        x[rows, :] = mm(low, bw[...]).astype(BF16).astype(F32) * scale2
        return carry

    lax.fori_loop(0, tiles, front, 0)

    def at_step(i, j, count=SUB):
        return pl.ds(pl.multiple_of(i * TILE + j * SUB, count), count)

    def pick(ref, i, j):
        rows = at_step(i, j)
        return ref[rows, lo], ref[rows, hi]

    def pick_tile(ref, i):
        return ref[i * SUB : (i + 1) * SUB, lo], ref[i * SUB : (i + 1) * SUB, hi]

    def both(value):
        return jnp.concatenate(value, axis=1)

    nothing = (jnp.zeros((SUB, chan), F32),) * 2
    zero_row = (jnp.zeros((1, chan), F32),) * 2

    def advance(j, carry):
        return [add(cmul(conj, carry[i]), pick(x, i, j)) for i in range(tiles)]

    def keep_edges(values):
        for i in range(tiles):
            edge[i * SUB : (i + 1) * SUB, :] = both(values[i])

    keep_edges(lax.fori_loop(0, STEPS, advance, [nothing] * tiles, unroll=4))

    def edge_row(k):
        return edge[k : k + 1, lo], edge[k : k + 1, hi]

    state = zero_row
    for k in range(blocks):
        state = add(edge_row(k), cmul(conj_step, kept(k, state)))

    others = pl.ds(1, seq - 1)

    def exchange(which, value):
        msg[which] = both(value)
        for o in range(seq - 1, 0, -1):
            remote(msg.at[which], rmsg.at[which, o], msend.at[which], mrecv.at[which], at.group(o))

    def gather(which, factor, ahead):
        take(rmsg.at[which, others], mrecv.at[which])
        result = zero_row
        for o in range(seq - 1, 0, -1):
            source = at.s + o if ahead else at.s - o
            slot = seq - o if ahead else o
            there = (rmsg[which, slot, :, lo], rmsg[which, slot, :, hi])
            k = keep_all(source)
            new = add(there, cmul((factor[0] * k, factor[1] * k), result))
            valid = source < seq if ahead else source >= 0
            result = tuple(jnp.where(valid, a, b) for a, b in zip(new, result))
        return result

    pl.semaphore_wait(barrier, len(peers))
    exchange(0, state)

    def turn_u(i, carry):
        ut[:, tile_rows(i)] = u[tile_rows(i), :].T
        return carry

    lax.fori_loop(0, tiles, turn_u, 0)
    carry = gather(0, conj_all, False)

    for k in range(blocks):
        begin = kept(k, carry)
        init[k : k + 1, :] = both(begin)
        if k + 1 < blocks:
            carry = add(edge_row(k), cmul(conj_step, begin))

    def advance_store(pair, carry):
        states = [[], []]
        for n in range(2):
            carry = advance(pair * 2 + n, carry)
            states[n] = [both(value) for value in carry]
        for i in range(tiles):
            rows = at_step(i, pair * 2, 2 * SUB)
            value = jnp.concatenate([states[0][i], states[1][i]], axis=0)
            h[rows, :] = value
            hl[rows, :] = value.astype(BF16)
        return carry

    lax.fori_loop(0, STEPS // 2, advance_store, [pick_tile(init, i) for i in range(tiles)], unroll=2)

    take(cw, load_sem.at[3])
    take(gw, load_sem.at[4])
    take(og, load_sem.at[5])

    def middle(i, skip_sum):
        rows = tile_rows(i)
        ul = u[rows, :].astype(F32)
        v = mm(hl[rows, :], cw[...]) + skip * ul
        square = v * v
        t = jnp.tanh(v * (0.7978845608028654 + 0.7978845608028654 * 0.044715 * square))
        half = 0.5 + 0.5 * t
        wide = v * half
        slope = half + wide * (1.0 - half) * (2 * 0.7978845608028654 + 6 * 0.7978845608028654 * 0.044715 * square)
        gl = wide.astype(BF16)
        gt[:, rows] = gl.T
        ht[:, rows] = hl[rows, :].T
        value = mm(gl, gw[:, :width])
        s = 0.5 + 0.5 * jnp.tanh(0.5 * mm(gl, gw[:, width:]))
        branch = value * s
        bout[rows, :] = (tok[rows, :].astype(F32) + branch).astype(BF16)
        cot = mm(order[...], og[rows, :])
        og[rows, :] = cot.astype(BF16)
        scaled = cot * s
        dvalue = scaled.astype(BF16)
        dgate = (scaled * (value - branch)).astype(BF16)
        dz[rows, :width] = dvalue
        dz[rows, width:] = dgate
        back = mm(dvalue, gw[:, :width], NT) + mm(dgate, gw[:, width:], NT)
        dyl = (back * slope).astype(BF16)
        dy[rows, :] = dyl
        dh[rows, :] = mm(dyl, cw[...], NT).astype(BF16).astype(F32)
        return skip_sum + fold(dyl.astype(F32) * ul)

    skip_sum = lax.fori_loop(0, tiles, middle, jnp.zeros((8, width), F32))

    def retreat(k, carry):
        j = STEPS - 1 - k
        return [cmul(lam, add(pick(dh, i, j), carry[i])) for i in range(tiles)]

    keep_edges(lax.fori_loop(0, STEPS, retreat, [nothing] * tiles, unroll=4))
    state = zero_row
    for k in range(blocks - 1, -1, -1):
        state = kept(k, add(edge_row(k), cmul(lam_step, state)))
    exchange(1, state)

    sums = [
        Sum(at, first, last, out, part.at[k], *refs)
        for k, ((first, last), out, refs) in enumerate(zip(unit_specs(at), out_refs, units))
    ]
    factors = [(gt, dz, 0), (gt, dz, 2), (ht, dy, 0), (ut, dg, 0)]

    def multiply(pair):
        left, right, column = factors[pair]
        half = ROWS // 2
        for core in (1 - at.c, at.c):
            rows = pl.ds(pl.multiple_of(core * half, half), half)

            def columns(n, carry, rows=rows):
                here = pl.ds(pl.multiple_of((column + n) * chan, chan), chan)
                part[2 * pair + n, rows, :] = mm(left[rows, :], right[:, here]).astype(BF16)
                return carry

            lax.fori_loop(0, 2, columns, 0)
            if core is not at.c:
                for n in range(2):
                    sums[2 * pair + n].start_core()

    def run(point):
        for step in PLAN[point]:
            if step[0] == "m":
                multiply(int(step[1]) // 2)
                continue
            for k in map(int, step[1:]):
                if step[0] == "s":
                    small_stage(k)
                else:
                    getattr(sums[k], STAGES[step[0]])()

    def spread(stage, buffer, index, targets):
        for target in targets:
            remote(buffer.at[index], buffer.at[index], ssend.at[stage], srecv.at[stage], target)

    def collect(stage, buffer):
        count = buffer.shape[0]
        if count > 1:
            take(buffer.at[pl.ds(0, count - 1)], srecv.at[stage])
            take(buffer.at[pl.ds(0, count - 1)], ssend.at[stage])
        value = buffer[0]
        for k in range(1, count):
            value = value + buffer[k]
        return value

    def small_stage(k):
        if k == 0:
            spread(0, smc, at.c, [at.core()])
        elif k == 1:
            smn[at.q] = collect(0, smc)
            spread(1, smn, at.q, [at.near(o) for o in range(1, at.near_count)])
        elif k == 2:
            smf[at.zh] = collect(1, smn)
            spread(2, smf, at.zh, [at.far(o) for o in range(1, at.far_count)])
        else:
            small_ref[...] = collect(2, smf)

    run(0)

    incoming = gather(1, lam_all, True)
    run(1)
    for k in range(blocks - 1, -1, -1):
        if k > 0:
            following = kept(k, add(edge_row(k), cmul(lam_step, incoming)))
        edge[k : k + 1, :] = both(incoming)
        if k > 0:
            incoming = following

    def adjoint(j, carry, before):
        states, sums_of = carry
        pre, pim, gsum = sums_of
        result, grads = [], []
        for i in range(tiles):
            wre, wim = add(pick(dh, i, j), states[i])
            yre, yim = before[i]
            xre, xim = pick(x, i, j)
            pre = pre + (yre * wre + yim * wim)
            pim = pim + (yim * wre - yre * wim)
            gsum = gsum + (xre * wre + xim * wim)
            grads.append(both((scaling * wre, -scaling * wim)))
            result.append(cmul(lam, (wre, wim)))
        return (result, (pre, pim, gsum)), grads

    def put_pair(pair, early, late):
        for i in range(tiles):
            dg[at_step(i, pair * 2, 2 * SUB), :] = jnp.concatenate([early[i], late[i]], axis=0).astype(BF16)

    def before_of(j):
        return [pick(h, i, j - 1) for i in range(tiles)]

    def adjoint_pair(k, carry):
        pair = STEPS // 2 - 1 - k
        carry, late = adjoint(pair * 2 + 1, carry, before_of(pair * 2 + 1))
        carry, early = adjoint(pair * 2, carry, before_of(pair * 2))
        put_pair(pair, early, late)
        return carry

    carry = ([pick_tile(edge, i) for i in range(tiles)], (jnp.zeros((SUB, chan), F32),) * 3)
    carry = lax.fori_loop(0, STEPS // 2 - 1, adjoint_pair, carry)
    carry, late = adjoint(1, carry, before_of(1))
    carry, early = adjoint(0, carry, [pick_tile(init, i) for i in range(tiles)])
    put_pair(0, early, late)
    pre, pim, gsum = (jnp.sum(value, axis=0, keepdims=True) for value in carry[1])

    run(2)
    run(3)

    def put_block(i, carry):
        block_ref[0, tile_rows(i), :] = mm(back_order[...], bout[tile_rows(i), :]).astype(BF16)
        return carry

    lax.fori_loop(0, tiles, put_block, 0)
    run(4)

    def last_tile(i, gain_sum):
        rows = tile_rows(i)
        du = mm(dg[rows, :], bw[...], NT) + skip * dy[rows, :].astype(F32)
        normal = xhat[rows, :]
        e = gain * du
        mean_e = jnp.mean(e, axis=1, keepdims=True)
        mean_ex = jnp.mean(e * normal, axis=1, keepdims=True)
        grad = og[rows, :].astype(F32) + (e - mean_e - normal * mean_ex) * rstd[rows, :]
        ing_ref[0, rows, :] = mm(back_order[...], grad.astype(BF16)).astype(BF16)
        return gain_sum + fold(du * normal)

    gain_sum = lax.fori_loop(0, tiles // 2, last_tile, jnp.zeros((8, width), F32))
    run(5)
    gain_sum = lax.fori_loop(tiles // 2, tiles, last_tile, gain_sum)

    small = [
        jnp.sum(gain_sum, axis=0, keepdims=True),
        jnp.sum(skip_sum, axis=0, keepdims=True),
        -jnp.exp(nu) * (lam[0] * pre + lam[1] * pim),
        angle * (lam[0] * pim - lam[1] * pre),
        gsum,
    ]
    row = 0
    for value in small:
        for k in range(value.shape[1] // LANES):
            smc[at.c, row : row + 1, :] = value[:, k * LANES : (k + 1) * LANES]
            row += 1
    smc[at.c, row:, :] = jnp.zeros((smc.shape[1] - row, LANES), F32)

    run(6)
    for which in range(2):
        take(rmsg.at[which, others], msend.at[which])


def finish(
    block_in, ing_in, sums, small,
    block_out, in_grad, b_grad, c_grad, glu_grad, gain, skip, nu, theta, gamma, wide, sem,
):
    chan = b_grad.shape[2]
    copies = []

    def store(src, dst):
        copy = pltpu.make_async_copy(src, dst, sem.at[len(copies)])
        copy.start()
        copies.append(copy)

    store(block_in, block_out)
    store(ing_in, in_grad)
    for k, value in enumerate(sums):
        wide[k] = value[...].astype(F32)
        if k < 4:
            store(wide.at[k], glu_grad.at[:, pl.ds(k * chan, chan)])
        elif k < 6:
            for n in range(2):
                store(wide.at[k, pl.ds(n * chan, chan)], c_grad.at[n, :, pl.ds((k - 4) * chan, chan)])
        else:
            store(wide.at[k], b_grad.at[k - 6])
    row = 0
    for ref in (gain, skip, nu, theta, gamma):
        ref[...] = small[row : row + ref.shape[0], :]
        row += ref.shape[0]
    for copy in copies:
        copy.wait()


def on_device(seq, dp, tokens, lengths, gain, b_proj, c_proj, skip, nu, theta, gamma_log, glu, out_grad):
    _, count, width = tokens.shape
    chan = nu.shape[0]
    at = Place(seq, dp)
    blocks = count // STEPS
    anywhere = pl.BlockSpec(memory_space=pl.ANY)
    vmem = pl.BlockSpec(memory_space=pltpu.VMEM)
    dma = pltpu.SemaphoreType.DMA
    wide, low = pltpu.VMEM((count, width), F32), pltpu.VMEM((count, width), BF16)
    specs = unit_specs(at)
    held = pl.pallas_call(
        functools.partial(kernel, at),
        out_shape=(
            pltpu.VMEM(tokens.shape, BF16),
            pltpu.VMEM(tokens.shape, BF16),
            [pltpu.VMEM((ROWS, chan), BF16) for _ in specs],
            pltpu.VMEM((16, LANES), F32),
        ),
        in_specs=[anywhere] * 11,
        out_specs=(vmem, vmem, [vmem] * len(specs), vmem),
        scratch_shapes=[
            low, low,
            pltpu.VMEM((width, 2 * chan), BF16),
            pltpu.VMEM((2 * chan, width), BF16),
            pltpu.VMEM((width, 2 * width), BF16),
            low,
            wide,
            pltpu.VMEM((count, 1), F32),
            low,
            wide, wide,
            low, low,
            *[pltpu.VMEM((width, count), BF16)] * 3,
            pltpu.VMEM((count, 2 * width), BF16),
            low,
            wide,
            pltpu.VMEM((TILE, TILE), BF16),
            pltpu.VMEM((TILE, TILE), BF16),
            pltpu.VMEM((blocks, 2 * chan), F32),
            pltpu.VMEM((blocks, 2 * chan), F32),
            pltpu.VMEM((2, 1, 2 * chan), F32),
            pltpu.VMEM((2, seq, 1, 2 * chan), F32),
            pltpu.VMEM((len(specs), ROWS, chan), BF16),
            [Sum.scratch(at, chan, first, last) for first, last in specs],
            pltpu.VMEM((2, 16, LANES), F32),
            pltpu.VMEM((at.near_count, 16, LANES), F32),
            pltpu.VMEM((at.far_count, 16, LANES), F32),
            pltpu.SMEM(lengths.shape, jnp.int32),
            pltpu.VMEM((1, 3 * chan + 2 * width), F32),
            dma((count // TILE + 6,)),
            dma((2,)),
            dma((2,)),
            dma((3,)),
            dma((3,)),
        ],
        compiler_params=pltpu.CompilerParams(
            collective_id=0, has_side_effects=True, vmem_limit_bytes=40 * 2**20
        ),
    )(
        *(
            pltpu.with_memory_space_constraint(value, pltpu.HBM)
            for value in (
                tokens, out_grad, b_proj, c_proj, glu, lengths,
                gain[None], skip[None], nu[None], theta[None], gamma_log[None],
            )
        )
    )
    lines = [(k, LANES) for k in (width // LANES,) * 2 + (chan // LANES,) * 3]
    block_out, in_grad, b_grad, c_grad, glu_grad, *rest = pl.pallas_call(
        finish,
        out_shape=(
            jax.ShapeDtypeStruct(tokens.shape, BF16),
            jax.ShapeDtypeStruct(tokens.shape, BF16),
            jax.ShapeDtypeStruct(b_proj.shape, F32),
            jax.ShapeDtypeStruct(c_proj.shape, F32),
            jax.ShapeDtypeStruct(glu.shape, F32),
        ) + tuple(jax.ShapeDtypeStruct(line, F32) for line in lines),
        in_specs=[vmem, vmem, [vmem] * len(specs), vmem],
        out_specs=(anywhere,) * 5 + (vmem,) * 5,
        scratch_shapes=[pltpu.VMEM((len(specs), ROWS, chan), F32), dma((12,))],
        compiler_params=pltpu.CompilerParams(vmem_limit_bytes=16 * 2**20),
    )(*held)
    gain_grad, skip_grad, nu_grad, theta_grad, gamma_grad = (value.reshape(-1) for value in rest)
    return (
        block_out, in_grad, gain_grad, b_grad, c_grad, skip_grad, nu_grad, theta_grad, gamma_grad, glu_grad,
    )


def solution(mesh):
    rows, whole = P("dp", "seq", None), P()
    return jax.shard_map(
        functools.partial(on_device, mesh.shape["seq"], mesh.shape["dp"]),
        mesh=mesh,
        in_specs=(rows, P("dp", None)) + (whole,) * 8 + (rows,),
        out_specs=(rows, rows) + (whole,) * 8,
        check_vma=False,
    )
```

```python
import functools
import math

import jax
import jax.numpy as jnp
from jax import lax
from jax.experimental import pallas as pl
from jax.experimental.pallas import tpu as pltpu
from jax.sharding import PartitionSpec as P

MESH = pl.DeviceIdType.MESH
F32, BF16 = jnp.float32, jnp.bfloat16
EPS = 1e-5
GROUP = 4
TILE = 256
CHUNK = 256
LANES = 128
SUB = 8
STEPS = TILE // SUB
ROWS = 512
NT = (((1,), (1,)), ((), ()))
TN = (((0,), (0,)), ((), ()))


def mm(a, b, dims=(((1,), (0,)), ((), ()))):
    return lax.dot_general(a, b, dims, preferred_element_type=F32)


def add(a, b):
    return a[0] + b[0], a[1] + b[1]


def cmul(a, b):
    return a[0] * b[0] - a[1] * b[1], a[0] * b[1] + a[1] * b[0]


def cpow2(a, times):
    for _ in range(times):
        a = cmul(a, a)
    return a


def chunks(i):
    for k in range(TILE // CHUNK):
        yield pl.ds(pl.multiple_of(i * TILE + k * CHUNK, CHUNK), CHUNK), slice(k * CHUNK, (k + 1) * CHUNK)


def weave(parts):
    parts = list(parts)
    while parts:
        parts = [part for part in parts if next(part, True) is None]


def fold(value):
    return jnp.sum(value.reshape(-1, 8, value.shape[1]), axis=0)


class Place:
    def __init__(self, seq, dp):
        self.seq, self.dp = seq, dp
        self.nx = max(1, math.isqrt(seq // 2))
        self.nz = seq // self.nx
        self.ny = dp // 2
        plane = self.nx * self.ny
        self.zl = 2 if self.nz % 2 == 0 and (ROWS // 2 // (2 * plane)) % 16 == 0 else 1
        self.near_count, self.far_count = self.zl * plane, self.nz // self.zl
        self.sizes = (self.zl, self.nx, self.ny)

    def here(self):
        self.s, self.d = lax.axis_index("seq"), lax.axis_index("dp")
        self.z, self.x = self.s // self.nx, lax.rem(self.s, self.nx)
        self.y, self.c = self.d // 2, lax.rem(self.d, 2)
        self.zh, self.zo = self.z // self.zl, lax.rem(self.z, self.zl)
        self.q = (self.zo * self.nx + self.x) * self.ny + self.y
        self.inner = (self.zo, self.x, self.y)
        return self

    def member(self, inner):
        return ((self.zh * self.zl + inner[0]) * self.nx + inner[1], inner[2] * 2 + self.c)

    def core(self):
        return (self.s, self.y * 2 + 1 - self.c)

    def near(self, o):
        q = lax.rem(self.q + o, self.near_count)
        return self.member((q // (self.nx * self.ny), lax.rem(q // self.ny, self.nx), lax.rem(q, self.ny)))

    def far(self, o):
        zh = lax.rem(self.zh + o, self.far_count)
        return ((zh * self.zl + self.zo) * self.nx + self.x, self.d)

    def group(self, o):
        return (lax.rem(self.s + o, self.seq), self.d)

    def peers(self):
        found = [self.core()] + [self.group(o) for o in range(1, self.seq)]
        for oy in range(1, self.ny):
            y = lax.rem(self.y + oy, self.ny)
            for zo in range(self.zl):
                for x in range(self.nx):
                    found.append(((self.zh * self.zl + zo) * self.nx + x, y * 2 + self.c))
        return found


def remote(src, dst, send, recv, device):
    copy = pltpu.make_async_remote_copy(
        src_ref=src, dst_ref=dst, send_sem=send, recv_sem=recv, device_id=device, device_id_type=MESH
    )
    copy.start()


def take(ref, sem):
    pltpu.make_async_copy(ref, ref, sem).wait()


class Sum:
    @staticmethod
    def scratch(at, width, first, last):
        half, piece = ROWS // 2, ROWS // 2 // at.near_count
        count = at.near_count // (1 if first is None else at.sizes[first])
        dma = pltpu.SemaphoreType.DMA
        shapes = [(half, width), (count - 1, piece, width), (count - 1, piece, width), (at.far_count, piece, width)]
        if first is not None:
            shapes += [(half // 2, width), (half // 2, width)]
        return [pltpu.VMEM(shape, BF16) for shape in shapes] + [
            dma((1,)), dma((5 + (first is not None) + 2 * (last is not None),))
        ]

    def __init__(self, at, first, last, out, part, rc, sc, rx, fz, *rest):
        self.at, self.first, self.last, self.out, self.part = at, first, last, out, part
        self.rc, self.sc, self.rx, self.fz = rc, sc, rx, fz
        self.send, self.recv = rest[-2:]
        if first is not None:
            self.s1, self.r1 = rest[:2]
        self.sent = 0
        self.half = ROWS // 2
        self.piece = self.half // at.near_count
        self.row0 = pl.multiple_of(at.c * self.half, 16)
        self.major = first if first is not None else last if last is not None else 0
        self.axes = [self.major] + [k for k in range(3) if k != self.major]
        self.rest = math.prod(at.sizes[k] for k in self.axes[1:])
        self.me = 0
        for k in self.axes:
            self.me = self.me * at.sizes[k] + at.inner[k]
        self.base = at.inner[self.major] * self.rest

    def others(self, axis):
        at = self.at
        count = at.near_count if axis is None else self.rest
        first = 0 if axis is None else self.base
        for o in range(1, count):
            place = first + lax.rem(self.me - first + o, count)
            inner, left = [None] * 3, place
            for k in reversed(self.axes):
                inner[k] = lax.rem(left, at.sizes[k])
                left = left // at.sizes[k]
            yield at.member(inner), place

    def mirror(self):
        inner = list(self.at.inner)
        inner[self.major] = 1 - inner[self.major]
        return self.at.member(inner)

    def go(self, slot, src, dst, device):
        remote(src, dst, self.send.at[0], self.recv.at[slot], device)
        self.sent += math.prod(src.shape[:-1])

    def share(self, slot, src, device):
        self.go(slot, src, src, device)

    def drain(self):
        if self.sent:
            take(self.part.at[pl.ds(0, self.sent)], self.send.at[0])
        self.sent = 0

    def local(self, place, count=1):
        return pl.ds(pl.multiple_of(place * self.piece, 16), count * self.piece)

    def rows(self, place, count=1):
        return pl.ds(pl.multiple_of(self.row0 + place * self.piece, 16), count * self.piece)

    def theirs(self):
        return (1 - self.at.inner[self.major]) * self.rest

    def start_core(self):
        other = pl.ds(pl.multiple_of((1 - self.at.c) * self.half, self.half), self.half)
        self.go(0, self.part.at[other], self.rc, self.at.core())

    def both(self, place, count=1):
        mine = self.part[self.rows(place, count), :].astype(F32)
        return mine + self.rc[self.local(place, count), :].astype(F32)

    def start_axis(self):
        take(self.rc, self.recv.at[0])
        self.drain()
        if self.first is not None:
            self.s1[...] = self.both(self.theirs(), self.rest).astype(BF16)
            self.go(5, self.s1, self.r1, self.mirror())

    def held(self, place):
        value = self.both(place)
        if self.first is not None:
            value = value + self.r1[self.local(place - self.base), :].astype(F32)
        return value

    def start_near(self):
        if self.first is not None:
            take(self.r1, self.recv.at[5])
            self.drain()
        for o, (device, place) in enumerate(self.others(self.first)):
            self.sc[o] = self.held(place).astype(BF16)
            self.go(1, self.sc.at[o], self.rx.at[o], device)

    def start_far(self):
        at = self.at
        total = self.held(self.me)
        take(self.rx, self.recv.at[1])
        self.drain()
        for o in range(self.rx.shape[0]):
            total += self.rx[o].astype(F32)
        self.fz[at.zh] = total.astype(BF16)
        for o in range(1, at.far_count):
            self.share(2, self.fz.at[at.zh], at.far(o))

    def back_near(self):
        at = self.at
        if at.far_count > 1:
            take(self.fz.at[pl.ds(0, at.far_count - 1)], self.recv.at[2])
        self.drain()
        total = self.fz[0].astype(F32)
        for k in range(1, at.far_count):
            total += self.fz[k].astype(F32)
        mine = self.rows(self.me)
        self.out[mine, :] = total.astype(BF16)
        for device, _ in self.others(self.last):
            self.share(3, self.out.at[mine], device)

    def back_axis(self):
        count = self.at.near_count if self.last is None else self.rest
        take(self.out.at[pl.ds(0, (count - 1) * self.piece)], self.recv.at[3])
        self.drain()
        src = self.out.at[self.rows(0 if self.last is None else self.base, count)]
        if self.last is not None:
            self.share(self.recv.shape[0] - 2, src, self.mirror())
        self.share(4, src, self.at.core())

    def back_core(self):
        if self.last is not None:
            src = self.out.at[self.rows(self.theirs(), self.rest)]
            take(src, self.recv.at[self.recv.shape[0] - 2])
            self.drain()
            self.share(self.recv.shape[0] - 1, src, self.at.core())

    def finish(self):
        count = self.at.near_count if self.last is None else self.rest
        took = self.out.at[pl.ds(0, count * self.piece)]
        take(took, self.recv.at[4])
        if self.last is not None:
            take(took, self.recv.at[self.recv.shape[0] - 1])
        self.drain()


STAGES = {
    "a": "start_axis", "n": "start_near", "f": "start_far",
    "b": "back_near", "x": "back_axis", "c": "back_core", "e": "finish",
}


PLAN = (
    ("m01", "m23", "m45", "a0", "a1", "a2", "a3", "n3",),
    (),
    ("a4", "a5", "n5",),
    ("m67",),
    (),
    ("a6", "a7", "n0", "n1", "n2",),
    (
        "s0", "n4", "f3", "s1", "f5", "n6", "n7", "f0", "f1", "f2", "b3", "f4", "s2", "b5",
        "f6", "f7", "b0", "b1", "b2", "s3", "x3", "b4", "x5", "b6", "c3", "e3", "b7", "x0",
        "x1", "x2", "x4", "c0", "e0", "c5", "e5", "x6", "c1", "x7", "c2", "c6", "e6", "c4",
        "e1", "c7", "e7", "e2", "e4",
    ),
)
AXES = (
    (0, None), (1, 1), (2, 2), (None, None), (0, 0), (None, 0), (1, None), (0, None),
)


def unit_specs(at):
    return AXES if at.sizes == (2, 2, 2) else ((None, None),) * len(AXES)


def kernel(
    at,
    tok_hbm, og_hbm, b_hbm, c_hbm, glu_hbm, len_hbm, gain_hbm, skip_hbm, nu_hbm, theta_hbm, gam_hbm,
    block_ref, ing_ref, out_refs, small_ref,
    tok, og, bw, cw, gw, bout, xhat, rstd, u, x, h, hl, dg, ut, ht, gt, dz, dy, dh, slope, g, order, back_order,
    edge, init, msg, rmsg, part, units, smc, smn, smf,
    len_ref, vectors,
    load_sem, msend, mrecv, ssend, srecv,
):
    at.here()
    seq = at.seq
    tokens, width = tok.shape
    chan = width // 2
    tiles = tokens // TILE
    blocks = tiles * SUB
    lo, hi = slice(0, chan), slice(chan, width)

    def tile_rows(i):
        return pl.ds(pl.multiple_of(i * TILE, TILE), TILE)

    barrier = pltpu.get_barrier_semaphore()
    peers = at.peers()
    for peer in peers:
        pl.semaphore_signal(barrier, inc=1, device_id=peer, device_id_type=MESH)

    def tok_in(i):
        return pltpu.make_async_copy(tok_hbm.at[0, tile_rows(i)], tok.at[tile_rows(i)], load_sem.at[6 + i])

    def load(src, dst, sem):
        pltpu.make_async_copy(src, dst, load_sem.at[sem]).start()

    vector_at, spans = 0, []
    for src in (nu_hbm, theta_hbm, gam_hbm, gain_hbm, skip_hbm):
        here = pl.ds(vector_at, src.shape[1])
        load(src, vectors.at[:, here], 0)
        spans.append(here)
        vector_at += src.shape[1]
    load(len_hbm, len_ref, 1)
    tok_in(0).start()
    for k in range(2):
        load(b_hbm.at[k], bw.at[:, pl.ds(k * chan, chan)], 2)
    for i in range(1, tiles):
        tok_in(i).start()
    for k in range(2):
        load(c_hbm.at[k], cw.at[pl.ds(k * chan, chan)], 3)
    load(glu_hbm, gw, 4)
    load(og_hbm.at[0], og, 5)

    first = lax.broadcasted_iota(jnp.int32, (TILE, TILE), 0)
    second = lax.broadcasted_iota(jnp.int32, (TILE, TILE), 1)
    order[...] = (second == (first % SUB) * STEPS + first // SUB).astype(F32).astype(BF16)
    back_order[...] = (first == (second % SUB) * STEPS + second // SUB).astype(F32).astype(BF16)

    take(vectors, load_sem.at[0])
    take(len_ref, load_sem.at[1])
    nu, theta, gamma, gain, skip = (vectors[:, here] for here in spans)
    modulus = jnp.exp(-jnp.exp(nu))
    angle = jnp.exp(theta)
    lam = (modulus * jnp.cos(angle), modulus * jnp.sin(angle))
    conj = (lam[0], -lam[1])
    lam_step = cpow2(lam, int(math.log2(STEPS)))
    lam_all = cpow2(lam_step, int(math.log2(blocks)))
    conj_step, conj_all = (lam_step[0], -lam_step[1]), (lam_all[0], -lam_all[1])
    scaling = jnp.exp(gamma)
    scale2 = jnp.concatenate([scaling, -scaling], axis=1)

    starts, total = [], jnp.int32(0)
    for k in range(len_ref.shape[1]):
        starts.append(total)
        total = total + len_ref[0, k]

    def keep_at(position):
        hit = functools.reduce(jnp.logical_or, [position == start for start in starts])
        return jnp.where(hit, 0.0, 1.0).astype(F32)

    def keep_all(device):
        begin = device * tokens
        hits = [jnp.logical_and(start >= begin, start < begin + tokens) for start in starts]
        return jnp.where(functools.reduce(jnp.logical_or, hits), 0.0, 1.0).astype(F32)

    tile_keep = [keep_at(at.s * tokens + i * TILE) for i in range(tiles)]

    def kept(k, value):
        if k % SUB:
            return value
        return value[0] * tile_keep[k // SUB], value[1] * tile_keep[k // SUB]

    take(bw, load_sem.at[2])

    def front_tile(i):
        rows = tile_rows(i)
        tok_in(i).wait()
        values = mm(order[...], tok[rows, :])
        yield
        for here, part in chunks(i):
            value = values[part]
            tok[here, :] = value.astype(BF16)
            centered = value - jnp.mean(value, axis=1, keepdims=True)
            inv = lax.rsqrt(jnp.mean(centered * centered, axis=1, keepdims=True) + EPS)
            normal = centered * inv
            xhat[here, :] = normal
            rstd[here, :] = inv
            u[here, :] = (normal * gain).astype(BF16)
        drive = mm(u[rows, :], bw[...])
        yield
        for here, part in chunks(i):
            x[here, :] = drive[part].astype(BF16).astype(F32) * scale2

    def front(k, carry):
        weave(front_tile(k * GROUP + n) for n in range(GROUP))
        return carry

    lax.fori_loop(0, tiles // GROUP, front, 0)

    def at_step(i, j, count=SUB):
        return pl.ds(pl.multiple_of(i * TILE + j * SUB, count), count)

    def pick(ref, i, j):
        rows = at_step(i, j)
        return ref[rows, lo], ref[rows, hi]

    def pick_tile(ref, i):
        return ref[i * SUB : (i + 1) * SUB, lo], ref[i * SUB : (i + 1) * SUB, hi]

    def both(value):
        return jnp.concatenate(value, axis=1)

    nothing = (jnp.zeros((SUB, chan), F32),) * 2
    zero_row = (jnp.zeros((1, chan), F32),) * 2

    def advance(j, carry):
        return [add(cmul(conj, carry[i]), pick(x, i, j)) for i in range(tiles)]

    def keep_edges(values):
        for i in range(tiles):
            edge[i * SUB : (i + 1) * SUB, :] = both(values[i])

    keep_edges(lax.fori_loop(0, STEPS, advance, [nothing] * tiles, unroll=4))

    def edge_row(k):
        return edge[k : k + 1, lo], edge[k : k + 1, hi]

    state = zero_row
    for k in range(blocks):
        state = add(edge_row(k), cmul(conj_step, kept(k, state)))

    others = pl.ds(1, seq - 1)

    def exchange(which, value):
        msg[which] = both(value)
        for o in range(seq - 1, 0, -1):
            remote(msg.at[which], rmsg.at[which, o], msend.at[which], mrecv.at[which], at.group(o))

    def gather(which, factor, ahead):
        take(rmsg.at[which, others], mrecv.at[which])
        result = zero_row
        for o in range(seq - 1, 0, -1):
            source = at.s + o if ahead else at.s - o
            slot = seq - o if ahead else o
            there = (rmsg[which, slot, :, lo], rmsg[which, slot, :, hi])
            k = keep_all(source)
            new = add(there, cmul((factor[0] * k, factor[1] * k), result))
            valid = source < seq if ahead else source >= 0
            result = tuple(jnp.where(valid, a, b) for a, b in zip(new, result))
        return result

    pl.semaphore_wait(barrier, len(peers))
    exchange(0, state)

    def turn_u(i, carry):
        ut[:, tile_rows(i)] = u[tile_rows(i), :].T
        return carry

    lax.fori_loop(0, tiles, turn_u, 0)
    carry = gather(0, conj_all, False)

    for k in range(blocks):
        begin = kept(k, carry)
        init[k : k + 1, :] = both(begin)
        if k + 1 < blocks:
            carry = add(edge_row(k), cmul(conj_step, begin))

    def advance_store(pair, carry):
        states = [[], []]
        for n in range(2):
            carry = advance(pair * 2 + n, carry)
            states[n] = [both(value) for value in carry]
        for i in range(tiles):
            rows = at_step(i, pair * 2, 2 * SUB)
            value = jnp.concatenate([states[0][i], states[1][i]], axis=0)
            h[rows, :] = value
            hl[rows, :] = value.astype(BF16)
        return carry

    lax.fori_loop(0, STEPS // 2, advance_store, [pick_tile(init, i) for i in range(tiles)], unroll=2)

    take(cw, load_sem.at[3])
    take(gw, load_sem.at[4])
    take(og, load_sem.at[5])

    def middle_tile(i, n, sums_of):
        rows = tile_rows(i)
        ht[:, rows] = hl[rows, :].T
        mixed = mm(hl[rows, :], cw[...])
        yield
        for here, part in chunks(i):
            v = mixed[part] + skip * u[here, :].astype(F32)
            square = v * v
            t = jnp.tanh(v * (0.7978845608028654 + 0.7978845608028654 * 0.044715 * square))
            half = 0.5 + 0.5 * t
            wide = v * half
            slope[n, part, :] = half + wide * (1.0 - half) * (
                2 * 0.7978845608028654 + 6 * 0.7978845608028654 * 0.044715 * square
            )
            g[n, part, :] = wide.astype(BF16)
        gt[:, rows] = g[n].T
        values, gates = mm(g[n], gw[:, :width]), mm(g[n], gw[:, width:])
        cots = mm(order[...], og[rows, :])
        yield
        for here, part in chunks(i):
            value, cot = values[part], cots[part]
            s = 0.5 + 0.5 * jnp.tanh(0.5 * gates[part])
            branch = value * s
            bout[here, :] = (tok[here, :].astype(F32) + branch).astype(BF16)
            og[here, :] = cot.astype(BF16)
            scaled = cot * s
            dz[here, :width] = scaled.astype(BF16)
            dz[here, width:] = (scaled * (value - branch)).astype(BF16)
        back = mm(dz[rows, :], gw[...], NT)
        yield
        for here, part in chunks(i):
            dyl = (back[part] * slope[n, part, :]).astype(BF16)
            dy[here, :] = dyl
            sums_of.append(fold(dyl.astype(F32) * u[here, :].astype(F32)))
        cot_h = mm(dy[rows, :], cw[...], NT)
        yield
        for here, part in chunks(i):
            dh[here, :] = cot_h[part].astype(BF16).astype(F32)

    def middle(k, skip_sum):
        sums_of = [skip_sum]
        weave(middle_tile(k * GROUP + n, n, sums_of) for n in range(GROUP))
        return functools.reduce(jnp.add, sums_of)

    skip_sum = lax.fori_loop(0, tiles // GROUP, middle, jnp.zeros((8, width), F32))

    def retreat(k, carry):
        j = STEPS - 1 - k
        return [cmul(lam, add(pick(dh, i, j), carry[i])) for i in range(tiles)]

    keep_edges(lax.fori_loop(0, STEPS, retreat, [nothing] * tiles, unroll=4))
    state = zero_row
    for k in range(blocks - 1, -1, -1):
        state = kept(k, add(edge_row(k), cmul(lam_step, state)))
    exchange(1, state)

    sums = [
        Sum(at, first, last, out, part.at[k], *refs)
        for k, ((first, last), out, refs) in enumerate(zip(unit_specs(at), out_refs, units))
    ]
    factors = [(gt, dz, 0), (gt, dz, 2), (ht, dy, 0), (ut, dg, 0)]

    def multiply(pair):
        left, right, column = factors[pair]
        half = ROWS // 2
        here = pl.ds(column * chan, 2 * chan)

        def one_half(k, carry):
            core = jnp.where(k == 0, 1 - at.c, at.c)
            rows = pl.ds(pl.multiple_of(core * half, half), half)
            product = mm(left[rows, :], right[:, here]).astype(BF16)
            part[2 * pair, rows, :] = product[:, :chan]
            part[2 * pair + 1, rows, :] = product[:, chan:]

            @pl.when(k == 0)
            def _():
                for n in range(2):
                    sums[2 * pair + n].start_core()

            return carry

        lax.fori_loop(0, 2, one_half, 0)
        for n in range(2):
            sums[2 * pair + n].sent = half

    def run(point):
        for step in PLAN[point]:
            if step[0] == "m":
                multiply(int(step[1]) // 2)
                continue
            for k in map(int, step[1:]):
                if step[0] == "s":
                    small_stage(k)
                else:
                    getattr(sums[k], STAGES[step[0]])()

    def spread(stage, buffer, index, targets):
        for target in targets:
            remote(buffer.at[index], buffer.at[index], ssend.at[stage], srecv.at[stage], target)

    def collect(stage, buffer):
        count = buffer.shape[0]
        if count > 1:
            take(buffer.at[pl.ds(0, count - 1)], srecv.at[stage])
            take(buffer.at[pl.ds(0, count - 1)], ssend.at[stage])
        value = buffer[0]
        for k in range(1, count):
            value = value + buffer[k]
        return value

    def small_stage(k):
        if k == 0:
            spread(0, smc, at.c, [at.core()])
        elif k == 1:
            smn[at.q] = collect(0, smc)
            spread(1, smn, at.q, [at.near(o) for o in range(1, at.near_count)])
        elif k == 2:
            smf[at.zh] = collect(1, smn)
            spread(2, smf, at.zh, [at.far(o) for o in range(1, at.far_count)])
        else:
            small_ref[...] = collect(2, smf)

    run(0)

    incoming = gather(1, lam_all, True)
    run(1)
    for k in range(blocks - 1, -1, -1):
        if k > 0:
            following = kept(k, add(edge_row(k), cmul(lam_step, incoming)))
        edge[k : k + 1, :] = both(incoming)
        if k > 0:
            incoming = following

    def adjoint(j, carry, before):
        states, sums_of = carry
        pre, pim, gsum = sums_of
        result, grads = [], []
        for i in range(tiles):
            wre, wim = add(pick(dh, i, j), states[i])
            yre, yim = before[i]
            xre, xim = pick(x, i, j)
            pre = pre + (yre * wre + yim * wim)
            pim = pim + (yim * wre - yre * wim)
            gsum = gsum + (xre * wre + xim * wim)
            grads.append(both((scaling * wre, -scaling * wim)))
            result.append(cmul(lam, (wre, wim)))
        return (result, (pre, pim, gsum)), grads

    def put_pair(pair, early, late):
        for i in range(tiles):
            dg[at_step(i, pair * 2, 2 * SUB), :] = jnp.concatenate([early[i], late[i]], axis=0).astype(BF16)

    def before_of(j):
        return [pick(h, i, j - 1) for i in range(tiles)]

    def adjoint_pair(k, carry):
        pair = STEPS // 2 - 1 - k
        carry, late = adjoint(pair * 2 + 1, carry, before_of(pair * 2 + 1))
        carry, early = adjoint(pair * 2, carry, before_of(pair * 2))
        put_pair(pair, early, late)
        return carry

    carry = ([pick_tile(edge, i) for i in range(tiles)], (jnp.zeros((SUB, chan), F32),) * 3)
    carry = lax.fori_loop(0, STEPS // 2 - 1, adjoint_pair, carry)
    carry, late = adjoint(1, carry, before_of(1))
    carry, early = adjoint(0, carry, [pick_tile(init, i) for i in range(tiles)])
    put_pair(0, early, late)
    pre, pim, gsum = (jnp.sum(value, axis=0, keepdims=True) for value in carry[1])

    run(2)
    run(3)

    def put_block(i, carry):
        block_ref[0, tile_rows(i), :] = mm(back_order[...], bout[tile_rows(i), :]).astype(BF16)
        return carry

    lax.fori_loop(0, tiles, put_block, 0)
    run(4)

    def last_tile(i, sums_of):
        rows = tile_rows(i)
        dus = mm(dg[rows, :], bw[...], NT)
        yield
        for here, part in chunks(i):
            du = dus[part] + skip * dy[here, :].astype(F32)
            normal = xhat[here, :]
            e = gain * du
            mean_e = jnp.mean(e, axis=1, keepdims=True)
            mean_ex = jnp.mean(e * normal, axis=1, keepdims=True)
            grad = og[here, :].astype(F32) + (e - mean_e - normal * mean_ex) * rstd[here, :]
            og[here, :] = grad.astype(BF16)
            sums_of.append(fold(du * normal))
        result = mm(back_order[...], og[rows, :])
        yield
        ing_ref[0, rows, :] = result.astype(BF16)

    def last(k, gain_sum):
        sums_of = [gain_sum]
        weave(last_tile(k * 2 + n, sums_of) for n in range(2))
        return functools.reduce(jnp.add, sums_of)

    gain_sum = last(0, jnp.zeros((8, width), F32))
    run(5)
    gain_sum = lax.fori_loop(1, tiles // 2, last, gain_sum)

    small = [
        jnp.sum(gain_sum, axis=0, keepdims=True),
        jnp.sum(skip_sum, axis=0, keepdims=True),
        -jnp.exp(nu) * (lam[0] * pre + lam[1] * pim),
        angle * (lam[0] * pim - lam[1] * pre),
        gsum,
    ]
    row = 0
    for value in small:
        for k in range(value.shape[1] // LANES):
            smc[at.c, row : row + 1, :] = value[:, k * LANES : (k + 1) * LANES]
            row += 1
    smc[at.c, row:, :] = jnp.zeros((smc.shape[1] - row, LANES), F32)

    run(6)
    for which in range(2):
        take(rmsg.at[which, others], msend.at[which])


def finish(
    block_in, ing_in, sums, small,
    block_out, in_grad, b_grad, c_grad, glu_grad, gain, skip, nu, theta, gamma, wide, sem,
):
    chan = b_grad.shape[2]
    copies = []

    def store(src, dst):
        copy = pltpu.make_async_copy(src, dst, sem.at[len(copies)])
        copy.start()
        copies.append(copy)

    store(block_in, block_out)
    store(ing_in, in_grad)
    for k, value in enumerate(sums):
        wide[k] = value[...].astype(F32)
        if k < 4:
            store(wide.at[k], glu_grad.at[:, pl.ds(k * chan, chan)])
        elif k < 6:
            for n in range(2):
                store(wide.at[k, pl.ds(n * chan, chan)], c_grad.at[n, :, pl.ds((k - 4) * chan, chan)])
        else:
            store(wide.at[k], b_grad.at[k - 6])
    row = 0
    for ref in (gain, skip, nu, theta, gamma):
        ref[...] = small[row : row + ref.shape[0], :]
        row += ref.shape[0]
    for copy in copies:
        copy.wait()


def on_device(seq, dp, tokens, lengths, gain, b_proj, c_proj, skip, nu, theta, gamma_log, glu, out_grad):
    _, count, width = tokens.shape
    chan = nu.shape[0]
    at = Place(seq, dp)
    blocks = count // STEPS
    anywhere = pl.BlockSpec(memory_space=pl.ANY)
    vmem = pl.BlockSpec(memory_space=pltpu.VMEM)
    dma = pltpu.SemaphoreType.DMA
    wide, low = pltpu.VMEM((count, width), F32), pltpu.VMEM((count, width), BF16)
    specs = unit_specs(at)
    held = pl.pallas_call(
        functools.partial(kernel, at),
        out_shape=(
            pltpu.VMEM(tokens.shape, BF16),
            pltpu.VMEM(tokens.shape, BF16),
            [pltpu.VMEM((ROWS, chan), BF16) for _ in specs],
            pltpu.VMEM((16, LANES), F32),
        ),
        in_specs=[anywhere] * 11,
        out_specs=(vmem, vmem, [vmem] * len(specs), vmem),
        scratch_shapes=[
            low, low,
            pltpu.VMEM((width, 2 * chan), BF16),
            pltpu.VMEM((2 * chan, width), BF16),
            pltpu.VMEM((width, 2 * width), BF16),
            low,
            wide,
            pltpu.VMEM((count, 1), F32),
            low,
            wide, wide,
            low, low,
            *[pltpu.VMEM((width, count), BF16)] * 3,
            pltpu.VMEM((count, 2 * width), BF16),
            low,
            wide,
            pltpu.VMEM((GROUP, TILE, width), F32),
            pltpu.VMEM((GROUP, TILE, width), BF16),
            pltpu.VMEM((TILE, TILE), BF16),
            pltpu.VMEM((TILE, TILE), BF16),
            pltpu.VMEM((blocks, 2 * chan), F32),
            pltpu.VMEM((blocks, 2 * chan), F32),
            pltpu.VMEM((2, 1, 2 * chan), F32),
            pltpu.VMEM((2, seq, 1, 2 * chan), F32),
            pltpu.VMEM((len(specs), ROWS, chan), BF16),
            [Sum.scratch(at, chan, first, last) for first, last in specs],
            pltpu.VMEM((2, 16, LANES), F32),
            pltpu.VMEM((at.near_count, 16, LANES), F32),
            pltpu.VMEM((at.far_count, 16, LANES), F32),
            pltpu.SMEM(lengths.shape, jnp.int32),
            pltpu.VMEM((1, 3 * chan + 2 * width), F32),
            dma((count // TILE + 6,)),
            dma((2,)),
            dma((2,)),
            dma((3,)),
            dma((3,)),
        ],
        compiler_params=pltpu.CompilerParams(
            collective_id=0, has_side_effects=True, vmem_limit_bytes=40 * 2**20
        ),
    )(
        *(
            pltpu.with_memory_space_constraint(value, pltpu.HBM)
            for value in (
                tokens, out_grad, b_proj, c_proj, glu, lengths,
                gain[None], skip[None], nu[None], theta[None], gamma_log[None],
            )
        )
    )
    lines = [(k, LANES) for k in (width // LANES,) * 2 + (chan // LANES,) * 3]
    block_out, in_grad, b_grad, c_grad, glu_grad, *rest = pl.pallas_call(
        finish,
        out_shape=(
            jax.ShapeDtypeStruct(tokens.shape, BF16),
            jax.ShapeDtypeStruct(tokens.shape, BF16),
            jax.ShapeDtypeStruct(b_proj.shape, F32),
            jax.ShapeDtypeStruct(c_proj.shape, F32),
            jax.ShapeDtypeStruct(glu.shape, F32),
        ) + tuple(jax.ShapeDtypeStruct(line, F32) for line in lines),
        in_specs=[vmem, vmem, [vmem] * len(specs), vmem],
        out_specs=(anywhere,) * 5 + (vmem,) * 5,
        scratch_shapes=[pltpu.VMEM((len(specs), ROWS, chan), F32), dma((12,))],
        compiler_params=pltpu.CompilerParams(vmem_limit_bytes=16 * 2**20),
    )(*held)
    gain_grad, skip_grad, nu_grad, theta_grad, gamma_grad = (value.reshape(-1) for value in rest)
    return (
        block_out, in_grad, gain_grad, b_grad, c_grad, skip_grad, nu_grad, theta_grad, gamma_grad, glu_grad,
    )


def solution(mesh):
    rows, whole = P("dp", "seq", None), P()
    return jax.shard_map(
        functools.partial(on_device, mesh.shape["seq"], mesh.shape["dp"]),
        mesh=mesh,
        in_specs=(rows, P("dp", None)) + (whole,) * 8 + (rows,),
        out_specs=(rows, rows) + (whole,) * 8,
        check_vma=False,
    )
```

```python
import functools
import math

import jax
import jax.numpy as jnp
from jax import lax
from jax.experimental import pallas as pl
from jax.experimental.pallas import tpu as pltpu
from jax.sharding import PartitionSpec as P

MESH = pl.DeviceIdType.MESH
F32, BF16 = jnp.float32, jnp.bfloat16
EPS = 1e-5
MIDDLE = 512
GROUP = 4
TILE = 256
CHUNK = 256
LANES = 128
SUB = 8
STEPS = TILE // SUB
ROWS = 512


def mm(a, b):
    return jnp.dot(a, b, preferred_element_type=F32)


def add(a, b):
    return a[0] + b[0], a[1] + b[1]


def cmul(a, b):
    return a[0] * b[0] - a[1] * b[1], a[0] * b[1] + a[1] * b[0]


def cpow2(a, times):
    for _ in range(times):
        a = cmul(a, a)
    return a


def chunks(i, tile=TILE):
    for k in range(tile // CHUNK):
        yield pl.ds(pl.multiple_of(i * tile + k * CHUNK, CHUNK), CHUNK), slice(k * CHUNK, (k + 1) * CHUNK)


def weave(parts):
    parts = list(parts)
    while parts:
        parts = [part for part in parts if next(part, True) is None]


def fold(value):
    return jnp.sum(value.reshape(-1, 8, value.shape[1]), axis=0)


class Place:
    def __init__(self, seq, dp):
        self.seq, self.dp = seq, dp
        self.nx = max(1, math.isqrt(seq // 2))
        self.nz = seq // self.nx
        self.ny = dp // 2
        plane = self.nx * self.ny
        self.zl = 2 if self.nz % 2 == 0 and (ROWS // 2 // (2 * plane)) % 16 == 0 else 1
        self.near_count, self.far_count = self.zl * plane, self.nz // self.zl
        self.sizes = (self.zl, self.nx, self.ny)

    def here(self):
        self.s, self.d = lax.axis_index("seq"), lax.axis_index("dp")
        self.z, self.x = self.s // self.nx, lax.rem(self.s, self.nx)
        self.y, self.c = self.d // 2, lax.rem(self.d, 2)
        self.zh, self.zo = self.z // self.zl, lax.rem(self.z, self.zl)
        self.q = (self.zo * self.nx + self.x) * self.ny + self.y
        self.inner = (self.zo, self.x, self.y)
        return self

    def member(self, inner):
        return ((self.zh * self.zl + inner[0]) * self.nx + inner[1], inner[2] * 2 + self.c)

    def core(self):
        return (self.s, self.y * 2 + 1 - self.c)

    def near(self, o):
        q = lax.rem(self.q + o, self.near_count)
        return self.member((q // (self.nx * self.ny), lax.rem(q // self.ny, self.nx), lax.rem(q, self.ny)))

    def far(self, o):
        zh = lax.rem(self.zh + o, self.far_count)
        return ((zh * self.zl + self.zo) * self.nx + self.x, self.d)

    def group(self, o):
        return (lax.rem(self.s + o, self.seq), self.d)

    def peers(self):
        found = [self.core()] + [self.group(o) for o in range(1, self.seq)]
        for oy in range(1, self.ny):
            y = lax.rem(self.y + oy, self.ny)
            for zo in range(self.zl):
                for x in range(self.nx):
                    found.append(((self.zh * self.zl + zo) * self.nx + x, y * 2 + self.c))
        return found


def remote(src, dst, send, recv, device):
    copy = pltpu.make_async_remote_copy(
        src_ref=src, dst_ref=dst, send_sem=send, recv_sem=recv, device_id=device, device_id_type=MESH
    )
    copy.start()


def take(ref, sem):
    pltpu.make_async_copy(ref, ref, sem).wait()


class Sum:
    @staticmethod
    def scratch(at, width, first, last):
        half, piece = ROWS // 2, ROWS // 2 // at.near_count
        count = at.near_count // (1 if first is None else at.sizes[first])
        dma = pltpu.SemaphoreType.DMA
        shapes = [(half, width), (count - 1, piece, width), (count - 1, piece, width), (at.far_count, piece, width)]
        if first is not None:
            shapes += [(half // 2, width), (half // 2, width)]
        return [pltpu.VMEM(shape, BF16) for shape in shapes] + [
            dma((1,)), dma((5 + (first is not None) + 2 * (last is not None),))
        ]

    def __init__(self, at, first, last, out, part, rc, sc, rx, fz, *rest):
        self.at, self.first, self.last, self.out, self.part = at, first, last, out, part
        self.rc, self.sc, self.rx, self.fz = rc, sc, rx, fz
        self.send, self.recv = rest[-2:]
        if first is not None:
            self.s1, self.r1 = rest[:2]
        self.sent = 0
        self.half = ROWS // 2
        self.piece = self.half // at.near_count
        self.row0 = pl.multiple_of(at.c * self.half, 16)
        self.major = first if first is not None else last if last is not None else 0
        self.axes = [self.major] + [k for k in range(3) if k != self.major]
        self.rest = math.prod(at.sizes[k] for k in self.axes[1:])
        self.me = 0
        for k in self.axes:
            self.me = self.me * at.sizes[k] + at.inner[k]
        self.base = at.inner[self.major] * self.rest

    def others(self, axis):
        at = self.at
        count = at.near_count if axis is None else self.rest
        first = 0 if axis is None else self.base
        for o in range(1, count):
            place = first + lax.rem(self.me - first + o, count)
            inner, left = [None] * 3, place
            for k in reversed(self.axes):
                inner[k] = lax.rem(left, at.sizes[k])
                left = left // at.sizes[k]
            yield at.member(inner), place

    def mirror(self):
        inner = list(self.at.inner)
        inner[self.major] = 1 - inner[self.major]
        return self.at.member(inner)

    def go(self, slot, src, dst, device):
        remote(src, dst, self.send.at[0], self.recv.at[slot], device)
        self.sent += math.prod(src.shape[:-1])

    def share(self, slot, src, device):
        self.go(slot, src, src, device)

    def drain(self):
        if self.sent:
            take(self.part.at[pl.ds(0, self.sent)], self.send.at[0])
        self.sent = 0

    def local(self, place, count=1):
        return pl.ds(pl.multiple_of(place * self.piece, 16), count * self.piece)

    def rows(self, place, count=1):
        return pl.ds(pl.multiple_of(self.row0 + place * self.piece, 16), count * self.piece)

    def theirs(self):
        return (1 - self.at.inner[self.major]) * self.rest

    def start_core(self):
        other = pl.ds(pl.multiple_of((1 - self.at.c) * self.half, self.half), self.half)
        self.go(0, self.part.at[other], self.rc, self.at.core())

    def both(self, place, count=1):
        mine = self.part[self.rows(place, count), :].astype(F32)
        return mine + self.rc[self.local(place, count), :].astype(F32)

    def start_axis(self):
        take(self.rc, self.recv.at[0])
        self.drain()
        if self.first is not None:
            self.s1[...] = self.both(self.theirs(), self.rest).astype(BF16)
            self.go(5, self.s1, self.r1, self.mirror())

    def held(self, place):
        value = self.both(place)
        if self.first is not None:
            value = value + self.r1[self.local(place - self.base), :].astype(F32)
        return value

    def start_near(self):
        if self.first is not None:
            take(self.r1, self.recv.at[5])
            self.drain()
        for o, (device, place) in enumerate(self.others(self.first)):
            self.sc[o] = self.held(place).astype(BF16)
            self.go(1, self.sc.at[o], self.rx.at[o], device)

    def start_far(self):
        at = self.at
        total = self.held(self.me)
        take(self.rx, self.recv.at[1])
        self.drain()
        for o in range(self.rx.shape[0]):
            total += self.rx[o].astype(F32)
        self.fz[at.zh] = total.astype(BF16)
        for o in range(1, at.far_count):
            self.share(2, self.fz.at[at.zh], at.far(o))

    def back_near(self):
        at = self.at
        if at.far_count > 1:
            take(self.fz.at[pl.ds(0, at.far_count - 1)], self.recv.at[2])
        self.drain()
        total = self.fz[0].astype(F32)
        for k in range(1, at.far_count):
            total += self.fz[k].astype(F32)
        mine = self.rows(self.me)
        self.out[mine, :] = total.astype(BF16)
        for device, _ in self.others(self.last):
            self.share(3, self.out.at[mine], device)

    def back_axis(self):
        count = self.at.near_count if self.last is None else self.rest
        take(self.out.at[pl.ds(0, (count - 1) * self.piece)], self.recv.at[3])
        self.drain()
        src = self.out.at[self.rows(0 if self.last is None else self.base, count)]
        if self.last is not None:
            self.share(self.recv.shape[0] - 2, src, self.mirror())
        self.share(4, src, self.at.core())

    def back_core(self):
        if self.last is not None:
            src = self.out.at[self.rows(self.theirs(), self.rest)]
            take(src, self.recv.at[self.recv.shape[0] - 2])
            self.drain()
            self.share(self.recv.shape[0] - 1, src, self.at.core())

    def finish(self):
        count = self.at.near_count if self.last is None else self.rest
        took = self.out.at[pl.ds(0, count * self.piece)]
        take(took, self.recv.at[4])
        if self.last is not None:
            take(took, self.recv.at[self.recv.shape[0] - 1])
        self.drain()


STAGES = {
    "a": "start_axis", "n": "start_near", "f": "start_far",
    "b": "back_near", "x": "back_axis", "c": "back_core", "e": "finish",
}


PLAN = (
    (),
    ("m01", "m23", "m45", "a0", "n0", "a1", "a2", "a3", "n3", ),
    (),
    ("a4", "n4", "a5", ),
    ("m67", "p0", "l0", "a6", "a7", "n7", "f0", "n1", "n2", "l1", "s0", "f3", "s1", "n5", "f4", "n6", "b0", "f1", "f7", "f2", "b3", "s2", "f5", "b4", "f6", "x0", "b1", "b7", "x3", "b2", "s3", "b5", "x4", "b6", "c0", "x1", "c4", "e4", "x7", "e0", "x2", "c3", "e3", "x5", "c1", "x6", "c7", "c5", "e5", "c2", "e1", "c6", "e6", "e7", "e2", ),
)
AXES = ((None, 1), (1, 1), (0, 0), (None, 0), (None, None), (2, None), (1, None), (None, 2))


def unit_specs(at):
    return AXES if at.sizes == (2, 2, 2) else ((None, None),) * len(AXES)


def kernel(
    at,
    tok_hbm, og_hbm, b_hbm, c_hbm, glu_hbm, len_hbm, gain_hbm, skip_hbm, nu_hbm, theta_hbm, gam_hbm,
    block_ref, ing_ref, out_refs, small_ref,
    tok, og, bw, cw, gw, bout, xhat, rstd, u, x, h, hl, dg, bt, ct, gwt, ut, ht, gt, dz, dy, dh, slope, g, order, back_order,
    edge, init, msg, rmsg, part, units, smc, smn, smf,
    len_ref, vectors,
    load_sem, msend, mrecv, ssend, srecv,
):
    at.here()
    seq = at.seq
    tokens, width = tok.shape
    chan = width // 2
    tiles = tokens // TILE
    blocks = tiles * SUB
    lo, hi = slice(0, chan), slice(chan, width)

    def tile_rows(i):
        return pl.ds(pl.multiple_of(i * TILE, TILE), TILE)

    barrier = pltpu.get_barrier_semaphore()
    peers = at.peers()
    for peer in peers:
        pl.semaphore_signal(barrier, inc=1, device_id=peer, device_id_type=MESH)

    def tok_in(i):
        return pltpu.make_async_copy(tok_hbm.at[0, tile_rows(i)], tok.at[tile_rows(i)], load_sem.at[6 + i])

    def load(src, dst, sem):
        pltpu.make_async_copy(src, dst, load_sem.at[sem]).start()

    vector_at, spans = 0, []
    for src in (nu_hbm, theta_hbm, gam_hbm, gain_hbm, skip_hbm):
        here = pl.ds(vector_at, src.shape[1])
        load(src, vectors.at[:, here], 0)
        spans.append(here)
        vector_at += src.shape[1]
    load(len_hbm, len_ref, 1)
    tok_in(0).start()
    for k in range(2):
        load(b_hbm.at[k], bw.at[:, pl.ds(k * chan, chan)], 2)
    for i in range(1, tiles):
        tok_in(i).start()

    first = lax.broadcasted_iota(jnp.int32, (TILE, TILE), 0)
    second = lax.broadcasted_iota(jnp.int32, (TILE, TILE), 1)
    order[...] = (second == (first % SUB) * STEPS + first // SUB).astype(F32).astype(BF16)
    back_order[...] = (first == (second % SUB) * STEPS + second // SUB).astype(F32).astype(BF16)

    take(vectors, load_sem.at[0])
    take(len_ref, load_sem.at[1])
    nu, theta, gamma, gain, skip = (vectors[:, here] for here in spans)
    modulus = jnp.exp(-jnp.exp(nu))
    angle = jnp.exp(theta)
    lam = (modulus * jnp.cos(angle), modulus * jnp.sin(angle))
    conj = (lam[0], -lam[1])
    lam_step = cpow2(lam, int(math.log2(STEPS)))
    lam_all = cpow2(lam_step, int(math.log2(blocks)))
    conj_step, conj_all = (lam_step[0], -lam_step[1]), (lam_all[0], -lam_all[1])
    scaling = jnp.exp(gamma)
    scale2 = jnp.concatenate([scaling, -scaling], axis=1)

    starts, total = [], jnp.int32(0)
    for k in range(len_ref.shape[1]):
        starts.append(total)
        total = total + len_ref[0, k]

    def keep_at(position):
        hit = functools.reduce(jnp.logical_or, [position == start for start in starts])
        return jnp.where(hit, 0.0, 1.0).astype(F32)

    def keep_all(device):
        begin = device * tokens
        hits = [jnp.logical_and(start >= begin, start < begin + tokens) for start in starts]
        return jnp.where(functools.reduce(jnp.logical_or, hits), 0.0, 1.0).astype(F32)

    tile_keep = [keep_at(at.s * tokens + i * TILE) for i in range(tiles)]

    def kept(k, value):
        if k % SUB:
            return value
        return value[0] * tile_keep[k // SUB], value[1] * tile_keep[k // SUB]

    take(bw, load_sem.at[2])

    def front_tile(i):
        rows = tile_rows(i)
        tok_in(i).wait()
        values = mm(order[...], tok[rows, :])
        yield
        for here, part in chunks(i):
            value = values[part]
            tok[here, :] = value.astype(BF16)
            centered = value - jnp.mean(value, axis=1, keepdims=True)
            inv = lax.rsqrt(jnp.mean(centered * centered, axis=1, keepdims=True) + EPS)
            normal = centered * inv
            xhat[here, :] = normal
            rstd[here, :] = inv
            u[here, :] = (normal * gain).astype(BF16)
        drive = mm(u[rows, :], bw[...])
        yield
        for here, part in chunks(i):
            x[here, :] = drive[part].astype(BF16).astype(F32) * scale2

    def front(k, carry):
        weave(front_tile(k * GROUP + n) for n in range(GROUP))
        return carry

    lax.fori_loop(0, tiles // GROUP, front, 0)
    for k in range(2):
        load(c_hbm.at[k], cw.at[pl.ds(k * chan, chan)], 3)
    load(glu_hbm, gw, 4)
    load(og_hbm.at[0], og, 5)

    def at_step(i, j, count=SUB):
        return pl.ds(pl.multiple_of(i * TILE + j * SUB, count), count)

    def pick(ref, i, j):
        rows = at_step(i, j)
        return ref[rows, lo], ref[rows, hi]

    def pick_tile(ref, i):
        return ref[i * SUB : (i + 1) * SUB, lo], ref[i * SUB : (i + 1) * SUB, hi]

    def both(value):
        return jnp.concatenate(value, axis=1)

    nothing = (jnp.zeros((SUB, chan), F32),) * 2
    zero_row = (jnp.zeros((1, chan), F32),) * 2

    def advance(j, carry):
        return [add(cmul(conj, carry[i]), pick(x, i, j)) for i in range(tiles)]

    def keep_edges(values):
        for i in range(tiles):
            edge[i * SUB : (i + 1) * SUB, :] = both(values[i])

    keep_edges(lax.fori_loop(0, STEPS, advance, [nothing] * tiles, unroll=4))

    def edge_row(k):
        return edge[k : k + 1, lo], edge[k : k + 1, hi]

    state = zero_row
    for k in range(blocks):
        state = add(edge_row(k), cmul(conj_step, kept(k, state)))

    def pairs(ahead):
        for o in range(seq - 1, 0, -1):
            to = at.s - o if ahead else at.s + o
            source = at.s + o if ahead else at.s - o
            yield o, (to >= 0 if ahead else to < seq), (to, at.d), (source < seq if ahead else source >= 0)

    def edge_copy(which, o, device):
        return pltpu.make_async_remote_copy(
            src_ref=msg.at[which], dst_ref=rmsg.at[which, o], send_sem=msend.at[which, o],
            recv_sem=mrecv.at[which, o], device_id=device, device_id_type=MESH,
        )

    def exchange(which, value):
        msg[which] = both(value)
        for o, needed, device, _ in pairs(which == 1):
            pl.when(needed)(edge_copy(which, o, device).start)

    def gather(which, factor, ahead):
        for o, _, device, coming in pairs(ahead):
            pl.when(coming)(edge_copy(which, o, device).wait_recv)
        result = zero_row
        for o in range(seq - 1, 0, -1):
            source = at.s + o if ahead else at.s - o
            there = (rmsg[which, o, :, lo], rmsg[which, o, :, hi])
            k = keep_all(source)
            new = add(there, cmul((factor[0] * k, factor[1] * k), result))
            valid = source < seq if ahead else source >= 0
            result = tuple(jnp.where(valid, a, b) for a, b in zip(new, result))
        return result

    pl.semaphore_wait(barrier, len(peers))
    exchange(0, state)

    def turn_u(i, carry):
        ut[:, tile_rows(i)] = u[tile_rows(i), :].T
        return carry

    lax.fori_loop(0, tiles, turn_u, 0)
    for k in range(2):
        bt[k * chan : (k + 1) * chan, :] = bw[:, k * chan : (k + 1) * chan].T
    take(cw, load_sem.at[3])
    for k in range(2):
        ct[:, k * chan : (k + 1) * chan] = cw[k * chan : (k + 1) * chan, :].T
    take(gw, load_sem.at[4])

    def turn_glu(k, carry):
        here = pl.ds(pl.multiple_of(k * chan, chan), chan)
        gwt[here, :] = gw[:, here].T
        return carry

    lax.fori_loop(0, gw.shape[1] // chan, turn_glu, 0)
    carry = gather(0, conj_all, False)

    for k in range(blocks):
        begin = kept(k, carry)
        init[k : k + 1, :] = both(begin)
        if k + 1 < blocks:
            carry = add(edge_row(k), cmul(conj_step, begin))

    def advance_store(pair, carry):
        states = [[], []]
        for n in range(2):
            carry = advance(pair * 2 + n, carry)
            states[n] = [both(value) for value in carry]
        for i in range(tiles):
            rows = at_step(i, pair * 2, 2 * SUB)
            value = jnp.concatenate([states[0][i], states[1][i]], axis=0)
            h[rows, :] = value
            hl[rows, :] = value.astype(BF16)
        return carry

    lax.fori_loop(0, STEPS // 2, advance_store, [pick_tile(init, i) for i in range(tiles)], unroll=2)

    take(og, load_sem.at[5])

    def middle_tile(i, n, sums_of):
        rows = pl.ds(pl.multiple_of(i * MIDDLE, MIDDLE), MIDDLE)
        ht[:, rows] = hl[rows, :].T
        mixed = mm(hl[rows, :], cw[...])
        yield
        for here, part in chunks(i, MIDDLE):
            v = mixed[part] + skip * u[here, :].astype(F32)
            square = v * v
            t = jnp.tanh(v * (0.7978845608028654 + 0.7978845608028654 * 0.044715 * square))
            half = 0.5 + 0.5 * t
            wide = v * half
            slope[n, part, :] = half + wide * (1.0 - half) * (
                2 * 0.7978845608028654 + 6 * 0.7978845608028654 * 0.044715 * square
            )
            g[n, part, :] = wide.astype(BF16)
        gt[:, rows] = g[n].T
        values, gates = mm(g[n], gw[:, :width]), mm(g[n], gw[:, width:])
        cots = [
            mm(order[...], og[tile_rows(i * (MIDDLE // TILE) + k), :]) for k in range(MIDDLE // TILE)
        ]
        yield
        for here, part in chunks(i, MIDDLE):
            value, cot = values[part], cots[part.start // TILE]
            s = 0.5 + 0.5 * jnp.tanh(0.5 * gates[part])
            branch = value * s
            bout[here, :] = (tok[here, :].astype(F32) + branch).astype(BF16)
            og[here, :] = cot.astype(BF16)
            scaled = cot * s
            dz[here, :width] = scaled.astype(BF16)
            dz[here, width:] = (scaled * (value - branch)).astype(BF16)
        back = mm(dz[rows, :], gwt[...])
        yield
        for here, part in chunks(i, MIDDLE):
            dyl = (back[part] * slope[n, part, :]).astype(BF16)
            dy[here, :] = dyl
            sums_of.append(fold(dyl.astype(F32) * u[here, :].astype(F32)))
        cot_h = mm(dy[rows, :], ct[...])
        yield
        for here, part in chunks(i, MIDDLE):
            dh[here, :] = cot_h[part].astype(BF16).astype(F32)

    def middle(k, skip_sum):
        sums_of = [skip_sum]
        count = tokens // MIDDLE
        weave(middle_tile(k * count + n, n, sums_of) for n in range(count))
        return functools.reduce(jnp.add, sums_of)

    skip_sum = middle(0, jnp.zeros((8, width), F32))

    sums = [
        Sum(at, first, last, out, part.at[k], *refs)
        for k, ((first, last), out, refs) in enumerate(zip(unit_specs(at), out_refs, units))
    ]
    factors = [(gt, dz, 0), (gt, dz, 2), (ht, dy, 0), (ut, dg, 0)]

    def multiply(pair):
        left, right, column = factors[pair]
        half = ROWS // 2
        here = pl.ds(column * chan, 2 * chan)

        def one_half(k, carry):
            core = jnp.where(k == 0, 1 - at.c, at.c)
            rows = pl.ds(pl.multiple_of(core * half, half), half)
            product = mm(left[rows, :], right[:, here]).astype(BF16)
            part[2 * pair, rows, :] = product[:, :chan]
            part[2 * pair + 1, rows, :] = product[:, chan:]

            @pl.when(k == 0)
            def _():
                for n in range(2):
                    sums[2 * pair + n].start_core()

            return carry

        lax.fori_loop(0, 2, one_half, 0)
        for n in range(2):
            sums[2 * pair + n].sent = half

    def put_block(i, carry):
        block_ref[0, tile_rows(i), :] = mm(back_order[...], bout[tile_rows(i), :]).astype(BF16)
        return carry

    def last_tile(i, sums_of):
        rows = tile_rows(i)
        dus = mm(dg[rows, :], bt[...])
        yield
        for here, part in chunks(i):
            du = dus[part] + skip * dy[here, :].astype(F32)
            normal = xhat[here, :]
            e = gain * du
            mean_e = jnp.mean(e, axis=1, keepdims=True)
            mean_ex = jnp.mean(e * normal, axis=1, keepdims=True)
            grad = og[here, :].astype(F32) + (e - mean_e - normal * mean_ex) * rstd[here, :]
            og[here, :] = grad.astype(BF16)
            sums_of.append(fold(du * normal))
        result = mm(back_order[...], og[rows, :])
        yield
        ing_ref[0, rows, :] = result.astype(BF16)

    def last(k, gain_sum):
        sums_of = [gain_sum]
        weave(last_tile(k * 2 + n, sums_of) for n in range(2))
        return functools.reduce(jnp.add, sums_of)

    found = {}

    def fill_small():
        small = [
            jnp.sum(found["gain"], axis=0, keepdims=True),
            jnp.sum(skip_sum, axis=0, keepdims=True),
            -jnp.exp(nu) * (lam[0] * found["sums"][0] + lam[1] * found["sums"][1]),
            angle * (lam[0] * found["sums"][1] - lam[1] * found["sums"][0]),
            found["sums"][2],
        ]
        row = 0
        for value in small:
            for k in range(value.shape[1] // LANES):
                smc[at.c, row : row + 1, :] = value[:, k * LANES : (k + 1) * LANES]
                row += 1
        smc[at.c, row:, :] = jnp.zeros((smc.shape[1] - row, LANES), F32)


    def run(point):
        for step in PLAN[point]:
            if step[0] == "m":
                multiply(int(step[1]) // 2)
                continue
            for k in map(int, step[1:]):
                if step[0] == "s":
                    small_stage(k)
                elif step[0] == "p":
                    lax.fori_loop(0, tiles, put_block, 0)
                elif step[0] == "l":
                    found["gain"] = last(k, found.get("gain", jnp.zeros((8, width), F32)))
                else:
                    getattr(sums[k], STAGES[step[0]])()

    def spread(stage, buffer, index, targets):
        for target in targets:
            remote(buffer.at[index], buffer.at[index], ssend.at[stage], srecv.at[stage], target)

    def collect(stage, buffer):
        count = buffer.shape[0]
        if count > 1:
            take(buffer.at[pl.ds(0, count - 1)], srecv.at[stage])
            take(buffer.at[pl.ds(0, count - 1)], ssend.at[stage])
        value = buffer[0]
        for k in range(1, count):
            value = value + buffer[k]
        return value

    def small_stage(k):
        if k == 0:
            fill_small()
            spread(0, smc, at.c, [at.core()])
        elif k == 1:
            smn[at.q] = collect(0, smc)
            spread(1, smn, at.q, [at.near(o) for o in range(1, at.near_count)])
        elif k == 2:
            smf[at.zh] = collect(1, smn)
            spread(2, smf, at.zh, [at.far(o) for o in range(1, at.far_count)])
        else:
            small_ref[...] = collect(2, smf)

    run(0)

    def retreat(k, carry):
        j = STEPS - 1 - k
        return [cmul(lam, add(pick(dh, i, j), carry[i])) for i in range(tiles)]

    keep_edges(lax.fori_loop(0, STEPS, retreat, [nothing] * tiles, unroll=4))
    state = zero_row
    for k in range(blocks - 1, -1, -1):
        state = kept(k, add(edge_row(k), cmul(lam_step, state)))
    exchange(1, state)

    run(1)

    incoming = gather(1, lam_all, True)
    run(2)
    for k in range(blocks - 1, -1, -1):
        if k > 0:
            following = kept(k, add(edge_row(k), cmul(lam_step, incoming)))
        edge[k : k + 1, :] = both(incoming)
        if k > 0:
            incoming = following

    def adjoint(j, carry, before):
        states, sums_of = carry
        pre, pim, gsum = sums_of
        result, grads = [], []
        for i in range(tiles):
            wre, wim = add(pick(dh, i, j), states[i])
            yre, yim = before[i]
            xre, xim = pick(x, i, j)
            pre = pre + (yre * wre + yim * wim)
            pim = pim + (yim * wre - yre * wim)
            gsum = gsum + (xre * wre + xim * wim)
            grads.append(both((scaling * wre, -scaling * wim)))
            result.append(cmul(lam, (wre, wim)))
        return (result, (pre, pim, gsum)), grads

    def put_pair(pair, early, late):
        for i in range(tiles):
            dg[at_step(i, pair * 2, 2 * SUB), :] = jnp.concatenate([early[i], late[i]], axis=0).astype(BF16)

    def before_of(j):
        return [pick(h, i, j - 1) for i in range(tiles)]

    def adjoint_pair(k, carry):
        pair = STEPS // 2 - 1 - k
        carry, late = adjoint(pair * 2 + 1, carry, before_of(pair * 2 + 1))
        carry, early = adjoint(pair * 2, carry, before_of(pair * 2))
        put_pair(pair, early, late)
        return carry

    carry = ([pick_tile(edge, i) for i in range(tiles)], (jnp.zeros((SUB, chan), F32),) * 3)
    carry = lax.fori_loop(0, STEPS // 2 - 1, adjoint_pair, carry)
    carry, late = adjoint(1, carry, before_of(1))
    carry, early = adjoint(0, carry, [pick_tile(init, i) for i in range(tiles)])
    put_pair(0, early, late)
    found["sums"] = [jnp.sum(value, axis=0, keepdims=True) for value in carry[1]]

    run(3)
    run(4)
    for which in range(2):
        for o, needed, device, _ in pairs(which == 1):
            pl.when(needed)(edge_copy(which, o, device).wait_send)


def finish(
    block_in, ing_in, sums, small,
    block_out, in_grad, b_grad, c_grad, glu_grad, gain, skip, nu, theta, gamma, wide, sem,
):
    chan = b_grad.shape[2]
    copies = []

    def store(src, dst):
        copy = pltpu.make_async_copy(src, dst, sem.at[len(copies)])
        copy.start()
        copies.append(copy)

    store(block_in, block_out)
    store(ing_in, in_grad)
    for k, value in enumerate(sums):
        wide[k] = value[...].astype(F32)
        if k < 4:
            store(wide.at[k], glu_grad.at[:, pl.ds(k * chan, chan)])
        elif k < 6:
            for n in range(2):
                store(wide.at[k, pl.ds(n * chan, chan)], c_grad.at[n, :, pl.ds((k - 4) * chan, chan)])
        else:
            store(wide.at[k], b_grad.at[k - 6])
    row = 0
    for ref in (gain, skip, nu, theta, gamma):
        ref[...] = small[row : row + ref.shape[0], :]
        row += ref.shape[0]
    for copy in copies:
        copy.wait()


def on_device(seq, dp, tokens, lengths, gain, b_proj, c_proj, skip, nu, theta, gamma_log, glu, out_grad):
    _, count, width = tokens.shape
    chan = nu.shape[0]
    at = Place(seq, dp)
    blocks = count // STEPS
    anywhere = pl.BlockSpec(memory_space=pl.ANY)
    vmem = pl.BlockSpec(memory_space=pltpu.VMEM)
    dma = pltpu.SemaphoreType.DMA
    wide, low = pltpu.VMEM((count, width), F32), pltpu.VMEM((count, width), BF16)
    specs = unit_specs(at)
    held = pl.pallas_call(
        functools.partial(kernel, at),
        out_shape=(
            pltpu.VMEM(tokens.shape, BF16),
            pltpu.VMEM(tokens.shape, BF16),
            [pltpu.VMEM((ROWS, chan), BF16) for _ in specs],
            pltpu.VMEM((16, LANES), F32),
        ),
        in_specs=[anywhere] * 11,
        out_specs=(vmem, vmem, [vmem] * len(specs), vmem),
        scratch_shapes=[
            low, low,
            pltpu.VMEM((width, 2 * chan), BF16),
            pltpu.VMEM((2 * chan, width), BF16),
            pltpu.VMEM((width, 2 * width), BF16),
            low,
            wide,
            pltpu.VMEM((count, 1), F32),
            low,
            wide, wide,
            low, low,
            pltpu.VMEM((2 * chan, width), BF16),
            pltpu.VMEM((width, 2 * chan), BF16),
            pltpu.VMEM((2 * width, width), BF16),
            *[pltpu.VMEM((width, count), BF16)] * 3,
            pltpu.VMEM((count, 2 * width), BF16),
            low,
            wide,
            pltpu.VMEM((count // MIDDLE, MIDDLE, width), F32),
            pltpu.VMEM((count // MIDDLE, MIDDLE, width), BF16),
            pltpu.VMEM((TILE, TILE), BF16),
            pltpu.VMEM((TILE, TILE), BF16),
            pltpu.VMEM((blocks, 2 * chan), F32),
            pltpu.VMEM((blocks, 2 * chan), F32),
            pltpu.VMEM((2, 1, 2 * chan), F32),
            pltpu.VMEM((2, seq, 1, 2 * chan), F32),
            pltpu.VMEM((len(specs), ROWS, chan), BF16),
            [Sum.scratch(at, chan, first, last) for first, last in specs],
            pltpu.VMEM((2, 16, LANES), F32),
            pltpu.VMEM((at.near_count, 16, LANES), F32),
            pltpu.VMEM((at.far_count, 16, LANES), F32),
            pltpu.SMEM(lengths.shape, jnp.int32),
            pltpu.VMEM((1, 3 * chan + 2 * width), F32),
            dma((count // TILE + 6,)),
            dma((2, seq)),
            dma((2, seq)),
            dma((3,)),
            dma((3,)),
        ],
        compiler_params=pltpu.CompilerParams(
            collective_id=0, has_side_effects=True, vmem_limit_bytes=48 * 2**20
        ),
    )(
        *(
            pltpu.with_memory_space_constraint(value, pltpu.HBM)
            for value in (
                tokens, out_grad, b_proj, c_proj, glu, lengths,
                gain[None], skip[None], nu[None], theta[None], gamma_log[None],
            )
        )
    )
    lines = [(k, LANES) for k in (width // LANES,) * 2 + (chan // LANES,) * 3]
    block_out, in_grad, b_grad, c_grad, glu_grad, *rest = pl.pallas_call(
        finish,
        out_shape=(
            jax.ShapeDtypeStruct(tokens.shape, BF16),
            jax.ShapeDtypeStruct(tokens.shape, BF16),
            jax.ShapeDtypeStruct(b_proj.shape, F32),
            jax.ShapeDtypeStruct(c_proj.shape, F32),
            jax.ShapeDtypeStruct(glu.shape, F32),
        ) + tuple(jax.ShapeDtypeStruct(line, F32) for line in lines),
        in_specs=[vmem, vmem, [vmem] * len(specs), vmem],
        out_specs=(anywhere,) * 5 + (vmem,) * 5,
        scratch_shapes=[pltpu.VMEM((len(specs), ROWS, chan), F32), dma((12,))],
        compiler_params=pltpu.CompilerParams(vmem_limit_bytes=16 * 2**20),
    )(*held)
    gain_grad, skip_grad, nu_grad, theta_grad, gamma_grad = (value.reshape(-1) for value in rest)
    return (
        block_out, in_grad, gain_grad, b_grad, c_grad, skip_grad, nu_grad, theta_grad, gamma_grad, glu_grad,
    )


def solution(mesh):
    rows, whole = P("dp", "seq", None), P()
    return jax.shard_map(
        functools.partial(on_device, mesh.shape["seq"], mesh.shape["dp"]),
        mesh=mesh,
        in_specs=(rows, P("dp", None)) + (whole,) * 8 + (rows,),
        out_specs=(rows, rows) + (whole,) * 8,
        check_vma=False,
    )
```

```python
import functools
import math

import jax
import jax.numpy as jnp
from jax import lax
from jax.experimental import pallas as pl
from jax.experimental.pallas import tpu as pltpu
from jax.sharding import PartitionSpec as P

MESH = pl.DeviceIdType.MESH
F32, BF16 = jnp.float32, jnp.bfloat16
EPS = 1e-5
MIDDLE = 512
GROUP = 4
TILE = 256
CHUNK = 256
LANES = 128
SUB = 8
STEPS = TILE // SUB
ROWS = 512


def mm(a, b):
    return jnp.dot(a, b, preferred_element_type=F32)


def add(a, b):
    return a[0] + b[0], a[1] + b[1]


def cmul(a, b):
    return a[0] * b[0] - a[1] * b[1], a[0] * b[1] + a[1] * b[0]


def cpow2(a, times):
    for _ in range(times):
        a = cmul(a, a)
    return a


def chunks(i, tile=TILE):
    for k in range(tile // CHUNK):
        yield pl.ds(pl.multiple_of(i * tile + k * CHUNK, CHUNK), CHUNK), slice(k * CHUNK, (k + 1) * CHUNK)


def weave(parts):
    parts = list(parts)
    while parts:
        parts = [part for part in parts if next(part, True) is None]


def fold(value):
    return jnp.sum(value.reshape(-1, 8, value.shape[1]), axis=0)


class Place:
    def __init__(self, seq, dp):
        self.seq, self.dp = seq, dp
        self.nx = max(1, math.isqrt(seq // 2))
        self.nz = seq // self.nx
        self.ny = dp // 2
        plane = self.nx * self.ny
        self.zl = 2 if self.nz % 2 == 0 and (ROWS // 2 // (2 * plane)) % 16 == 0 else 1
        self.near_count, self.far_count = self.zl * plane, self.nz // self.zl
        self.sizes = (self.zl, self.nx, self.ny)

    def here(self):
        self.s, self.d = lax.axis_index("seq"), lax.axis_index("dp")
        self.z, self.x = self.s // self.nx, lax.rem(self.s, self.nx)
        self.y, self.c = self.d // 2, lax.rem(self.d, 2)
        self.zh, self.zo = self.z // self.zl, lax.rem(self.z, self.zl)
        self.q = (self.zo * self.nx + self.x) * self.ny + self.y
        self.inner = (self.zo, self.x, self.y)
        return self

    def member(self, inner):
        return ((self.zh * self.zl + inner[0]) * self.nx + inner[1], inner[2] * 2 + self.c)

    def core(self):
        return (self.s, self.y * 2 + 1 - self.c)

    def near(self, o):
        q = lax.rem(self.q + o, self.near_count)
        return self.member((q // (self.nx * self.ny), lax.rem(q // self.ny, self.nx), lax.rem(q, self.ny)))

    def far(self, o):
        zh = lax.rem(self.zh + o, self.far_count)
        return ((zh * self.zl + self.zo) * self.nx + self.x, self.d)

    def group(self, o):
        return (lax.rem(self.s + o, self.seq), self.d)

    def peers(self):
        found = [self.core()] + [self.group(o) for o in range(1, self.seq)]
        for oy in range(1, self.ny):
            y = lax.rem(self.y + oy, self.ny)
            for zo in range(self.zl):
                for x in range(self.nx):
                    found.append(((self.zh * self.zl + zo) * self.nx + x, y * 2 + self.c))
        return found


def remote(src, dst, send, recv, device):
    copy = pltpu.make_async_remote_copy(
        src_ref=src, dst_ref=dst, send_sem=send, recv_sem=recv, device_id=device, device_id_type=MESH
    )
    copy.start()


def take(ref, sem):
    pltpu.make_async_copy(ref, ref, sem).wait()


class Sum:
    @staticmethod
    def scratch(at, width, first, last):
        half, piece = ROWS // 2, ROWS // 2 // at.near_count
        count = at.near_count // (1 if first is None else at.sizes[first])
        dma = pltpu.SemaphoreType.DMA
        shapes = [(half, width), (count - 1, piece, width), (count - 1, piece, width), (at.far_count, piece, width)]
        if first is not None:
            shapes += [(half // 2, width), (half // 2, width)]
        return [pltpu.VMEM(shape, BF16) for shape in shapes] + [
            dma((1,)), dma((5 + (first is not None) + 2 * (last is not None),))
        ]

    def __init__(self, at, first, last, out, part, rc, sc, rx, fz, *rest):
        self.at, self.first, self.last, self.out, self.part = at, first, last, out, part
        self.rc, self.sc, self.rx, self.fz = rc, sc, rx, fz
        self.send, self.recv = rest[-2:]
        if first is not None:
            self.s1, self.r1 = rest[:2]
        self.sent = 0
        self.half = ROWS // 2
        self.piece = self.half // at.near_count
        self.row0 = pl.multiple_of(at.c * self.half, 16)
        self.major = first if first is not None else last if last is not None else 0
        self.axes = [self.major] + [k for k in range(3) if k != self.major]
        self.rest = math.prod(at.sizes[k] for k in self.axes[1:])
        self.me = 0
        for k in self.axes:
            self.me = self.me * at.sizes[k] + at.inner[k]
        self.base = at.inner[self.major] * self.rest

    def others(self, axis):
        at = self.at
        count = at.near_count if axis is None else self.rest
        first = 0 if axis is None else self.base
        for o in range(1, count):
            place = first + lax.rem(self.me - first + o, count)
            inner, left = [None] * 3, place
            for k in reversed(self.axes):
                inner[k] = lax.rem(left, at.sizes[k])
                left = left // at.sizes[k]
            yield at.member(inner), place

    def mirror(self):
        inner = list(self.at.inner)
        inner[self.major] = 1 - inner[self.major]
        return self.at.member(inner)

    def go(self, slot, src, dst, device):
        remote(src, dst, self.send.at[0], self.recv.at[slot], device)
        self.sent += math.prod(src.shape[:-1])

    def share(self, slot, src, device):
        self.go(slot, src, src, device)

    def drain(self):
        if self.sent:
            take(self.part.at[pl.ds(0, self.sent)], self.send.at[0])
        self.sent = 0

    def local(self, place, count=1):
        return pl.ds(pl.multiple_of(place * self.piece, 16), count * self.piece)

    def rows(self, place, count=1):
        return pl.ds(pl.multiple_of(self.row0 + place * self.piece, 16), count * self.piece)

    def theirs(self):
        return (1 - self.at.inner[self.major]) * self.rest

    def start_core(self):
        other = pl.ds(pl.multiple_of((1 - self.at.c) * self.half, self.half), self.half)
        self.go(0, self.part.at[other], self.rc, self.at.core())

    def both(self, place, count=1):
        mine = self.part[self.rows(place, count), :].astype(F32)
        return mine + self.rc[self.local(place, count), :].astype(F32)

    def start_axis(self):
        take(self.rc, self.recv.at[0])
        self.drain()
        if self.first is not None:
            self.s1[...] = self.both(self.theirs(), self.rest).astype(BF16)
            self.go(5, self.s1, self.r1, self.mirror())

    def held(self, place):
        value = self.both(place)
        if self.first is not None:
            value = value + self.r1[self.local(place - self.base), :].astype(F32)
        return value

    def start_near(self):
        if self.first is not None:
            take(self.r1, self.recv.at[5])
            self.drain()
        for o, (device, place) in enumerate(self.others(self.first)):
            self.sc[o] = self.held(place).astype(BF16)
            self.go(1, self.sc.at[o], self.rx.at[o], device)

    def start_far(self):
        at = self.at
        total = self.held(self.me)
        take(self.rx, self.recv.at[1])
        self.drain()
        for o in range(self.rx.shape[0]):
            total += self.rx[o].astype(F32)
        self.fz[at.zh] = total.astype(BF16)
        for o in range(1, at.far_count):
            self.share(2, self.fz.at[at.zh], at.far(o))

    def back_near(self):
        at = self.at
        if at.far_count > 1:
            take(self.fz.at[pl.ds(0, at.far_count - 1)], self.recv.at[2])
        self.drain()
        total = self.fz[0].astype(F32)
        for k in range(1, at.far_count):
            total += self.fz[k].astype(F32)
        mine = self.rows(self.me)
        self.out[mine, :] = total.astype(BF16)
        for device, _ in self.others(self.last):
            self.share(3, self.out.at[mine], device)

    def back_axis(self):
        count = self.at.near_count if self.last is None else self.rest
        take(self.out.at[pl.ds(0, (count - 1) * self.piece)], self.recv.at[3])
        self.drain()
        src = self.out.at[self.rows(0 if self.last is None else self.base, count)]
        if self.last is not None:
            self.share(self.recv.shape[0] - 2, src, self.mirror())
        self.share(4, src, self.at.core())

    def back_core(self):
        if self.last is not None:
            src = self.out.at[self.rows(self.theirs(), self.rest)]
            take(src, self.recv.at[self.recv.shape[0] - 2])
            self.drain()
            self.share(self.recv.shape[0] - 1, src, self.at.core())

    def finish(self):
        count = self.at.near_count if self.last is None else self.rest
        took = self.out.at[pl.ds(0, count * self.piece)]
        take(took, self.recv.at[4])
        if self.last is not None:
            take(took, self.recv.at[self.recv.shape[0] - 1])
        self.drain()


STAGES = {
    "a": "start_axis", "n": "start_near", "f": "start_far",
    "b": "back_near", "x": "back_axis", "c": "back_core", "e": "finish",
}


PLAN = (
    (),
    ("m01", "m23", "m45", "a0", "n0", "a1", "a2", "a3", "n3", ),
    (),
    ("a4", "n4", "a5", ),
    ("m67", "p0", "l0", "a6", "a7", "n7", "f0", "n1", "n2", "l1", "s0", "f3", "s1", "n5", "f4", "n6", "b0", "f1", "f7", "f2", "b3", "s2", "f5", "b4", "f6", "x0", "b1", "b7", "x3", "b2", "s3", "b5", "x4", "b6", "c0", "x1", "c4", "e4", "x7", "e0", "x2", "c3", "e3", "x5", "c1", "x6", "c7", "c5", "e5", "c2", "e1", "c6", "e6", "e7", "e2", ),
)
AXES = ((None, 1), (1, 1), (2, 2), (None, 2), (None, None), (0, None), (1, None), (None, 0))


def unit_specs(at):
    return AXES if at.sizes == (2, 2, 2) else ((None, None),) * len(AXES)


def kernel(
    at,
    tok_hbm, og_hbm, b_hbm, c_hbm, glu_hbm, len_hbm, gain_hbm, skip_hbm, nu_hbm, theta_hbm, gam_hbm,
    block_ref, ing_ref, out_refs, small_ref,
    tok, og, bw, cw, gw, bout, xhat, rstd, u, x, h, hl, dg, bt, ct, gwt, ut, ht, gt, dz, dy, dh, slope, g, order, back_order,
    edge, init, ends, reach, msg, rmsg, part, units, smc, smn, smf,
    len_ref, vectors,
    load_sem, msend, mrecv, ssend, srecv,
):
    at.here()
    seq = at.seq
    tokens, width = tok.shape
    chan = width // 2
    tiles = tokens // TILE
    blocks = tiles * SUB
    lo, hi = slice(0, chan), slice(chan, width)

    def tile_rows(i):
        return pl.ds(pl.multiple_of(i * TILE, TILE), TILE)

    barrier = pltpu.get_barrier_semaphore()
    peers = at.peers()
    for peer in peers:
        pl.semaphore_signal(barrier, inc=1, device_id=peer, device_id_type=MESH)

    def tok_in(i):
        return pltpu.make_async_copy(tok_hbm.at[0, tile_rows(i)], tok.at[tile_rows(i)], load_sem.at[6 + i])

    def load(src, dst, sem):
        pltpu.make_async_copy(src, dst, load_sem.at[sem]).start()

    vector_at, spans = 0, []
    for src in (nu_hbm, theta_hbm, gam_hbm, gain_hbm, skip_hbm):
        here = pl.ds(vector_at, src.shape[1])
        load(src, vectors.at[:, here], 0)
        spans.append(here)
        vector_at += src.shape[1]
    load(len_hbm, len_ref, 1)
    tok_in(0).start()
    for k in range(2):
        load(b_hbm.at[k], bw.at[:, pl.ds(k * chan, chan)], 2)
    for i in range(1, tiles):
        tok_in(i).start()

    first = lax.broadcasted_iota(jnp.int32, (TILE, TILE), 0)
    second = lax.broadcasted_iota(jnp.int32, (TILE, TILE), 1)
    order[...] = (second == (first % SUB) * STEPS + first // SUB).astype(F32).astype(BF16)
    back_order[...] = (first == (second % SUB) * STEPS + second // SUB).astype(F32).astype(BF16)

    take(vectors, load_sem.at[0])
    take(len_ref, load_sem.at[1])
    nu, theta, gamma, gain, skip = (vectors[:, here] for here in spans)
    modulus = jnp.exp(-jnp.exp(nu))
    angle = jnp.exp(theta)
    lam = (modulus * jnp.cos(angle), modulus * jnp.sin(angle))
    conj = (lam[0], -lam[1])
    lam_step = cpow2(lam, int(math.log2(STEPS)))
    lam_all = cpow2(lam_step, int(math.log2(blocks)))
    conj_step, conj_all = (lam_step[0], -lam_step[1]), (lam_all[0], -lam_all[1])
    scaling = jnp.exp(gamma)
    scale2 = jnp.concatenate([scaling, -scaling], axis=1)

    starts, total = [], jnp.int32(0)
    for k in range(len_ref.shape[1]):
        starts.append(total)
        total = total + len_ref[0, k]

    def keep_at(position):
        hit = functools.reduce(jnp.logical_or, [position == start for start in starts])
        return jnp.where(hit, 0.0, 1.0).astype(F32)

    def keep_all(device):
        begin = device * tokens
        hits = [jnp.logical_and(start >= begin, start < begin + tokens) for start in starts]
        return jnp.where(functools.reduce(jnp.logical_or, hits), 0.0, 1.0).astype(F32)

    tile_keep = [keep_at(at.s * tokens + i * TILE) for i in range(tiles)]

    def kept(k, value):
        if k % SUB:
            return value
        return value[0] * tile_keep[k // SUB], value[1] * tile_keep[k // SUB]

    take(bw, load_sem.at[2])

    def front_tile(i):
        rows = tile_rows(i)
        tok_in(i).wait()
        values = mm(order[...], tok[rows, :])
        yield
        for here, part in chunks(i):
            value = values[part]
            tok[here, :] = value.astype(BF16)
            centered = value - jnp.mean(value, axis=1, keepdims=True)
            inv = lax.rsqrt(jnp.mean(centered * centered, axis=1, keepdims=True) + EPS)
            normal = centered * inv
            xhat[here, :] = normal
            rstd[here, :] = inv
            u[here, :] = (normal * gain).astype(BF16)
        drive = mm(u[rows, :], bw[...])
        yield
        for here, part in chunks(i):
            x[here, :] = drive[part].astype(BF16).astype(F32) * scale2

    def front(k, carry):
        weave(front_tile(k * GROUP + n) for n in range(GROUP))
        return carry

    lax.fori_loop(0, tiles // GROUP, front, 0)
    for k in range(2):
        load(c_hbm.at[k], cw.at[pl.ds(k * chan, chan)], 3)
    load(glu_hbm, gw, 4)
    load(og_hbm.at[0], og, 5)

    def at_step(i, j, count=SUB):
        return pl.ds(pl.multiple_of(i * TILE + j * SUB, count), count)

    def pick(ref, i, j):
        rows = at_step(i, j)
        return ref[rows, lo], ref[rows, hi]

    def pick_tile(ref, i):
        return ref[i * SUB : (i + 1) * SUB, lo], ref[i * SUB : (i + 1) * SUB, hi]

    def both(value):
        return jnp.concatenate(value, axis=1)

    nothing = (jnp.zeros((SUB, chan), F32),) * 2
    zero_row = (jnp.zeros((1, chan), F32),) * 2

    def advance(j, carry):
        return [add(cmul(conj, carry[i]), pick(x, i, j)) for i in range(tiles)]

    def keep_edges(values):
        for i in range(tiles):
            edge[i * SUB : (i + 1) * SUB, :] = both(values[i])

    keep_edges(lax.fori_loop(0, STEPS, advance, [nothing] * tiles, unroll=4))

    def edge_row(k):
        return edge[k : k + 1, lo], edge[k : k + 1, hi]

    def spread_keeps(factor, ahead):
        value = (jnp.ones((1, chan), F32), jnp.zeros((1, chan), F32))
        if ahead:
            for k in range(blocks - 1, -1, -1):
                reach[k : k + 1, :] = both(value)
                value = kept(k, cmul(factor, value))
        else:
            for k in range(blocks):
                value = kept(k, value)
                reach[k : k + 1, :] = both(value)
                value = cmul(factor, value)

    def with_carry(ref, carry):
        change = cmul((reach[:, lo], reach[:, hi]), carry)
        ref[:, lo] = ref[:, lo] + change[0]
        ref[:, hi] = ref[:, hi] + change[1]

    state = zero_row
    for k in range(blocks):
        state = kept(k, state)
        init[k : k + 1, :] = both(state)
        state = add(edge_row(k), cmul(conj_step, state))

    def pairs(ahead):
        for o in range(seq - 1, 0, -1):
            to = at.s - o if ahead else at.s + o
            source = at.s + o if ahead else at.s - o
            yield o, (to >= 0 if ahead else to < seq), (to, at.d), (source < seq if ahead else source >= 0)

    def edge_copy(which, o, device):
        return pltpu.make_async_remote_copy(
            src_ref=msg.at[which], dst_ref=rmsg.at[which, o], send_sem=msend.at[which, o],
            recv_sem=mrecv.at[which, o], device_id=device, device_id_type=MESH,
        )

    def exchange(which, value):
        msg[which] = both(value)
        for o, needed, device, _ in pairs(which == 1):
            pl.when(needed)(edge_copy(which, o, device).start)

    def chain(factor, ahead):
        value, result = (jnp.ones((1, chan), F32), jnp.zeros((1, chan), F32)), {}
        for o in range(1, seq):
            result[o] = value
            k = keep_all(at.s + o if ahead else at.s - o)
            value = cmul((factor[0] * k, factor[1] * k), value)
        return result

    def gather(which, way):
        for o, _, device, coming in pairs(which == 1):
            pl.when(coming)(edge_copy(which, o, device).wait_recv)
        result = zero_row
        for o, _, _, coming in pairs(which == 1):
            there = cmul(way[o], (rmsg[which, o, :, lo], rmsg[which, o, :, hi]))
            result = add(result, tuple(jnp.where(coming, value, 0.0) for value in there))
        return result

    pl.semaphore_wait(barrier, len(peers))
    exchange(0, state)

    def turn_u(i, carry):
        ut[:, tile_rows(i)] = u[tile_rows(i), :].T
        return carry

    lax.fori_loop(0, tiles, turn_u, 0)
    for k in range(2):
        bt[k * chan : (k + 1) * chan, :] = bw[:, k * chan : (k + 1) * chan].T
    take(cw, load_sem.at[3])
    for k in range(2):
        ct[:, k * chan : (k + 1) * chan] = cw[k * chan : (k + 1) * chan, :].T
    take(gw, load_sem.at[4])

    def turn_glu(k, carry):
        here = pl.ds(pl.multiple_of(k * chan, chan), chan)
        gwt[here, :] = gw[:, here].T
        return carry

    lax.fori_loop(0, gw.shape[1] // chan, turn_glu, 0)
    spread_keeps(conj_step, False)
    way = chain(conj_all, False)
    carry = gather(0, way)

    with_carry(init, carry)

    def advance_store(pair, carry):
        states = [[], []]
        for n in range(2):
            carry = advance(pair * 2 + n, carry)
            states[n] = [both(value) for value in carry]
        for i in range(tiles):
            rows = at_step(i, pair * 2, 2 * SUB)
            value = jnp.concatenate([states[0][i], states[1][i]], axis=0)
            h[rows, :] = value
            hl[rows, :] = value.astype(BF16)
        return carry

    lax.fori_loop(0, STEPS // 2, advance_store, [pick_tile(init, i) for i in range(tiles)], unroll=2)

    take(og, load_sem.at[5])

    def middle_tile(i, n, sums_of):
        rows = pl.ds(pl.multiple_of(i * MIDDLE, MIDDLE), MIDDLE)
        ht[:, rows] = hl[rows, :].T
        mixed = mm(hl[rows, :], cw[...])
        yield
        for here, part in chunks(i, MIDDLE):
            v = mixed[part] + skip * u[here, :].astype(F32)
            square = v * v
            t = jnp.tanh(v * (0.7978845608028654 + 0.7978845608028654 * 0.044715 * square))
            half = 0.5 + 0.5 * t
            wide = v * half
            slope[n, part, :] = half + wide * (1.0 - half) * (
                2 * 0.7978845608028654 + 6 * 0.7978845608028654 * 0.044715 * square
            )
            g[n, part, :] = wide.astype(BF16)
        gt[:, rows] = g[n].T
        values, gates = mm(g[n], gw[:, :width]), mm(g[n], gw[:, width:])
        cots = [
            mm(order[...], og[tile_rows(i * (MIDDLE // TILE) + k), :]) for k in range(MIDDLE // TILE)
        ]
        yield
        for here, part in chunks(i, MIDDLE):
            value, cot = values[part], cots[part.start // TILE]
            s = 0.5 + 0.5 * jnp.tanh(0.5 * gates[part])
            branch = value * s
            bout[here, :] = (tok[here, :].astype(F32) + branch).astype(BF16)
            og[here, :] = cot.astype(BF16)
            scaled = cot * s
            dz[here, :width] = scaled.astype(BF16)
            dz[here, width:] = (scaled * (value - branch)).astype(BF16)
        back = mm(dz[rows, :], gwt[...])
        yield
        for here, part in chunks(i, MIDDLE):
            dyl = (back[part] * slope[n, part, :]).astype(BF16)
            dy[here, :] = dyl
            sums_of.append(fold(dyl.astype(F32) * u[here, :].astype(F32)))
        cot_h = mm(dy[rows, :], ct[...])
        yield
        for here, part in chunks(i, MIDDLE):
            dh[here, :] = cot_h[part].astype(BF16).astype(F32)

    def middle(k, skip_sum):
        sums_of = [skip_sum]
        count = tokens // MIDDLE
        weave(middle_tile(k * count + n, n, sums_of) for n in range(count))
        return functools.reduce(jnp.add, sums_of)

    skip_sum = middle(0, jnp.zeros((8, width), F32))

    sums = [
        Sum(at, first, last, out, part.at[k], *refs)
        for k, ((first, last), out, refs) in enumerate(zip(unit_specs(at), out_refs, units))
    ]
    factors = [(gt, dz, 0), (gt, dz, 2), (ht, dy, 0), (ut, dg, 0)]

    def multiply(pair):
        left, right, column = factors[pair]
        half = ROWS // 2
        here = pl.ds(column * chan, 2 * chan)

        def one_half(k, carry):
            core = jnp.where(k == 0, 1 - at.c, at.c)
            rows = pl.ds(pl.multiple_of(core * half, half), half)
            product = mm(left[rows, :], right[:, here]).astype(BF16)
            part[2 * pair, rows, :] = product[:, :chan]
            part[2 * pair + 1, rows, :] = product[:, chan:]

            @pl.when(k == 0)
            def _():
                for n in range(2):
                    sums[2 * pair + n].start_core()

            return carry

        lax.fori_loop(0, 2, one_half, 0)
        for n in range(2):
            sums[2 * pair + n].sent = half

    def put_block(i, carry):
        block_ref[0, tile_rows(i), :] = mm(back_order[...], bout[tile_rows(i), :]).astype(BF16)
        return carry

    def last_tile(i, sums_of):
        rows = tile_rows(i)
        dus = mm(dg[rows, :], bt[...])
        yield
        for here, part in chunks(i):
            du = dus[part] + skip * dy[here, :].astype(F32)
            normal = xhat[here, :]
            e = gain * du
            mean_e = jnp.mean(e, axis=1, keepdims=True)
            mean_ex = jnp.mean(e * normal, axis=1, keepdims=True)
            grad = og[here, :].astype(F32) + (e - mean_e - normal * mean_ex) * rstd[here, :]
            og[here, :] = grad.astype(BF16)
            sums_of.append(fold(du * normal))
        result = mm(back_order[...], og[rows, :])
        yield
        ing_ref[0, rows, :] = result.astype(BF16)

    def last(k, gain_sum):
        sums_of = [gain_sum]
        weave(last_tile(k * 2 + n, sums_of) for n in range(2))
        return functools.reduce(jnp.add, sums_of)

    found = {}

    def fill_small():
        small = [
            jnp.sum(found["gain"], axis=0, keepdims=True),
            jnp.sum(skip_sum, axis=0, keepdims=True),
            -jnp.exp(nu) * (lam[0] * found["sums"][0] + lam[1] * found["sums"][1]),
            angle * (lam[0] * found["sums"][1] - lam[1] * found["sums"][0]),
            found["sums"][2],
        ]
        row = 0
        for value in small:
            for k in range(value.shape[1] // LANES):
                smc[at.c, row : row + 1, :] = value[:, k * LANES : (k + 1) * LANES]
                row += 1
        smc[at.c, row:, :] = jnp.zeros((smc.shape[1] - row, LANES), F32)


    def run(point):
        for step in PLAN[point]:
            if step[0] == "m":
                multiply(int(step[1]) // 2)
                continue
            for k in map(int, step[1:]):
                if step[0] == "s":
                    small_stage(k)
                elif step[0] == "p":
                    lax.fori_loop(0, tiles, put_block, 0)
                elif step[0] == "l":
                    found["gain"] = last(k, found.get("gain", jnp.zeros((8, width), F32)))
                else:
                    getattr(sums[k], STAGES[step[0]])()

    def spread(stage, buffer, index, targets):
        for target in targets:
            remote(buffer.at[index], buffer.at[index], ssend.at[stage], srecv.at[stage], target)

    def collect(stage, buffer):
        count = buffer.shape[0]
        if count > 1:
            take(buffer.at[pl.ds(0, count - 1)], srecv.at[stage])
            take(buffer.at[pl.ds(0, count - 1)], ssend.at[stage])
        value = buffer[0]
        for k in range(1, count):
            value = value + buffer[k]
        return value

    def small_stage(k):
        if k == 0:
            fill_small()
            spread(0, smc, at.c, [at.core()])
        elif k == 1:
            smn[at.q] = collect(0, smc)
            spread(1, smn, at.q, [at.near(o) for o in range(1, at.near_count)])
        elif k == 2:
            smf[at.zh] = collect(1, smn)
            spread(2, smf, at.zh, [at.far(o) for o in range(1, at.far_count)])
        else:
            small_ref[...] = collect(2, smf)

    run(0)

    def retreat(k, carry):
        j = STEPS - 1 - k
        return [cmul(lam, add(pick(dh, i, j), carry[i])) for i in range(tiles)]

    keep_edges(lax.fori_loop(0, STEPS, retreat, [nothing] * tiles, unroll=4))
    state = zero_row
    for k in range(blocks - 1, -1, -1):
        ends[k : k + 1, :] = both(state)
        state = kept(k, add(edge_row(k), cmul(lam_step, state)))
    exchange(1, state)
    spread_keeps(lam_step, True)
    way = chain(lam_all, True)

    run(1)

    with_carry(ends, gather(1, way))
    run(2)
    def adjoint(j, carry, before):
        states, sums_of = carry
        pre, pim, gsum = sums_of
        result, grads = [], []
        for i in range(tiles):
            wre, wim = add(pick(dh, i, j), states[i])
            yre, yim = before[i]
            xre, xim = pick(x, i, j)
            pre = pre + (yre * wre + yim * wim)
            pim = pim + (yim * wre - yre * wim)
            gsum = gsum + (xre * wre + xim * wim)
            grads.append(both((scaling * wre, -scaling * wim)))
            result.append(cmul(lam, (wre, wim)))
        return (result, (pre, pim, gsum)), grads

    def put_pair(pair, early, late):
        for i in range(tiles):
            dg[at_step(i, pair * 2, 2 * SUB), :] = jnp.concatenate([early[i], late[i]], axis=0).astype(BF16)

    def before_of(j):
        return [pick(h, i, j - 1) for i in range(tiles)]

    def adjoint_pair(k, carry):
        pair = STEPS // 2 - 1 - k
        carry, late = adjoint(pair * 2 + 1, carry, before_of(pair * 2 + 1))
        carry, early = adjoint(pair * 2, carry, before_of(pair * 2))
        put_pair(pair, early, late)
        return carry

    carry = ([pick_tile(ends, i) for i in range(tiles)], (jnp.zeros((SUB, chan), F32),) * 3)
    carry = lax.fori_loop(0, STEPS // 2 - 1, adjoint_pair, carry)
    carry, late = adjoint(1, carry, before_of(1))
    carry, early = adjoint(0, carry, [pick_tile(init, i) for i in range(tiles)])
    put_pair(0, early, late)
    found["sums"] = [jnp.sum(value, axis=0, keepdims=True) for value in carry[1]]

    run(3)
    run(4)
    for which in range(2):
        for o, needed, device, _ in pairs(which == 1):
            pl.when(needed)(edge_copy(which, o, device).wait_send)


def finish(
    block_in, ing_in, sums, small,
    block_out, in_grad, b_grad, c_grad, glu_grad, gain, skip, nu, theta, gamma, wide, sem,
):
    chan = b_grad.shape[2]
    copies = []

    def store(src, dst):
        copy = pltpu.make_async_copy(src, dst, sem.at[len(copies)])
        copy.start()
        copies.append(copy)

    store(block_in, block_out)
    store(ing_in, in_grad)
    for k, value in enumerate(sums):
        wide[k] = value[...].astype(F32)
        if k < 4:
            store(wide.at[k], glu_grad.at[:, pl.ds(k * chan, chan)])
        elif k < 6:
            for n in range(2):
                store(wide.at[k, pl.ds(n * chan, chan)], c_grad.at[n, :, pl.ds((k - 4) * chan, chan)])
        else:
            store(wide.at[k], b_grad.at[k - 6])
    row = 0
    for ref in (gain, skip, nu, theta, gamma):
        ref[...] = small[row : row + ref.shape[0], :]
        row += ref.shape[0]
    for copy in copies:
        copy.wait()


def on_device(seq, dp, tokens, lengths, gain, b_proj, c_proj, skip, nu, theta, gamma_log, glu, out_grad):
    _, count, width = tokens.shape
    chan = nu.shape[0]
    at = Place(seq, dp)
    blocks = count // STEPS
    anywhere = pl.BlockSpec(memory_space=pl.ANY)
    vmem = pl.BlockSpec(memory_space=pltpu.VMEM)
    dma = pltpu.SemaphoreType.DMA
    wide, low = pltpu.VMEM((count, width), F32), pltpu.VMEM((count, width), BF16)
    specs = unit_specs(at)
    held = pl.pallas_call(
        functools.partial(kernel, at),
        out_shape=(
            pltpu.VMEM(tokens.shape, BF16),
            pltpu.VMEM(tokens.shape, BF16),
            [pltpu.VMEM((ROWS, chan), BF16) for _ in specs],
            pltpu.VMEM((16, LANES), F32),
        ),
        in_specs=[anywhere] * 11,
        out_specs=(vmem, vmem, [vmem] * len(specs), vmem),
        scratch_shapes=[
            low, low,
            pltpu.VMEM((width, 2 * chan), BF16),
            pltpu.VMEM((2 * chan, width), BF16),
            pltpu.VMEM((width, 2 * width), BF16),
            low,
            wide,
            pltpu.VMEM((count, 1), F32),
            low,
            wide, wide,
            low, low,
            pltpu.VMEM((2 * chan, width), BF16),
            pltpu.VMEM((width, 2 * chan), BF16),
            pltpu.VMEM((2 * width, width), BF16),
            *[pltpu.VMEM((width, count), BF16)] * 3,
            pltpu.VMEM((count, 2 * width), BF16),
            low,
            wide,
            pltpu.VMEM((count // MIDDLE, MIDDLE, width), F32),
            pltpu.VMEM((count // MIDDLE, MIDDLE, width), BF16),
            pltpu.VMEM((TILE, TILE), BF16),
            pltpu.VMEM((TILE, TILE), BF16),
            *[pltpu.VMEM((blocks, 2 * chan), F32)] * 4,
            pltpu.VMEM((2, 1, 2 * chan), F32),
            pltpu.VMEM((2, seq, 1, 2 * chan), F32),
            pltpu.VMEM((len(specs), ROWS, chan), BF16),
            [Sum.scratch(at, chan, first, last) for first, last in specs],
            pltpu.VMEM((2, 16, LANES), F32),
            pltpu.VMEM((at.near_count, 16, LANES), F32),
            pltpu.VMEM((at.far_count, 16, LANES), F32),
            pltpu.SMEM(lengths.shape, jnp.int32),
            pltpu.VMEM((1, 3 * chan + 2 * width), F32),
            dma((count // TILE + 6,)),
            dma((2, seq)),
            dma((2, seq)),
            dma((3,)),
            dma((3,)),
        ],
        compiler_params=pltpu.CompilerParams(
            collective_id=0, has_side_effects=True, vmem_limit_bytes=48 * 2**20
        ),
    )(
        *(
            pltpu.with_memory_space_constraint(value, pltpu.HBM)
            for value in (
                tokens, out_grad, b_proj, c_proj, glu, lengths,
                gain[None], skip[None], nu[None], theta[None], gamma_log[None],
            )
        )
    )
    lines = [(k, LANES) for k in (width // LANES,) * 2 + (chan // LANES,) * 3]
    block_out, in_grad, b_grad, c_grad, glu_grad, *rest = pl.pallas_call(
        finish,
        out_shape=(
            jax.ShapeDtypeStruct(tokens.shape, BF16),
            jax.ShapeDtypeStruct(tokens.shape, BF16),
            jax.ShapeDtypeStruct(b_proj.shape, F32),
            jax.ShapeDtypeStruct(c_proj.shape, F32),
            jax.ShapeDtypeStruct(glu.shape, F32),
        ) + tuple(jax.ShapeDtypeStruct(line, F32) for line in lines),
        in_specs=[vmem, vmem, [vmem] * len(specs), vmem],
        out_specs=(anywhere,) * 5 + (vmem,) * 5,
        scratch_shapes=[pltpu.VMEM((len(specs), ROWS, chan), F32), dma((12,))],
        compiler_params=pltpu.CompilerParams(vmem_limit_bytes=16 * 2**20),
    )(*held)
    gain_grad, skip_grad, nu_grad, theta_grad, gamma_grad = (value.reshape(-1) for value in rest)
    return (
        block_out, in_grad, gain_grad, b_grad, c_grad, skip_grad, nu_grad, theta_grad, gamma_grad, glu_grad,
    )


def solution(mesh):
    rows, whole = P("dp", "seq", None), P()
    return jax.shard_map(
        functools.partial(on_device, mesh.shape["seq"], mesh.shape["dp"]),
        mesh=mesh,
        in_specs=(rows, P("dp", None)) + (whole,) * 8 + (rows,),
        out_specs=(rows, rows) + (whole,) * 8,
        check_vma=False,
    )
```

```python
import functools
import math

import jax
import jax.numpy as jnp
from jax import lax
from jax.experimental import pallas as pl
from jax.experimental.pallas import tpu as pltpu
from jax.sharding import PartitionSpec as P

MESH = pl.DeviceIdType.MESH
F32, BF16 = jnp.float32, jnp.bfloat16
EPS = 1e-5
MIDDLE = 512
GROUP = 4
TILE = 256
CHUNK = 256
LANES = 128
SUB = 8
STEPS = TILE // SUB
ROWS = 512


def mm(a, b):
    return jnp.dot(a, b, preferred_element_type=F32)


def add(a, b):
    return a[0] + b[0], a[1] + b[1]


def cmul(a, b):
    return a[0] * b[0] - a[1] * b[1], a[0] * b[1] + a[1] * b[0]


def cpow2(a, times):
    for _ in range(times):
        a = cmul(a, a)
    return a


def chunks(i, tile=TILE):
    for k in range(tile // CHUNK):
        yield pl.ds(pl.multiple_of(i * tile + k * CHUNK, CHUNK), CHUNK), slice(k * CHUNK, (k + 1) * CHUNK)


def weave(parts):
    parts = list(parts)
    while parts:
        parts = [part for part in parts if next(part, True) is None]


def fold(value):
    return jnp.sum(value.reshape(-1, 8, value.shape[1]), axis=0)


class Place:
    def __init__(self, seq, dp):
        self.seq, self.dp = seq, dp
        self.nx = max(1, math.isqrt(seq // 2))
        self.nz = seq // self.nx
        self.ny = dp // 2
        plane = self.nx * self.ny
        self.zl = 2 if self.nz % 2 == 0 and (ROWS // 2 // (2 * plane)) % 16 == 0 else 1
        self.near_count, self.far_count = self.zl * plane, self.nz // self.zl
        self.sizes = (self.zl, self.nx, self.ny)

    def here(self):
        self.s, self.d = lax.axis_index("seq"), lax.axis_index("dp")
        self.z, self.x = self.s // self.nx, lax.rem(self.s, self.nx)
        self.y, self.c = self.d // 2, lax.rem(self.d, 2)
        self.zh, self.zo = self.z // self.zl, lax.rem(self.z, self.zl)
        self.q = (self.zo * self.nx + self.x) * self.ny + self.y
        self.inner = (self.zo, self.x, self.y)
        return self

    def member(self, inner):
        return ((self.zh * self.zl + inner[0]) * self.nx + inner[1], inner[2] * 2 + self.c)

    def core(self):
        return (self.s, self.y * 2 + 1 - self.c)

    def near(self, o):
        q = lax.rem(self.q + o, self.near_count)
        return self.member((q // (self.nx * self.ny), lax.rem(q // self.ny, self.nx), lax.rem(q, self.ny)))

    def far(self, o):
        zh = lax.rem(self.zh + o, self.far_count)
        return ((zh * self.zl + self.zo) * self.nx + self.x, self.d)

    def group(self, o):
        return (lax.rem(self.s + o, self.seq), self.d)

    def peers(self):
        found = [self.core()] + [self.group(o) for o in range(1, self.seq)]
        for oy in range(1, self.ny):
            y = lax.rem(self.y + oy, self.ny)
            for zo in range(self.zl):
                for x in range(self.nx):
                    found.append(((self.zh * self.zl + zo) * self.nx + x, y * 2 + self.c))
        return found


def remote(src, dst, send, recv, device):
    copy = pltpu.make_async_remote_copy(
        src_ref=src, dst_ref=dst, send_sem=send, recv_sem=recv, device_id=device, device_id_type=MESH
    )
    copy.start()


def take(ref, sem):
    pltpu.make_async_copy(ref, ref, sem).wait()


class Sum:
    @staticmethod
    def scratch(at, width, first, last):
        half, piece = ROWS // 2, ROWS // 2 // at.near_count
        count = at.near_count // (1 if first is None else at.sizes[first])
        dma = pltpu.SemaphoreType.DMA
        shapes = [(half, width), (count - 1, piece, width), (count - 1, piece, width), (at.far_count, piece, width)]
        if first is not None:
            shapes += [(half // 2, width), (half // 2, width)]
        return [pltpu.VMEM(shape, BF16) for shape in shapes] + [
            dma((1,)), dma((5 + (first is not None) + 2 * (last is not None),))
        ]

    def __init__(self, at, first, last, out, part, rc, sc, rx, fz, *rest):
        self.at, self.first, self.last, self.out, self.part = at, first, last, out, part
        self.rc, self.sc, self.rx, self.fz = rc, sc, rx, fz
        self.send, self.recv = rest[-2:]
        if first is not None:
            self.s1, self.r1 = rest[:2]
        self.sent = 0
        self.half = ROWS // 2
        self.piece = self.half // at.near_count
        self.row0 = pl.multiple_of(at.c * self.half, 16)
        self.major = first if first is not None else last if last is not None else 0
        self.axes = [self.major] + [k for k in range(3) if k != self.major]
        self.rest = math.prod(at.sizes[k] for k in self.axes[1:])
        self.me = 0
        for k in self.axes:
            self.me = self.me * at.sizes[k] + at.inner[k]
        self.base = at.inner[self.major] * self.rest

    def others(self, axis):
        at = self.at
        count = at.near_count if axis is None else self.rest
        first = 0 if axis is None else self.base
        for o in range(1, count):
            place = first + lax.rem(self.me - first + o, count)
            inner, left = [None] * 3, place
            for k in reversed(self.axes):
                inner[k] = lax.rem(left, at.sizes[k])
                left = left // at.sizes[k]
            yield at.member(inner), place

    def mirror(self):
        inner = list(self.at.inner)
        inner[self.major] = 1 - inner[self.major]
        return self.at.member(inner)

    def go(self, slot, src, dst, device):
        remote(src, dst, self.send.at[0], self.recv.at[slot], device)
        self.sent += math.prod(src.shape[:-1])

    def share(self, slot, src, device):
        self.go(slot, src, src, device)

    def drain(self):
        if self.sent:
            take(self.part.at[pl.ds(0, self.sent)], self.send.at[0])
        self.sent = 0

    def local(self, place, count=1):
        return pl.ds(pl.multiple_of(place * self.piece, 16), count * self.piece)

    def rows(self, place, count=1):
        return pl.ds(pl.multiple_of(self.row0 + place * self.piece, 16), count * self.piece)

    def theirs(self):
        return (1 - self.at.inner[self.major]) * self.rest

    def start_core(self):
        other = pl.ds(pl.multiple_of((1 - self.at.c) * self.half, self.half), self.half)
        self.go(0, self.part.at[other], self.rc, self.at.core())

    def both(self, place, count=1):
        mine = self.part[self.rows(place, count), :].astype(F32)
        return mine + self.rc[self.local(place, count), :].astype(F32)

    def start_axis(self):
        take(self.rc, self.recv.at[0])
        self.drain()
        if self.first is not None:
            self.s1[...] = self.both(self.theirs(), self.rest).astype(BF16)
            self.go(5, self.s1, self.r1, self.mirror())

    def held(self, place):
        value = self.both(place)
        if self.first is not None:
            value = value + self.r1[self.local(place - self.base), :].astype(F32)
        return value

    def start_near(self):
        if self.first is not None:
            take(self.r1, self.recv.at[5])
            self.drain()
        for o, (device, place) in enumerate(self.others(self.first)):
            self.sc[o] = self.held(place).astype(BF16)
            self.go(1, self.sc.at[o], self.rx.at[o], device)

    def start_far(self):
        at = self.at
        total = self.held(self.me)
        take(self.rx, self.recv.at[1])
        self.drain()
        for o in range(self.rx.shape[0]):
            total += self.rx[o].astype(F32)
        self.fz[at.zh] = total.astype(BF16)
        for o in range(1, at.far_count):
            self.share(2, self.fz.at[at.zh], at.far(o))

    def back_near(self):
        at = self.at
        if at.far_count > 1:
            take(self.fz.at[pl.ds(0, at.far_count - 1)], self.recv.at[2])
        self.drain()
        total = self.fz[0].astype(F32)
        for k in range(1, at.far_count):
            total += self.fz[k].astype(F32)
        mine = self.rows(self.me)
        self.out[mine, :] = total.astype(BF16)
        for device, _ in self.others(self.last):
            self.share(3, self.out.at[mine], device)

    def back_axis(self):
        count = self.at.near_count if self.last is None else self.rest
        take(self.out.at[pl.ds(0, (count - 1) * self.piece)], self.recv.at[3])
        self.drain()
        src = self.out.at[self.rows(0 if self.last is None else self.base, count)]
        if self.last is not None:
            self.share(self.recv.shape[0] - 2, src, self.mirror())
        self.share(4, src, self.at.core())

    def back_core(self):
        if self.last is not None:
            src = self.out.at[self.rows(self.theirs(), self.rest)]
            take(src, self.recv.at[self.recv.shape[0] - 2])
            self.drain()
            self.share(self.recv.shape[0] - 1, src, self.at.core())

    def finish(self):
        count = self.at.near_count if self.last is None else self.rest
        took = self.out.at[pl.ds(0, count * self.piece)]
        take(took, self.recv.at[4])
        if self.last is not None:
            take(took, self.recv.at[self.recv.shape[0] - 1])
        self.drain()


STAGES = {
    "a": "start_axis", "n": "start_near", "f": "start_far",
    "b": "back_near", "x": "back_axis", "c": "back_core", "e": "finish",
}


PLAN = (
    (),
    ("m01", "m23", "m45", "a0", "n0", "a1", "a2", "a3", "n3", ),
    (),
    ("a4", "n4", "a5", ),
    ("m67", "p0", "l0", "a6", "a7", "n7", "f0", "n1", "n2", "l1", "s0", "f3", "s1", "n5", "f4", "n6", "b0", "f1", "f7", "f2", "b3", "s2", "f5", "b4", "f6", "x0", "b1", "b7", "x3", "b2", "s3", "b5", "x4", "b6", "c0", "x1", "c4", "e4", "x7", "e0", "x2", "c3", "e3", "x5", "c1", "x6", "c7", "c5", "e5", "c2", "e1", "c6", "e6", "e7", "e2", ),
)
AXES = ((None, 1), (1, 1), (2, 2), (None, 2), (None, None), (0, None), (1, None), (None, 0))


def unit_specs(at):
    return AXES if at.sizes == (2, 2, 2) else ((None, None),) * len(AXES)


def kernel(
    at,
    tok_hbm, og_hbm, b_hbm, c_hbm, glu_hbm, len_hbm, gain_hbm, skip_hbm, nu_hbm, theta_hbm, gam_hbm,
    block_ref, ing_ref, out_refs, small_ref,
    tok, og, bw, cw, gw, bout, xhat, rstd, u, x, h, hl, dg, bt, ct, gwt, ut, ht, gt, dz, dy, dh, slope, g, order, back_order,
    edge, init, ends, reach, msg, rmsg, part, units, smc, smn, smf,
    len_ref, vectors,
    load_sem, msend, mrecv, ssend, srecv,
):
    at.here()
    seq = at.seq
    tokens, width = tok.shape
    chan = width // 2
    tiles = tokens // TILE
    blocks = tiles * SUB
    lo, hi = slice(0, chan), slice(chan, width)

    def tile_rows(i):
        return pl.ds(pl.multiple_of(i * TILE, TILE), TILE)

    barrier = pltpu.get_barrier_semaphore()
    peers = at.peers()
    for peer in peers:
        pl.semaphore_signal(barrier, inc=1, device_id=peer, device_id_type=MESH)

    def tok_in(i):
        return pltpu.make_async_copy(tok_hbm.at[0, tile_rows(i)], tok.at[tile_rows(i)], load_sem.at[6 + i])

    def load(src, dst, sem):
        pltpu.make_async_copy(src, dst, load_sem.at[sem]).start()

    vector_at, spans = 0, []
    for src in (nu_hbm, theta_hbm, gam_hbm, gain_hbm, skip_hbm):
        here = pl.ds(vector_at, src.shape[1])
        load(src, vectors.at[:, here], 0)
        spans.append(here)
        vector_at += src.shape[1]
    load(len_hbm, len_ref, 1)
    tok_in(0).start()
    for k in range(2):
        load(b_hbm.at[k], bw.at[:, pl.ds(k * chan, chan)], 2)
    for i in range(1, tiles):
        tok_in(i).start()

    first = lax.broadcasted_iota(jnp.int32, (TILE, TILE), 0)
    second = lax.broadcasted_iota(jnp.int32, (TILE, TILE), 1)
    order[...] = (second == (first % SUB) * STEPS + first // SUB).astype(F32).astype(BF16)
    back_order[...] = (first == (second % SUB) * STEPS + second // SUB).astype(F32).astype(BF16)

    take(vectors, load_sem.at[0])
    take(len_ref, load_sem.at[1])
    nu, theta, gamma, gain, skip = (vectors[:, here] for here in spans)
    modulus = jnp.exp(-jnp.exp(nu))
    angle = jnp.exp(theta)
    lam = (modulus * jnp.cos(angle), modulus * jnp.sin(angle))
    conj = (lam[0], -lam[1])
    lam_step = cpow2(lam, int(math.log2(STEPS)))
    lam_all = cpow2(lam_step, int(math.log2(blocks)))
    conj_step, conj_all = (lam_step[0], -lam_step[1]), (lam_all[0], -lam_all[1])
    scaling = jnp.exp(gamma)
    scale2 = jnp.concatenate([scaling, -scaling], axis=1)

    starts, total = [], jnp.int32(0)
    for k in range(len_ref.shape[1]):
        starts.append(total)
        total = total + len_ref[0, k]

    def keep_at(position):
        hit = functools.reduce(jnp.logical_or, [position == start for start in starts])
        return jnp.where(hit, 0.0, 1.0).astype(F32)

    def keep_all(device):
        begin = device * tokens
        hits = [jnp.logical_and(start >= begin, start < begin + tokens) for start in starts]
        return jnp.where(functools.reduce(jnp.logical_or, hits), 0.0, 1.0).astype(F32)

    tile_keep = [keep_at(at.s * tokens + i * TILE) for i in range(tiles)]

    def kept(k, value):
        if k % SUB:
            return value
        return value[0] * tile_keep[k // SUB], value[1] * tile_keep[k // SUB]

    take(bw, load_sem.at[2])

    def front_tile(i):
        rows = tile_rows(i)
        tok_in(i).wait()
        values = mm(order[...], tok[rows, :])
        yield
        for here, part in chunks(i):
            value = values[part]
            tok[here, :] = value.astype(BF16)
            centered = value - jnp.mean(value, axis=1, keepdims=True)
            inv = lax.rsqrt(jnp.mean(centered * centered, axis=1, keepdims=True) + EPS)
            normal = centered * inv
            xhat[here, :] = normal
            rstd[here, :] = inv
            u[here, :] = (normal * gain).astype(BF16)
        drive = mm(u[rows, :], bw[...])
        yield
        for here, part in chunks(i):
            x[here, :] = drive[part].astype(BF16).astype(F32) * scale2

    def front(k, carry):
        weave(front_tile(k * GROUP + n) for n in range(GROUP))
        return carry

    lax.fori_loop(0, tiles // GROUP, front, 0)
    for k in range(2):
        load(c_hbm.at[k], cw.at[pl.ds(k * chan, chan)], 3)
    load(glu_hbm, gw, 4)
    load(og_hbm.at[0], og, 5)

    def at_step(i, j, count=SUB):
        return pl.ds(pl.multiple_of(i * TILE + j * SUB, count), count)

    def pick(ref, i, j):
        rows = at_step(i, j)
        return ref[rows, lo], ref[rows, hi]

    def pick_tile(ref, i):
        return ref[i * SUB : (i + 1) * SUB, lo], ref[i * SUB : (i + 1) * SUB, hi]

    def both(value):
        return jnp.concatenate(value, axis=1)

    nothing = (jnp.zeros((SUB, chan), F32),) * 2
    zero_row = (jnp.zeros((1, chan), F32),) * 2

    def advance(j, carry):
        return [add(cmul(conj, carry[i]), pick(x, i, j)) for i in range(tiles)]

    def keep_edges(values):
        for i in range(tiles):
            edge[i * SUB : (i + 1) * SUB, :] = both(values[i])

    keep_edges(lax.fori_loop(0, STEPS, advance, [nothing] * tiles, unroll=4))

    def edge_row(k):
        return edge[k : k + 1, lo], edge[k : k + 1, hi]

    def spread_keeps(factor, ahead):
        value = (jnp.ones((1, chan), F32), jnp.zeros((1, chan), F32))
        if ahead:
            for k in range(blocks - 1, -1, -1):
                reach[k : k + 1, :] = both(value)
                value = kept(k, cmul(factor, value))
        else:
            for k in range(blocks):
                value = kept(k, value)
                reach[k : k + 1, :] = both(value)
                value = cmul(factor, value)

    def with_carry(ref, carry):
        change = cmul((reach[:, lo], reach[:, hi]), carry)
        ref[:, lo] = ref[:, lo] + change[0]
        ref[:, hi] = ref[:, hi] + change[1]

    state = zero_row
    for k in range(blocks):
        state = kept(k, state)
        init[k : k + 1, :] = both(state)
        state = add(edge_row(k), cmul(conj_step, state))

    def pairs(ahead):
        for o in range(seq - 1, 0, -1):
            to = at.s - o if ahead else at.s + o
            source = at.s + o if ahead else at.s - o
            yield o, (to >= 0 if ahead else to < seq), (to, at.d), (source < seq if ahead else source >= 0)

    def edge_copy(which, o, device):
        return pltpu.make_async_remote_copy(
            src_ref=msg.at[which], dst_ref=rmsg.at[which, o], send_sem=msend.at[which, o],
            recv_sem=mrecv.at[which, o], device_id=device, device_id_type=MESH,
        )

    def exchange(which, value):
        msg[which] = both(value)
        for o, needed, device, _ in pairs(which == 1):
            pl.when(needed)(edge_copy(which, o, device).start)

    def chain(factor, ahead):
        value, result = (jnp.ones((1, chan), F32), jnp.zeros((1, chan), F32)), {}
        for o in range(1, seq):
            result[o] = value
            k = keep_all(at.s + o if ahead else at.s - o)
            value = cmul((factor[0] * k, factor[1] * k), value)
        return result

    def gather(which, way):
        for o, _, device, coming in pairs(which == 1):
            pl.when(coming)(edge_copy(which, o, device).wait_recv)
        result = zero_row
        for o, _, _, coming in pairs(which == 1):
            there = cmul(way[o], (rmsg[which, o, :, lo], rmsg[which, o, :, hi]))
            result = add(result, tuple(jnp.where(coming, value, 0.0) for value in there))
        return result

    pl.semaphore_wait(barrier, len(peers))
    exchange(0, state)

    def turn_u(i, carry):
        ut[:, tile_rows(i)] = u[tile_rows(i), :].T
        return carry

    lax.fori_loop(0, tiles, turn_u, 0)
    take(cw, load_sem.at[3])
    for k in range(2):
        ct[:, k * chan : (k + 1) * chan] = cw[k * chan : (k + 1) * chan, :].T
    take(gw, load_sem.at[4])

    def turn_glu(k, carry):
        here = pl.ds(pl.multiple_of(k * chan, chan), chan)
        gwt[here, :] = gw[:, here].T
        return carry

    lax.fori_loop(0, gw.shape[1] // chan, turn_glu, 0)
    spread_keeps(conj_step, False)
    way = chain(conj_all, False)
    carry = gather(0, way)

    with_carry(init, carry)

    def advance_store(pair, carry):
        states = [[], []]
        for n in range(2):
            carry = advance(pair * 2 + n, carry)
            states[n] = [both(value) for value in carry]
        for i in range(tiles):
            rows = at_step(i, pair * 2, 2 * SUB)
            value = jnp.concatenate([states[0][i], states[1][i]], axis=0)
            h[rows, :] = value
            hl[rows, :] = value.astype(BF16)
        return carry

    lax.fori_loop(0, STEPS // 2, advance_store, [pick_tile(init, i) for i in range(tiles)], unroll=2)

    take(og, load_sem.at[5])

    def middle_tile(i, n, sums_of):
        rows = pl.ds(pl.multiple_of(i * MIDDLE, MIDDLE), MIDDLE)
        ht[:, rows] = hl[rows, :].T
        mixed = mm(hl[rows, :], cw[...])
        yield
        for here, part in chunks(i, MIDDLE):
            v = mixed[part] + skip * u[here, :].astype(F32)
            square = v * v
            t = jnp.tanh(v * (0.7978845608028654 + 0.7978845608028654 * 0.044715 * square))
            half = 0.5 + 0.5 * t
            wide = v * half
            slope[n, part, :] = half + wide * (1.0 - half) * (
                2 * 0.7978845608028654 + 6 * 0.7978845608028654 * 0.044715 * square
            )
            g[n, part, :] = wide.astype(BF16)
        gt[:, rows] = g[n].T
        values, gates = mm(g[n], gw[:, :width]), mm(g[n], gw[:, width:])
        cots = [
            mm(order[...], og[tile_rows(i * (MIDDLE // TILE) + k), :]) for k in range(MIDDLE // TILE)
        ]
        yield
        for here, part in chunks(i, MIDDLE):
            value, cot = values[part], cots[part.start // TILE]
            s = 0.5 + 0.5 * jnp.tanh(0.5 * gates[part])
            branch = value * s
            bout[here, :] = (tok[here, :].astype(F32) + branch).astype(BF16)
            og[here, :] = cot.astype(BF16)
            scaled = cot * s
            dz[here, :width] = scaled.astype(BF16)
            dz[here, width:] = (scaled * (value - branch)).astype(BF16)
        back = mm(dz[rows, :], gwt[...])
        yield
        for here, part in chunks(i, MIDDLE):
            dyl = (back[part] * slope[n, part, :]).astype(BF16)
            dy[here, :] = dyl
            sums_of.append(fold(dyl.astype(F32) * u[here, :].astype(F32)))
        cot_h = mm(dy[rows, :], ct[...])
        yield
        for here, part in chunks(i, MIDDLE):
            dh[here, :] = cot_h[part].astype(BF16).astype(F32)

    def middle(k, skip_sum):
        sums_of = [skip_sum]
        count = tokens // MIDDLE
        weave(middle_tile(k * count + n, n, sums_of) for n in range(count))
        return functools.reduce(jnp.add, sums_of)

    skip_sum = middle(0, jnp.zeros((8, width), F32))

    sums = [
        Sum(at, first, last, out, part.at[k], *refs)
        for k, ((first, last), out, refs) in enumerate(zip(unit_specs(at), out_refs, units))
    ]
    factors = [(gt, dz, 0), (gt, dz, 2), (ht, dy, 0), (ut, dg, 0)]

    def multiply(pair):
        left, right, column = factors[pair]
        half = ROWS // 2
        here = pl.ds(column * chan, 2 * chan)

        def one_half(k, carry):
            core = jnp.where(k == 0, 1 - at.c, at.c)
            rows = pl.ds(pl.multiple_of(core * half, half), half)
            product = mm(left[rows, :], right[:, here]).astype(BF16)
            part[2 * pair, rows, :] = product[:, :chan]
            part[2 * pair + 1, rows, :] = product[:, chan:]

            @pl.when(k == 0)
            def _():
                for n in range(2):
                    sums[2 * pair + n].start_core()

            return carry

        lax.fori_loop(0, 2, one_half, 0)
        for n in range(2):
            sums[2 * pair + n].sent = half

    def put_block(i, carry):
        block_ref[0, tile_rows(i), :] = mm(back_order[...], bout[tile_rows(i), :]).astype(BF16)
        return carry

    def last_tile(i, sums_of):
        rows = tile_rows(i)
        dus = mm(dg[rows, :], bt[...])
        yield
        for here, part in chunks(i):
            du = dus[part] + skip * dy[here, :].astype(F32)
            normal = xhat[here, :]
            e = gain * du
            mean_e = jnp.mean(e, axis=1, keepdims=True)
            mean_ex = jnp.mean(e * normal, axis=1, keepdims=True)
            grad = og[here, :].astype(F32) + (e - mean_e - normal * mean_ex) * rstd[here, :]
            og[here, :] = grad.astype(BF16)
            sums_of.append(fold(du * normal))
        result = mm(back_order[...], og[rows, :])
        yield
        ing_ref[0, rows, :] = result.astype(BF16)

    def last(k, gain_sum):
        sums_of = [gain_sum]
        weave(last_tile(k * 2 + n, sums_of) for n in range(2))
        return functools.reduce(jnp.add, sums_of)

    found = {}

    def fill_small():
        small = [
            jnp.sum(found["gain"], axis=0, keepdims=True),
            jnp.sum(skip_sum, axis=0, keepdims=True),
            -jnp.exp(nu) * (lam[0] * found["sums"][0] + lam[1] * found["sums"][1]),
            angle * (lam[0] * found["sums"][1] - lam[1] * found["sums"][0]),
            found["sums"][2],
        ]
        row = 0
        for value in small:
            for k in range(value.shape[1] // LANES):
                smc[at.c, row : row + 1, :] = value[:, k * LANES : (k + 1) * LANES]
                row += 1
        smc[at.c, row:, :] = jnp.zeros((smc.shape[1] - row, LANES), F32)


    def run(point):
        for step in PLAN[point]:
            if step[0] == "m":
                multiply(int(step[1]) // 2)
                continue
            for k in map(int, step[1:]):
                if step[0] == "s":
                    small_stage(k)
                elif step[0] == "p":
                    for n in range(2):
                        bt[n * chan : (n + 1) * chan, :] = bw[:, n * chan : (n + 1) * chan].T
                    lax.fori_loop(0, tiles, put_block, 0)
                elif step[0] == "l":
                    found["gain"] = last(k, found.get("gain", jnp.zeros((8, width), F32)))
                else:
                    getattr(sums[k], STAGES[step[0]])()

    def spread(stage, buffer, index, targets):
        for target in targets:
            remote(buffer.at[index], buffer.at[index], ssend.at[stage], srecv.at[stage], target)

    def collect(stage, buffer):
        count = buffer.shape[0]
        if count > 1:
            take(buffer.at[pl.ds(0, count - 1)], srecv.at[stage])
            take(buffer.at[pl.ds(0, count - 1)], ssend.at[stage])
        value = buffer[0]
        for k in range(1, count):
            value = value + buffer[k]
        return value

    def small_stage(k):
        if k == 0:
            fill_small()
            spread(0, smc, at.c, [at.core()])
        elif k == 1:
            smn[at.q] = collect(0, smc)
            spread(1, smn, at.q, [at.near(o) for o in range(1, at.near_count)])
        elif k == 2:
            smf[at.zh] = collect(1, smn)
            spread(2, smf, at.zh, [at.far(o) for o in range(1, at.far_count)])
        else:
            small_ref[...] = collect(2, smf)

    run(0)

    def retreat(k, carry):
        j = STEPS - 1 - k
        return [cmul(lam, add(pick(dh, i, j), carry[i])) for i in range(tiles)]

    keep_edges(lax.fori_loop(0, STEPS, retreat, [nothing] * tiles, unroll=4))
    state = zero_row
    for k in range(blocks - 1, -1, -1):
        ends[k : k + 1, :] = both(state)
        state = kept(k, add(edge_row(k), cmul(lam_step, state)))
    exchange(1, state)
    spread_keeps(lam_step, True)
    way = chain(lam_all, True)

    run(1)

    with_carry(ends, gather(1, way))
    run(2)
    def adjoint(j, carry, before):
        states, sums_of = carry
        pre, pim, gsum = sums_of
        result, grads = [], []
        for i in range(tiles):
            wre, wim = add(pick(dh, i, j), states[i])
            yre, yim = before[i]
            xre, xim = pick(x, i, j)
            pre = pre + (yre * wre + yim * wim)
            pim = pim + (yim * wre - yre * wim)
            gsum = gsum + (xre * wre + xim * wim)
            grads.append(both((scaling * wre, -scaling * wim)))
            result.append(cmul(lam, (wre, wim)))
        return (result, (pre, pim, gsum)), grads

    def put_pair(pair, early, late):
        for i in range(tiles):
            dg[at_step(i, pair * 2, 2 * SUB), :] = jnp.concatenate([early[i], late[i]], axis=0).astype(BF16)

    def before_of(j):
        return [pick(h, i, j - 1) for i in range(tiles)]

    def adjoint_pair(k, carry):
        pair = STEPS // 2 - 1 - k
        carry, late = adjoint(pair * 2 + 1, carry, before_of(pair * 2 + 1))
        carry, early = adjoint(pair * 2, carry, before_of(pair * 2))
        put_pair(pair, early, late)
        return carry

    carry = ([pick_tile(ends, i) for i in range(tiles)], (jnp.zeros((SUB, chan), F32),) * 3)
    carry = lax.fori_loop(0, STEPS // 2 - 1, adjoint_pair, carry)
    carry, late = adjoint(1, carry, before_of(1))
    carry, early = adjoint(0, carry, [pick_tile(init, i) for i in range(tiles)])
    put_pair(0, early, late)
    found["sums"] = [jnp.sum(value, axis=0, keepdims=True) for value in carry[1]]

    run(3)
    run(4)
    for which in range(2):
        for o, needed, device, _ in pairs(which == 1):
            pl.when(needed)(edge_copy(which, o, device).wait_send)


def finish(
    block_in, ing_in, sums, small,
    block_out, in_grad, b_grad, c_grad, glu_grad, gain, skip, nu, theta, gamma, wide, sem,
):
    chan = b_grad.shape[2]
    copies = []

    def store(src, dst):
        copy = pltpu.make_async_copy(src, dst, sem.at[len(copies)])
        copy.start()
        copies.append(copy)

    store(block_in, block_out)
    store(ing_in, in_grad)
    for k, value in enumerate(sums):
        wide[k] = value[...].astype(F32)
        if k < 4:
            store(wide.at[k], glu_grad.at[:, pl.ds(k * chan, chan)])
        elif k < 6:
            for n in range(2):
                store(wide.at[k, pl.ds(n * chan, chan)], c_grad.at[n, :, pl.ds((k - 4) * chan, chan)])
        else:
            store(wide.at[k], b_grad.at[k - 6])
    row = 0
    for ref in (gain, skip, nu, theta, gamma):
        ref[...] = small[row : row + ref.shape[0], :]
        row += ref.shape[0]
    for copy in copies:
        copy.wait()


def on_device(seq, dp, tokens, lengths, gain, b_proj, c_proj, skip, nu, theta, gamma_log, glu, out_grad):
    _, count, width = tokens.shape
    chan = nu.shape[0]
    at = Place(seq, dp)
    blocks = count // STEPS
    anywhere = pl.BlockSpec(memory_space=pl.ANY)
    vmem = pl.BlockSpec(memory_space=pltpu.VMEM)
    dma = pltpu.SemaphoreType.DMA
    wide, low = pltpu.VMEM((count, width), F32), pltpu.VMEM((count, width), BF16)
    specs = unit_specs(at)
    held = pl.pallas_call(
        functools.partial(kernel, at),
        out_shape=(
            pltpu.VMEM(tokens.shape, BF16),
            pltpu.VMEM(tokens.shape, BF16),
            [pltpu.VMEM((ROWS, chan), BF16) for _ in specs],
            pltpu.VMEM((16, LANES), F32),
        ),
        in_specs=[anywhere] * 11,
        out_specs=(vmem, vmem, [vmem] * len(specs), vmem),
        scratch_shapes=[
            low, low,
            pltpu.VMEM((width, 2 * chan), BF16),
            pltpu.VMEM((2 * chan, width), BF16),
            pltpu.VMEM((width, 2 * width), BF16),
            low,
            wide,
            pltpu.VMEM((count, 1), F32),
            low,
            wide, wide,
            low, low,
            pltpu.VMEM((2 * chan, width), BF16),
            pltpu.VMEM((width, 2 * chan), BF16),
            pltpu.VMEM((2 * width, width), BF16),
            *[pltpu.VMEM((width, count), BF16)] * 3,
            pltpu.VMEM((count, 2 * width), BF16),
            low,
            wide,
            pltpu.VMEM((count // MIDDLE, MIDDLE, width), F32),
            pltpu.VMEM((count // MIDDLE, MIDDLE, width), BF16),
            pltpu.VMEM((TILE, TILE), BF16),
            pltpu.VMEM((TILE, TILE), BF16),
            *[pltpu.VMEM((blocks, 2 * chan), F32)] * 4,
            pltpu.VMEM((2, 1, 2 * chan), F32),
            pltpu.VMEM((2, seq, 1, 2 * chan), F32),
            pltpu.VMEM((len(specs), ROWS, chan), BF16),
            [Sum.scratch(at, chan, first, last) for first, last in specs],
            pltpu.VMEM((2, 16, LANES), F32),
            pltpu.VMEM((at.near_count, 16, LANES), F32),
            pltpu.VMEM((at.far_count, 16, LANES), F32),
            pltpu.SMEM(lengths.shape, jnp.int32),
            pltpu.VMEM((1, 3 * chan + 2 * width), F32),
            dma((count // TILE + 6,)),
            dma((2, seq)),
            dma((2, seq)),
            dma((3,)),
            dma((3,)),
        ],
        compiler_params=pltpu.CompilerParams(
            collective_id=0, has_side_effects=True, vmem_limit_bytes=48 * 2**20
        ),
    )(
        *(
            pltpu.with_memory_space_constraint(value, pltpu.HBM)
            for value in (
                tokens, out_grad, b_proj, c_proj, glu, lengths,
                gain[None], skip[None], nu[None], theta[None], gamma_log[None],
            )
        )
    )
    lines = [(k, LANES) for k in (width // LANES,) * 2 + (chan // LANES,) * 3]
    block_out, in_grad, b_grad, c_grad, glu_grad, *rest = pl.pallas_call(
        finish,
        out_shape=(
            jax.ShapeDtypeStruct(tokens.shape, BF16),
            jax.ShapeDtypeStruct(tokens.shape, BF16),
            jax.ShapeDtypeStruct(b_proj.shape, F32),
            jax.ShapeDtypeStruct(c_proj.shape, F32),
            jax.ShapeDtypeStruct(glu.shape, F32),
        ) + tuple(jax.ShapeDtypeStruct(line, F32) for line in lines),
        in_specs=[vmem, vmem, [vmem] * len(specs), vmem],
        out_specs=(anywhere,) * 5 + (vmem,) * 5,
        scratch_shapes=[pltpu.VMEM((len(specs), ROWS, chan), F32), dma((12,))],
        compiler_params=pltpu.CompilerParams(vmem_limit_bytes=16 * 2**20),
    )(*held)
    gain_grad, skip_grad, nu_grad, theta_grad, gamma_grad = (value.reshape(-1) for value in rest)
    return (
        block_out, in_grad, gain_grad, b_grad, c_grad, skip_grad, nu_grad, theta_grad, gamma_grad, glu_grad,
    )


def solution(mesh):
    rows, whole = P("dp", "seq", None), P()
    return jax.shard_map(
        functools.partial(on_device, mesh.shape["seq"], mesh.shape["dp"]),
        mesh=mesh,
        in_specs=(rows, P("dp", None)) + (whole,) * 8 + (rows,),
        out_specs=(rows, rows) + (whole,) * 8,
        check_vma=False,
    )
```
